32 devices in a mesh: gz: 4 (over z), row: 8 (over y, x, core).
Axes of the slice: x: 2, y: 2, z: 4, core: 2. Of those that a mesh axis runs over, the one named last changes fastest.
Arguments:
- rhs_local: float32 [8, 8, 8, 8192], P(None, None, None, ('gz', 'row')), may hold values from -10 to 10
- stretch: float32 [3, 8192], P(None, ('gz', 'row')), may hold values from 0.25 to 4
Outputs:
- precond: float32 [8, 8, 8, 8192], P(None, None, None, ('gz', 'row'))
The draws below stay inside these ranges and needn't reach their ends.
All inputs are finite; a program needn't handle non-finite values.
Results may differ from the reference program's by a relative error of at most 0.0003.
Values sent between devices are 32-bit elements; how exact they have to be, the bound alone decides.
No kernel may reach another device: no remote copies, remote signals or barrier semaphores. Data moves between devices by JAX's collectives and lax.ppermute only.
A program may use at most 128 MiB of HBM per device.

```python
import math
import jax
import jax.numpy as jnp
from jax import lax

ORDER = 7
MID = 3
ITERS = 5
EZ = 4
EA = 4
ER = 16
ELEMS = 8192
N_GZ = 4
N_ROW = 8


def draw_rhs_local(key, part):
    key = jax.random.fold_in(key, 7)
    value_key, scale_key = jax.random.split(key)
    points = ORDER + 1
    scales = jnp.exp(jax.random.uniform(scale_key, (1, 1, 1, ELEMS), jnp.float32, 0.0, math.log(10.0)))
    values = jnp.clip(jax.random.normal(value_key, (points, points, points, ELEMS), jnp.float32), -4.0, 4.0)
    return (values * scales * 0.25).astype(jnp.float32)


def steps_of(own_key, extent, shards, low, largest):
    factor_of, own = 1.0, jax.random.fold_in(own_key, 6)
    for dim, shards_of in shards:
        steps = jnp.exp(jax.random.uniform(jax.random.fold_in(own, dim), (shards_of,), jnp.float32, low / len(shards), largest / len(shards)))
        factor_of = factor_of * jnp.repeat(steps, extent[dim] // shards_of).reshape([-1 if axis == dim else 1 for axis in range(len(extent))])
    return factor_of


def setup_inputs(seed: int = 0) -> dict:
    splits = jax.random.split(jax.random.key(seed), 3)
    rhs_local = draw_rhs_local(jax.random.fold_in(splits[2], 71), 0)
    stretch = jnp.clip(jnp.exp(math.log(4.0) - 2.7725887 * jax.random.uniform(splits[1], (3, ELEMS), jnp.float32) ** steps_of(splits[1], (3, ELEMS), ((1, 32),), -0.2, 0.2)), 0.25, 4.0)
    return dict(rhs_local=rhs_local, stretch=stretch)


LOW_BOUND = 0.4
HIGH_BOUND = 4.0
HIGHEST = lax.Precision.HIGHEST


def node_points(order):
    steps = jnp.arange(order + 1).astype(jnp.float32)
    return -jnp.cos(steps * (math.pi / order))


def level_tables(order):
    points = node_points(order)
    count = order + 1
    identity = jnp.eye(count, dtype=jnp.float32)
    distance = points[:, None] - points[None, :] + identity
    barycentric = 1.0 / jnp.prod(distance, axis=1)
    offdiag = (barycentric[None, :] / barycentric[:, None]) / distance * (1.0 - identity)
    derivative = offdiag - jnp.diag(jnp.sum(offdiag, axis=1))
    place = jnp.arange(count).astype(jnp.float32)
    running = jnp.ones((count,), jnp.float32)
    for freq in range(1, order // 2 + 1):
        factor = 1.0 if 2 * freq == order else 2.0
        running = running - factor / (4.0 * freq * freq - 1.0) * jnp.cos(2.0 * freq * place * math.pi / order)
    endpoint = jnp.where((place == 0) | (place == order), 1.0, 2.0).astype(jnp.float32)
    weights = endpoint / order * running
    stiffness = jnp.dot(derivative.T * weights[None, :], derivative, precision=HIGHEST)
    return weights, stiffness


def interpolation(fine_order, coarse_order):
    fine_points = node_points(fine_order)
    coarse_points = node_points(coarse_order)
    columns = []
    for column in range(coarse_order + 1):
        value = jnp.ones((fine_order + 1,), jnp.float32)
        for other in range(coarse_order + 1):
            if other != column:
                value = value * (fine_points - coarse_points[other]) / (coarse_points[column] - coarse_points[other])
        columns.append(value)
    return jnp.stack(columns, axis=1)


def weight_shape(values, position, ndim):
    shape = [1] * ndim
    shape[position] = values.shape[0]
    return values.reshape(shape)


def element_apply(field, coeff, weights, stiffness):
    ndim = field.ndim
    along_z = weight_shape(weights, 0, ndim)
    along_a = weight_shape(weights, 1, ndim)
    along_r = weight_shape(weights, 2, ndim)
    part_z = jnp.einsum("ij,jbc...->ibc...", stiffness, field, precision=HIGHEST)
    part_a = jnp.einsum("ij,ajc...->aic...", stiffness, field, precision=HIGHEST)
    part_r = jnp.einsum("ij,abj...->abi...", stiffness, field, precision=HIGHEST)
    return coeff[0] * along_a * along_r * part_z + coeff[1] * along_z * along_r * part_a + coeff[2] * along_z * along_a * part_r


def element_diagonal(coeff, weights, stiffness, ndim):
    diag_k = jnp.diagonal(stiffness)
    term_z = weight_shape(diag_k, 0, ndim) * weight_shape(weights, 1, ndim) * weight_shape(weights, 2, ndim)
    term_a = weight_shape(weights, 0, ndim) * weight_shape(diag_k, 1, ndim) * weight_shape(weights, 2, ndim)
    term_r = weight_shape(weights, 0, ndim) * weight_shape(weights, 1, ndim) * weight_shape(diag_k, 2, ndim)
    return coeff[0] * term_z + coeff[1] * term_a + coeff[2] * term_r


def global_face_add(field, node_dim, periodic):
    count = field.shape[node_dim]
    moved = jnp.moveaxis(field, node_dim, 0)
    low_face = moved[0]
    high_face = moved[count - 1]
    elem_dim = 2 + node_dim
    from_below = jnp.roll(high_face, 1, axis=elem_dim)
    from_above = jnp.roll(low_face, -1, axis=elem_dim)
    if not periodic:
        length = low_face.shape[elem_dim]
        place = weight_shape(jnp.arange(length), elem_dim, low_face.ndim)
        from_below = jnp.where(place > 0, from_below, 0.0)
        from_above = jnp.where(place < length - 1, from_above, 0.0)
    moved = moved.at[0].set(low_face + from_below)
    moved = moved.at[count - 1].set(high_face + from_above)
    return jnp.moveaxis(moved, 0, node_dim)


def assemble(field):
    field = global_face_add(field, 2, False)
    field = global_face_add(field, 1, True)
    return global_face_add(field, 0, True)


def level_data(order):
    weights, stiffness = level_tables(order)
    count = order + 1
    node_index = jnp.arange(count)
    radial = jnp.arange(ER)
    at_wall = ((node_index[:, None] == 0) & (radial[None, :] == 0)) | ((node_index[:, None] == count - 1) & (radial[None, :] == ER - 1))
    wall_mask = jnp.where(at_wall, 0.0, 1.0).astype(jnp.float32).reshape(1, 1, count, 1, 1, ER)
    edge = jnp.where((node_index == 0) | (node_index == count - 1), 0.5, 1.0).astype(jnp.float32)
    share = (edge[:, None, None] * edge[None, :, None] * edge[None, None, :]).reshape(count, count, count, 1, 1, 1)
    return weights, stiffness, wall_mask, share


def chebyshev(operate, inverse_diag, rhs):
    theta = 0.5 * (HIGH_BOUND + LOW_BOUND)
    delta = 0.5 * (HIGH_BOUND - LOW_BOUND)
    rho_now = delta / theta
    step = inverse_diag * rhs / theta
    solution = step
    residual = rhs - operate(step)
    rho_next = 1.0 / (2.0 * theta / delta - rho_now)
    step = rho_next * rho_now * step + (2.0 * rho_next / delta) * inverse_diag * residual
    return solution + step, step, residual


def restrict(field, table):
    return jnp.einsum("ia,jb,kc,ijk...->abc...", table, table, table, field, precision=HIGHEST)


def prolong(field, table):
    return jnp.einsum("ia,jb,kc,abc...->ijk...", table, table, table, field, precision=HIGHEST)


def reference(rhs_local, stretch):
    points = ORDER + 1
    whole_z = N_GZ * EZ
    whole_a = N_ROW * EA
    fine_rhs = rhs_local.reshape(points, points, points, N_GZ, N_ROW, EZ, EA, ER).transpose(0, 1, 2, 3, 5, 4, 6, 7).reshape(points, points, points, whole_z, whole_a, ER)
    coeff = stretch.reshape(3, N_GZ, N_ROW, EZ, EA, ER).transpose(0, 1, 3, 2, 4, 5).reshape(3, whole_z, whole_a, ER)
    fine_tab = level_data(ORDER)
    mid_tab = level_data(MID)
    low_tab = level_data(1)

    def make_operator(tables):
        def operate(field):
            return tables[2] * assemble(element_apply(field, coeff, tables[0], tables[1]))
        return operate

    fine_op = make_operator(fine_tab)
    mid_op = make_operator(mid_tab)
    low_op = make_operator(low_tab)
    fine_inv = fine_tab[2] / assemble(element_diagonal(coeff, fine_tab[0], fine_tab[1], 6))
    mid_inv = mid_tab[2] / assemble(element_diagonal(coeff, mid_tab[0], mid_tab[1], 6))
    to_mid = interpolation(ORDER, MID)
    to_low = interpolation(MID, 1)

    fine_b = fine_tab[2] * assemble(fine_rhs)
    fine_sol, fine_step, fine_res = chebyshev(fine_op, fine_inv, fine_b)
    fine_res = fine_res - fine_op(fine_step)
    mid_b = mid_tab[2] * assemble(restrict(fine_tab[3] * fine_res, to_mid))
    mid_sol, mid_step, mid_res = chebyshev(mid_op, mid_inv, mid_b)
    mid_res = mid_res - mid_op(mid_step)
    low_b = low_tab[2] * assemble(restrict(mid_tab[3] * mid_res, to_low))

    weight = low_tab[2] * low_tab[3]
    low_sol = jnp.zeros_like(low_b)
    low_res = low_b
    direction = low_b
    norm_now = jnp.sum(weight * low_res * low_res)
    for iteration in range(ITERS):
        image = low_op(direction)
        alpha = norm_now / jnp.sum(weight * direction * image)
        low_sol = low_sol + alpha * direction
        low_res = low_res - alpha * image
        norm_next = jnp.sum(weight * low_res * low_res)
        direction = low_res + (norm_next / norm_now) * direction
        norm_now = norm_next

    lifted = prolong(low_sol, to_low)
    mid_sol = mid_sol + lifted
    mid_res = mid_res - mid_op(lifted)
    mid_sol = mid_sol + chebyshev(mid_op, mid_inv, mid_res)[0]
    raised = prolong(mid_sol, to_mid)
    fine_sol = fine_sol + raised
    fine_res = fine_res - fine_op(raised)
    fine_sol = fine_sol + chebyshev(fine_op, fine_inv, fine_res)[0]
    return fine_sol.reshape(points, points, points, N_GZ, EZ, N_ROW, EA, ER).transpose(0, 1, 2, 3, 5, 4, 6, 7).reshape(points, points, points, ELEMS)
```

```python
import functools

import jax
import jax.numpy as jnp
import numpy as np
from jax import lax
from jax.experimental import pallas as pl
from jax.experimental.pallas import tpu as pltpu
from jax.sharding import PartitionSpec as P

ITERS = 5
EZ = 4
EA = 4
ER = 16
HALF = 128
GROUP = EA * ER

THETA = 2.2
DELTA = 1.8
RHO = DELTA / THETA
RHO2 = 1.0 / (2.0 * THETA / DELTA - RHO)
C1 = RHO2 * RHO
C2 = 2.0 * RHO2 / DELTA


def points_of(order):
    return -np.cos(np.pi * np.arange(order + 1) / order)


def tables_of(order):
    x = points_of(order)
    n = order + 1
    dist = x[:, None] - x[None, :] + np.eye(n)
    bary = 1.0 / np.prod(dist, axis=1)
    off = bary[None, :] / bary[:, None] / dist * (1.0 - np.eye(n))
    deriv = off - np.diag(off.sum(axis=1))
    place = np.arange(n)
    run = np.ones(n)
    for j in range(1, order // 2 + 1):
        b = 1.0 if 2 * j == order else 2.0
        run = run - b / (4.0 * j * j - 1.0) * np.cos(2.0 * j * place * np.pi / order)
    ends = np.where((place == 0) | (place == order), 1.0, 2.0)
    w = ends / order * run
    k = deriv.T @ np.diag(w) @ deriv
    return w, k


def interp_of(fine, coarse):
    x, y = points_of(fine), points_of(coarse)
    cols = []
    for j in range(coarse + 1):
        v = np.ones(fine + 1)
        for k in range(coarse + 1):
            if k != j:
                v = v * (x - y[k]) / (y[j] - y[k])
        cols.append(v)
    return np.stack(cols, axis=1)


W7, K7 = tables_of(7)
W3, K3 = tables_of(3)
J73 = interp_of(7, 3)
J31 = interp_of(3, 1)
KRON73 = np.kron(np.kron(J73, J73), J73).astype(np.float32)


def weighted_sum(coefs, vals):
    total = None
    for c, v in zip(coefs, vals):
        term = v * float(c)
        total = term if total is None else total + term
    return total


def along(table, vals):
    rows, cols = table.shape
    half = cols // 2
    even = [vals[j] + vals[cols - 1 - j] for j in range(half)]
    odd = [vals[j] - vals[cols - 1 - j] for j in range(half)]
    out = [None] * rows
    for i in range(rows // 2):
        e = weighted_sum([(table[i, j] + table[i, cols - 1 - j]) / 2 for j in range(half)], even)
        o = weighted_sum([(table[i, j] - table[i, cols - 1 - j]) / 2 for j in range(half)], odd)
        out[i] = e + o
        out[rows - 1 - i] = e - o
    return out


def sub_iota(shape=(8, HALF)):
    return lax.broadcasted_iota(jnp.int32, shape, len(shape) - 2)


def lane_iota(shape=(8, HALF)):
    return lax.broadcasted_iota(jnp.int32, shape, len(shape) - 1)


def column(values):
    it = sub_iota()
    out = jnp.full((8, HALF), float(values[0]), jnp.float32)
    for i in range(1, 8):
        out = jnp.where(it == i, float(values[i]), out)
    return out


def lroll(v, shift):
    n = v.shape[-1]
    shift = shift % n
    return v if shift == 0 else pltpu.roll(v, shift, v.ndim - 1)


def sroll(v, shift):
    n = v.shape[-2]
    shift = shift % n
    return v if shift == 0 else pltpu.roll(v, shift, v.ndim - 2)


def half_of(h):
    return slice(h * HALF, (h + 1) * HALF)


def radial_masks():
    sub, lane = sub_iota(), lane_iota()
    r = lane % ER
    low = (sub == 0) & (r > 0)
    high = (sub == 7) & (r < ER - 1)
    wall = ((sub == 0) & (r == 0)) | ((sub == 7) & (r == ER - 1))
    return low, high, wall


def radial_add(v, masks):
    below = lroll(sroll(v, 1), 1)
    above = lroll(sroll(v, 7), HALF - 1)
    return v + jnp.where(masks[0], below, jnp.where(masks[1], above, 0.0))


def radial_columns():
    return [column([K7[i, (i - s) % 8] for i in range(8)]) for s in range(8)]


def radial_apply(rolls, v):
    total = rolls[0] * v
    for s in range(1, 8):
        total = total + rolls[s] * sroll(v, s)
    return total


def fine_apply(src, dst, base, s_half, sign):
    rolls = radial_columns()
    wr = column(W7)
    for h in range(2):
        sl = half_of(h)
        s0, s1, s2 = [v * sign for v in stretch_rows(s_half[h])]
        s0, s1 = s0 * wr, s1 * wr
        for iz in range(8):
            vals = [src[iz, ia, :, sl] for ia in range(8)]
            part_a = along(K7, vals)
            s1z = s1 * float(W7[iz])
            s2z = s2 * float(W7[iz])
            for ia in range(8):
                part = part_a[ia] * s1z + radial_apply(rolls, vals[ia]) * (s2z * float(W7[ia]))
                dst[iz, ia, :, sl] = part if base is None else base[iz, ia, :, sl] + part
        for ia in range(8):
            vals = [src[iz, ia, :, sl] for iz in range(8)]
            part_z = along(K7, vals)
            s0a = s0 * float(W7[ia])
            for iz in range(8):
                dst[iz, ia, :, sl] = dst[iz, ia, :, sl] + part_z[iz] * s0a


def diag_at(s_ref, h, iz, ia, wr, kr):
    sl = half_of(h)
    s0, s1, s2 = (jnp.broadcast_to(s_ref[c : c + 1, sl], (8, HALF)) for c in range(3))
    ends = s0 * float(K7[iz, iz] * W7[ia]) + s1 * float(W7[iz] * K7[ia, ia])
    return ends * wr + s2 * (kr * float(W7[iz] * W7[ia]))


def pack_a(plane, slot):
    place = (lane_iota() // ER) % EA
    out = []
    for i in range(4):
        parts = [plane(0, i), plane(1, i), plane(0, i + 4), plane(1, i + 4)]
        parts = [lroll(v, (s - slot) * ER) for s, v in enumerate(parts)]
        out.append(jnp.where(place == 0, parts[0], jnp.where(place == 1, parts[1], jnp.where(place == 2, parts[2], parts[3]))))
    return out


def unpack_a(msg, slot, h, iz):
    s = h + 2 * (iz // 4)
    return lroll(msg[iz % 4], (slot - s) * ER)


def pack_z(plane, upper):
    low = lane_iota() < GROUP
    out = []
    for i in range(4):
        a, b = plane(i), plane(i + 4)
        out.append(jnp.where(low, lroll(a, GROUP) if upper else a, b if upper else lroll(b, GROUP)))
    return out


def unpack_z(msg, ia, upper):
    m = msg[ia % 4]
    return lroll(m, GROUP) if (ia < 4) == upper else m


def parity(axis):
    return lax.axis_index(axis) % 2 == 0


def choose(flag, a, b):
    return [jnp.where(flag, x, y) for x, y in zip(a, b)]


def got(axis, r1, r2, lo, hi):
    even = parity(axis)
    one = [r1[i] for i in range(lo, hi)]
    two = [r2[i] for i in range(lo, hi)]
    return choose(even, two, one), choose(even, one, two)


def post(axis, lower, upper, m1, m2, start):
    even = parity(axis)
    for i, (lo, up) in enumerate(zip(lower, upper)):
        m1[start + i] = jnp.where(even, up, lo)
        m2[start + i] = jnp.where(even, lo, up)


def place_of():
    return (lane_iota() // ER) % EA


def every_fine():
    for h in range(2):
        for iz in range(8):
            for ia in range(8):
                yield iz, ia, half_of(h)


def join_a(y, iz, h, left, right):
    place, sl = place_of(), half_of(h)
    lo, hi = y[iz, 0, :, sl], y[iz, 7, :, sl]
    y[iz, 0, :, sl] = lo + jnp.where(place > 0, lroll(hi, ER), left)
    y[iz, 7, :, sl] = hi + jnp.where(place < EA - 1, lroll(lo, HALF - ER), right)


def join_z(y, ia, beyond):
    low = lane_iota() < GROUP
    lo0, lo1 = y[0, ia, :, half_of(0)], y[0, ia, :, half_of(1)]
    hi0, hi1 = y[7, ia, :, half_of(0)], y[7, ia, :, half_of(1)]
    up0, up1 = lroll(hi0, GROUP), lroll(hi1, GROUP)
    dn0, dn1 = lroll(lo0, GROUP), lroll(lo1, GROUP)
    y[0, ia, :, half_of(0)] = lo0 + jnp.where(low, beyond, up0)
    y[0, ia, :, half_of(1)] = lo1 + jnp.where(low, up0, up1)
    y[7, ia, :, half_of(0)] = hi0 + jnp.where(low, dn0, dn1)
    y[7, ia, :, half_of(1)] = hi1 + jnp.where(low, dn1, beyond)


def sum_inside(y):
    for iz in range(8):
        for h in range(2):
            join_a(y, iz, h, 0.0, 0.0)
    for ia in range(8):
        join_z(y, ia, 0.0)


FIRST, LATER = 17, 9


def send_z(q, inverse, m1, m2):
    top_q = pack_z(lambda ia: q[7, ia, :, half_of(1)], True)
    bottom_q = pack_z(lambda ia: q[0, ia, :, half_of(0)], False)
    post("gz", bottom_q, top_q, m1, m2, 0)

    def behind(ia, h):
        nodes = range(7) if h else range(1, 8)
        row = K7[7 if h else 0] / THETA
        return weighted_sum([row[j] for j in nodes], [inverse(j, ia, h) * q[j, ia, :, half_of(h)] for j in nodes])

    top_t = pack_z(lambda ia: behind(ia, 1), True)
    bottom_t = pack_z(lambda ia: behind(ia, 0), False)
    post("gz", bottom_t, top_t, m1, m2, 4)


def edge_lines(f, ia, h):
    slot = lane_iota() // ER
    source = (EA - 1 if ia else 0) + (EA if h else 0)
    out = None
    for j in range(1, 8):
        v = lroll(f[7 - j if h else j, ia, :, half_of(h)], (j - 1 - source) * ER)
        out = v if out is None else jnp.where(slot == j - 1, v, out)
    return out


def k_first(rhs_any, s_any, q, g, m1, m2, s_ref, rhs, sems):
    copy_s = pltpu.make_async_copy(s_any, s_ref, sems.at[0])
    copy_rhs = pltpu.make_async_copy(rhs_any, rhs, sems.at[1])
    copy_s.start()
    copy_rhs.start()
    masks = radial_masks()
    wr, kr = column(W7), column(np.diag(K7))
    copy_s.wait()
    for iz, ia, sl in every_fine():
        g[iz, ia, :, sl] = radial_add(diag_at(s_ref, sl.start // HALF, iz, ia, wr, kr), masks)
    sum_inside(g)
    copy_rhs.wait()
    for iz, ia, sl in every_fine():
        q[iz, ia, :, sl] = radial_add(rhs[iz, ia, :, sl], masks)
    sum_inside(q)
    send_z(q, lambda iz, ia, h: jnp.where(masks[2], 0.0, 1.0 / g[iz, ia, :, half_of(h)]), m1, m2)
    post(
        "gz",
        pack_z(lambda ia: g[0, ia, :, half_of(0)], False),
        pack_z(lambda ia: g[7, ia, :, half_of(1)], True),
        m1,
        m2,
        8,
    )
    lines = [[edge_lines(f, ia, h) for f in (q, g) for ia in (0, 7)] for h in range(2)]
    post("gz", lines[0], lines[1], m1, m2, 12)
    even = parity("gz")
    top, bottom = lroll(s_ref[:, half_of(1)], GROUP), s_ref[:, half_of(0)]
    m1[16] = jnp.where(even, top, bottom)
    m2[16] = jnp.where(even, bottom, top)


def with_z(f, below, above, iz, ia, h):
    v = f[iz, ia, :, half_of(h)]
    low = lane_iota() < GROUP
    if iz == 0 and h == 0:
        v = v + jnp.where(low, unpack_z(below, ia, False), 0.0)
    if iz == 7 and h == 1:
        v = v + jnp.where(low, 0.0, unpack_z(above, ia, True))
    return v


def both_z(below, above, ia):
    return jnp.where(lane_iota() < GROUP, unpack_z(below, ia, False), unpack_z(above, ia, True))


def send_a(first, q, g, z1, z2, m1, m2):
    wall = radial_masks()[2]
    q_below, q_above = got("gz", z1, z2, 0, 4)
    if first:
        g_below, g_above = got("gz", z1, z2, 8, 12)
        diag = lambda iz, ia, h: with_z(g, g_below, g_above, iz, ia, h)
        inverse = lambda iz, ia, h: jnp.where(wall, 0.0, 1.0 / diag(iz, ia, h))
    else:
        inverse = lambda iz, ia, h: g[iz, ia, :, half_of(h)]
    full = lambda iz, ia, h: with_z(q, q_below, q_above, iz, ia, h)
    post("row", pack_a(lambda h, iz: full(iz, 0, h), 0), pack_a(lambda h, iz: full(iz, 7, h), EA - 1), m1, m2, 0)
    left, right = {}, {}
    for h in range(2):
        for iz in range(8):
            scaled = [inverse(iz, ia, h) * full(iz, ia, h) for ia in range(8)]
            left[h, iz] = weighted_sum(K7[0, 1:] / THETA, scaled[1:])
            right[h, iz] = weighted_sum(K7[7, :7] / THETA, scaled[:7])
    post("row", pack_a(lambda h, iz: left[h, iz], 0), pack_a(lambda h, iz: right[h, iz], EA - 1), m1, m2, 4)


def k_first_a(q, g, s_ref, z1, z2, m1, m2):
    send_a(True, q, g, z1, z2, m1, m2)
    g_below, g_above = got("gz", z1, z2, 8, 12)
    full = lambda iz, ia, h: with_z(g, g_below, g_above, iz, ia, h)
    post("row", pack_a(lambda h, iz: full(iz, 0, h), 0), pack_a(lambda h, iz: full(iz, 7, h), EA - 1), m1, m2, 8)
    below, above = got("gz", z1, z2, 12, 16)
    post("row", [below[0], below[2], above[0], above[2]], [below[1], below[3], above[1], above[3]], m1, m2, 12)
    s_below, s_above = got("gz", z1, z2, 16, 17)
    s_z = jnp.where(lane_iota() < GROUP, s_below[0], lroll(s_above[0], GROUP))
    place = place_of()
    even = parity("row")

    def stretch_of(slot):
        parts = [s_ref[:, half_of(0)], s_ref[:, half_of(1)], s_z]
        parts = [lroll(v, (s - slot) * ER) for s, v in enumerate(parts)]
        return jnp.where(place == 0, parts[0], jnp.where(place == 1, parts[1], parts[2]))

    to_left, to_right = stretch_of(0), stretch_of(EA - 1)
    m1[16] = jnp.where(even, to_right, to_left)
    m2[16] = jnp.where(even, to_left, to_right)


def k_later_a(q, inv, z1, z2, m1, m2):
    send_a(False, q, inv, z1, z2, m1, m2)
    below, above = got("gz", z1, z2, 4, 8)
    post("row", [both_z(below, above, 0)], [both_z(below, above, 7)], m1, m2, 8)


def complete(f, z1, z2, r1, r2, start, put):
    place = place_of()
    below, above = got("gz", z1, z2, start, start + 4)
    left, right = got("row", r1, r2, start, start + 4)
    for h in range(2):
        for iz in range(8):
            for ia in range(8):
                v = with_z(f, below, above, iz, ia, h)
                if ia == 0:
                    v = v + jnp.where(place == 0, unpack_a(left, 0, h, iz), 0.0)
                if ia == 7:
                    v = v + jnp.where(place == EA - 1, unpack_a(right, EA - 1, h, iz), 0.0)
                put(iz, ia, h, v)


def halves(ghost):
    return [ghost[4], ghost[5]]


def stretch_rows(v):
    return [jnp.broadcast_to(v[k : k + 1], (8, HALF)) for k in range(3)]


def meanwhile(q, z1, z2, inverse, ghost, d, y):
    place = place_of()
    below, above = got("gz", z1, z2, 0, 4)
    for iz, ia, sl in every_fine():
        h = sl.start // HALF
        v = inverse(iz, ia, h) * with_z(q, below, above, iz, ia, h) * (1.0 / THETA)
        if ia == 0:
            v = jnp.where(place == 0, 0.0, v)
        if ia == 7:
            v = jnp.where(place == EA - 1, 0.0, v)
        d[iz, ia, :, sl] = v
    fine_apply(d, y, None, ghost, 1.0)


def k_first_mean(q, g, s_ref, z1, z2, inv, d, y):
    wall = radial_masks()[2]
    below, above = got("gz", z1, z2, 8, 12)
    for iz, ia, sl in every_fine():
        inv[iz, ia, :, sl] = jnp.where(wall, 0.0, 1.0 / with_z(g, below, above, iz, ia, sl.start // HALF))
    meanwhile(q, z1, z2, lambda iz, ia, h: inv[iz, ia, :, half_of(h)], [s_ref[:, half_of(0)], s_ref[:, half_of(1)]], d, y)


def k_later_mean(q, inv, ghost, z1, z2, d, y):
    meanwhile(q, z1, z2, lambda iz, ia, h: inv[iz, ia, :, half_of(h)], halves(ghost), d, y)


def with_face(d, face):
    def whole(iz, ia, h):
        v = d[iz, ia, :, half_of(h)]
        if ia == 0:
            v = jnp.where(place_of() == 0, face[iz, h], v)
        if ia == 7:
            v = jnp.where(place_of() == EA - 1, face[iz, h], v)
        return v

    return whole


def edge_faces(q, inv, z1, z2, r1, r2, put):
    place = place_of()
    below, above = got("gz", z1, z2, 0, 4)
    left, right = got("row", r1, r2, 0, 4)
    for h in range(2):
        for iz in range(8):
            low = with_z(q, below, above, iz, 0, h) + jnp.where(place == 0, unpack_a(left, 0, h, iz), 0.0)
            high = with_z(q, below, above, iz, 7, h) + jnp.where(place == EA - 1, unpack_a(right, EA - 1, h, iz), 0.0)
            put(iz, h, low, high)


def add_beyond(d, y0, y, face, s_own, s_n, s_z, s_m, t_left, t_right, t_z):
    place, low = place_of(), lane_iota() < GROUP
    wr, rolls = column(W7), radial_columns()
    w0, k00 = float(W7[0]), float(K7[0, 0])
    first, last = place == 0, place == EA - 1
    k_face = [jnp.where(last, float(K7[ia, 7]), float(K7[ia, 0])) for ia in range(8)]
    t_edge = []
    for h in range(2):
        sl = half_of(h)
        s0, s1, s2 = s_n[h]
        o0, o1, o2 = s_own[h]
        vals = [face[iz, h] for iz in range(8)]
        part_z = along(K7, vals)
        for iz in range(8):
            t = jnp.where(last, unpack_a(t_right, EA - 1, h, iz), unpack_a(t_left, 0, h, iz))
            if (h, iz) in ((0, 0), (1, 7)):
                t_edge.append(t)
            wz = float(W7[iz])
            part_z_w, part_r = w0 * wr * part_z[iz], (w0 * wz) * radial_apply(rolls, vals[iz])
            beyond = (s1 * wr) * (vals[iz] * k00 + t) * wz + s0 * part_z_w + s2 * part_r
            inside = o0 * part_z_w + o2 * part_r
            lines = (o1 * wr) * (vals[iz] * wz)
            for ia in range(1, 7):
                y[iz, ia, :, sl] = y0[iz, ia, :, sl] + lines * k_face[ia]
            lo = y0[iz, 0, :, sl] + lines * k_face[0] + jnp.where(first, inside, 0.0)
            hi = y0[iz, 7, :, sl] + lines * k_face[7] + jnp.where(last, inside, 0.0)
            y[iz, 0, :, sl] = lo + jnp.where(first, beyond, lroll(hi, ER))
            y[iz, 7, :, sl] = hi + jnp.where(last, beyond, lroll(lo, HALF - ER))
    t_a = jnp.where(low, t_edge[0], t_edge[1])
    vals = [jnp.where(low, d(0, ia, 0), d(7, ia, 1)) for ia in range(8)]
    part_a = along(K7, vals)
    s0, s1, s2 = s_z
    beyond = []
    for ia in range(8):
        wa = float(W7[ia])
        beyond.append((s0 * wr) * (vals[ia] * k00 + t_z[ia]) * wa + w0 * (s1 * wr * part_a[ia] + s2 * wa * radial_apply(rolls, vals[ia])))
    edge = jnp.where(place == EA - 1, vals[7], vals[0])
    edge_t = jnp.where(place == EA - 1, t_z[7], t_z[0])
    s0, s1, s2 = s_m
    corner = w0 * wr * (s0 * (edge * k00 + edge_t) + s1 * (edge * k00 + t_a)) + (w0 * w0) * s2 * radial_apply(rolls, edge)
    lo = beyond[0] + jnp.where(place > 0, lroll(beyond[7], ER), corner)
    hi = beyond[7] + jnp.where(place < EA - 1, lroll(beyond[0], -ER), corner)
    beyond[0], beyond[7] = lo, hi
    for ia in range(8):
        join_z(y, ia, beyond[ia])


def k_first_done(rhs, q, g, inv0, d, y0, s_ref, table, z1, z2, r1, r2, inv, x, rho, mid, ghost, face, y):
    masks = radial_masks()
    place, low = place_of(), lane_iota() < GROUP
    first, last = place == 0, place == EA - 1
    for iz in range(8):
        for h in range(2):
            for ia in range(1, 7):
                inv[iz, ia, :, half_of(h)] = inv0[iz, ia, :, half_of(h)]
    g_below, g_above = got("gz", z1, z2, 8, 12)
    g_left, g_right = got("row", r1, r2, 8, 12)
    for iz in range(8):
        for h in range(2):
            v = with_z(g, g_below, g_above, iz, 0, h) + jnp.where(first, unpack_a(g_left, 0, h, iz), 0.0)
            inv[iz, 0, :, half_of(h)] = jnp.where(masks[2], 0.0, 1.0 / v)
            v = with_z(g, g_below, g_above, iz, 7, h) + jnp.where(last, unpack_a(g_right, EA - 1, h, iz), 0.0)
            inv[iz, 7, :, half_of(h)] = jnp.where(masks[2], 0.0, 1.0 / v)

    def put_face(iz, h, lo, hi):
        lo, hi = inv[iz, 0, :, half_of(h)] * lo, inv[iz, 7, :, half_of(h)] * hi
        face[iz, h] = jnp.where(first, lo, jnp.where(last, hi, 0.0)) * (1.0 / THETA)

    edge_faces(q, inv, z1, z2, r1, r2, put_face)
    below, above = got("gz", z1, z2, 16, 17)
    left, right = got("row", r1, r2, 16, 17)
    ghost[2] = jnp.where(low, below[0], lroll(above[0], GROUP))
    ghost[4] = s_ref[:, half_of(0)]
    ghost[5] = s_ref[:, half_of(1)]
    for k, s in ((0, 0), (1, 1), (3, 2)):
        ghost[k] = jnp.where(place == EA - 1, lroll(right[0], (EA - 1 - s) * ER), lroll(left[0], -s * ER))
    z_lines = got("gz", z1, z2, 12, 16)
    a_lines = got("row", r1, r2, 12, 16)
    slot = lane_iota() // ER
    weight = jnp.zeros((8, HALF), jnp.float32)
    for j in range(1, 8):
        weight = jnp.where(slot == j - 1, float(K7[0, j] / THETA), weight)
    t_edge = [[None, None], [None, None]]
    for side in range(2):
        for end in range(2):
            qs = z_lines[end][side] + a_lines[side][2 * end]
            gs = z_lines[end][2 + side] + a_lines[side][2 * end + 1]
            v = jnp.where(masks[2] | (slot == 7), 0.0, weight * qs / gs)
            for shift in (64, 32, 16):
                v = v + lroll(v, shift)
            t_edge[side][end] = v
    below, above = got("gz", z1, z2, 4, 8)
    t_z = [both_z(below, above, ia) for ia in range(8)]
    t_z[0] = jnp.where(place == 0, jnp.where(low, t_edge[0][0], t_edge[0][1]), t_z[0])
    t_z[7] = jnp.where(place == EA - 1, jnp.where(low, t_edge[1][0], t_edge[1][1]), t_z[7])
    t_left, t_right = got("row", r1, r2, 4, 8)
    s_n, s_z, s_m = [stretch_rows(ghost[0]), stretch_rows(ghost[1])], stretch_rows(ghost[2]), stretch_rows(ghost[3])
    s_own = [stretch_rows(v) for v in halves(ghost)]
    whole = with_face(d, face)
    add_beyond(whole, y0, y, face, s_own, s_n, s_z, s_m, t_left, t_right, t_z)

    def put_x(iz, ia, h, v):
        sl = half_of(h)
        r = v - radial_add(y[iz, ia, :, sl], masks)
        x[iz, ia, :, sl] = (1.0 + C1) * whole(iz, ia, h) + C2 * inv[iz, ia, :, sl] * r

    complete(q, z1, z2, r1, r2, 0, put_x)
    fine_apply(x, rho, rhs, halves(ghost), -1.0)
    for iz, ia, sl in every_fine():
        y[iz, ia, :, sl] = jnp.where(masks[2], 0.0, rho[iz, ia, :, sl])
    down = jnp.dot(table[...], y[...].reshape(512, 256), preferred_element_type=jnp.float32, precision=lax.Precision.HIGHEST)
    inner = lane_iota((56, HALF)) % ER > 0
    for h in range(2):
        sl = half_of(h)
        mid[:, sl] = down[0:56, sl] + jnp.where(inner, lroll(down[56:112, sl], 1), 0.0)
    mid[48:56, :] = s_ref[...]


def k_last(q, inv, d, y0, x, ghost, z1, z2, r1, r2, out, face, y):
    masks = radial_masks()
    place = place_of()
    first, last = place == 0, place == EA - 1

    def put_face(iz, h, lo, hi):
        lo, hi = inv[iz, 0, :, half_of(h)] * lo, inv[iz, 7, :, half_of(h)] * hi
        face[iz, h] = jnp.where(first, lo, jnp.where(last, hi, 0.0)) * (1.0 / THETA)

    edge_faces(q, inv, z1, z2, r1, r2, put_face)
    below, above = got("gz", z1, z2, 4, 8)
    t_z = [both_z(below, above, ia) for ia in range(8)]
    left, right = got("row", r1, r2, 8, 9)
    t_z[0] = t_z[0] + jnp.where(first, lroll(left[0], -(EA - 1) * ER), 0.0)
    t_z[7] = t_z[7] + jnp.where(last, lroll(right[0], (EA - 1) * ER), 0.0)
    t_left, t_right = got("row", r1, r2, 4, 8)
    s_n, s_z, s_m = [stretch_rows(ghost[0]), stretch_rows(ghost[1])], stretch_rows(ghost[2]), stretch_rows(ghost[3])
    s_own = [stretch_rows(v) for v in halves(ghost)]
    whole = with_face(d, face)
    add_beyond(whole, y0, y, face, s_own, s_n, s_z, s_m, t_left, t_right, t_z)

    def put_out(iz, ia, h, v):
        sl = half_of(h)
        r = v - radial_add(y[iz, ia, :, sl], masks)
        out[iz, ia, :, sl] = x[iz, ia, :, sl] + (1.0 + C1) * whole(iz, ia, h) + C2 * inv[iz, ia, :, sl] * r

    complete(q, z1, z2, r1, r2, 0, put_out)


NODES = [(iz, ia, ir) for iz in range(3) for ia in range(3) for ir in range(3)]


def node(iz, ia, ir):
    return (iz * 3 + ia) * 3 + ir


def restrict_rows():
    picks = [(iz, ia, ir) for iz, ia, ir in NODES]
    picks += [(iz, 3, ir) for iz in range(3) for ir in range(3)]
    picks += [(3, ia, ir) for ia in range(3) for ir in range(3)]
    picks += [(3, 3, ir) for ir in range(3)]
    out = np.zeros((112, 512))
    for i, (iz, ia, ir) in enumerate(picks):
        out[i] = np.kron(np.kron(J73[:, iz], J73[:, ia]), J73[:, ir])
        if ir == 0:
            out[56 + i] = np.kron(np.kron(J73[:, iz], J73[:, ia]), J73[:, 3])
    return out.astype(np.float32)


RESTRICT = restrict_rows()
PACKED = 17


def prev_z(v):
    return sroll(v, 1)


def prev_a(v):
    return lroll(v, ER)


def prev_r(v):
    return lroll(v, 1)


def next_z(v):
    return sroll(v, -1)


def next_a(v):
    return lroll(v, -ER)


def next_r(v):
    return lroll(v, -1)


def mid_coefs(s):
    prev = (prev_z, prev_a, prev_r)
    out = []
    for direction in range(3):
        one, two = [k for k in range(3) if k != direction]
        table = {}
        for e1 in range(2):
            v = s[direction] * float(W3[e1])
            v = v + prev[one](v) if e1 == 0 else v
            for e2 in range(2):
                u = v * float(W3[e2])
                table[e1, e2] = u + prev[two](u) if e2 == 0 else u
        out.append(table)
    return out


def mid_inverse(c, inner):
    out = {}
    for ez in range(2):
        for ea in range(2):
            for er in range(2):
                total = None
                for v, e, prev in ((c[0][ea, er], ez, prev_z), (c[1][ez, er], ea, prev_a), (c[2][ez, ea], er, prev_r)):
                    term = v * float(K3[1, 1]) if e else (v + prev(v)) * float(K3[0, 0])
                    total = term if total is None else total + term
                value = 1.0 / total
                out[ez, ea, er] = value if er else jnp.where(inner, value, 0.0)
    return out


def end(i):
    return 0 if i == 0 else 1


def mid_apply(get, nz, na, nr, c, acc):
    for ia in range(3):
        for ir in range(3):
            part = along(K3, [get(0, ia, ir), get(1, ia, ir), get(2, ia, ir), nz(ia, ir)])
            part = [v * c[0][end(ia), end(ir)] for v in part]
            acc[node(0, ia, ir)] = part[0] + prev_z(part[3])
            acc[node(1, ia, ir)] = part[1]
            acc[node(2, ia, ir)] = part[2]
    for iz in range(3):
        for ir in range(3):
            part = along(K3, [get(iz, 0, ir), get(iz, 1, ir), get(iz, 2, ir), na(iz, ir)])
            part = [v * c[1][end(iz), end(ir)] for v in part]
            acc[node(iz, 0, ir)] = acc[node(iz, 0, ir)] + part[0] + prev_a(part[3])
            acc[node(iz, 1, ir)] = acc[node(iz, 1, ir)] + part[1]
            acc[node(iz, 2, ir)] = acc[node(iz, 2, ir)] + part[2]
    for iz in range(3):
        for ia in range(3):
            part = along(K3, [get(iz, ia, 0), get(iz, ia, 1), get(iz, ia, 2), nr(iz, ia)])
            part = [v * c[2][end(iz), end(ia)] for v in part]
            acc[node(iz, ia, 0)] = acc[node(iz, ia, 0)] + part[0] + prev_r(part[3])
            acc[node(iz, ia, 1)] = acc[node(iz, ia, 1)] + part[1]
            acc[node(iz, ia, 2)] = acc[node(iz, ia, 2)] + part[2]


def k_column(rows, *refs):
    blocks, out, wide = refs[:-2], refs[-2], refs[-1]
    for k, block in enumerate(blocks):
        for z in range(EZ):
            v = block[:, half_of(z // 2)]
            wide[pl.ds((2 - EZ * k + z) % rows, 56, stride=rows), :] = lroll(v, GROUP) if z % 2 else v

    def entry(i):
        return wide[i * rows : (i + 1) * rows, :]

    shape = (rows, HALF)
    lane = lane_iota(shape)
    own, face = {}, {}
    for iz, ia, ir in NODES:
        v = entry(node(iz, ia, ir))
        own[iz, ia, ir] = v + prev_z(entry(36 + ia * 3 + ir)) if iz == 0 else v
    for iz in range(3):
        for ir in range(3):
            v = entry(27 + iz * 3 + ir)
            v = v + prev_z(entry(45 + ir)) if iz == 0 else v
            face[iz * 3 + ir] = v
            own[iz, 0, ir] = own[iz, 0, ir] + jnp.where(lane >= ER, prev_a(v), 0.0)
    flat = [own[n] for n in NODES] + [entry(48 + k) for k in range(3)]
    for p in range(15):
        out[p] = jnp.where(lane < GROUP, flat[2 * p], lroll(flat[2 * p + 1], GROUP))
    for p in range(2):
        v = None
        for slot, i in enumerate(range(8 * p, min(9, 8 * p + 8))):
            moved = lroll(face[i], (slot - (EA - 1)) * ER)
            v = moved if v is None else jnp.where(lane // ER == slot, moved, v)
        out[15 + p] = v


def k_mid(own, r1, r2, coarse, res, x, inv_out, c_out, b, d, y, y2):
    rows = own.shape[1]
    even = parity("row")
    lane = lane_iota((rows, HALF))

    def sides(i):
        one, two = r1[i], r2[i]
        return jnp.where(even, two, one), jnp.where(even, one, two)

    def halo(i):
        p, base = i // 2, GROUP * (i % 2)
        left, right = sides(p)
        left, right = lroll(left, 96 - base), lroll(right, 96 - base)
        mine = lroll(own[p], 32 - base)
        first = jnp.where(lane < 32, left, jnp.where(lane < 96, mine, right))
        return first, jnp.where(lane < 32, right, left)

    for iz, ia, ir in NODES:
        n = node(iz, ia, ir)
        first, second = halo(n)
        if ia == 0:
            i = iz * 3 + ir
            left, _ = sides(15 + i // 8)
            slot = i % 8
            from_left = lroll(left, 32 - slot * ER)
            to_right = lroll(own[15 + i // 8], 96 - slot * ER)
            first = first + jnp.where((lane >= 32) & (lane < 48), from_left, jnp.where((lane >= 96) & (lane < 112), to_right, 0.0))
        b[n, :, 0:HALF] = first
        b[n, :, HALF:] = second
    s = []
    for k in range(3):
        first, second = halo(27 + k)
        second = jnp.where((lane >= 32) & (lane < 96), 1.0, second)
        coarse[1 + k] = lroll(first, -32)[:, 0:GROUP]
        s.append(jnp.concatenate([first, second], axis=1))

    inner = lane_iota((rows, 2 * HALF)) % ER > 0
    c = mid_coefs(s)
    inverse = mid_inverse(c, inner)
    for i, e in enumerate([(ez, ea, er) for ez in range(2) for ea in range(2) for er in range(2)]):
        inv_out[i] = inverse[e][0:8, 0:HALF]
    for k in range(3):
        for i, e in enumerate([(0, 0), (0, 1), (1, 0), (1, 1)]):
            c_out[4 * k + i] = c[k][e][0:8, 0:HALF]

    def kind(iz, ia, ir):
        return inverse[end(iz), end(ia), end(ir)]

    def get(iz, ia, ir):
        return d[node(iz, ia, ir)]

    for iz, ia, ir in NODES:
        n = node(iz, ia, ir)
        d[n] = kind(iz, ia, ir) * b[n] * (1.0 / THETA)
    mid_apply(
        get,
        lambda ia, ir: next_z(get(0, ia, ir)),
        lambda iz, ir: next_a(get(iz, 0, ir)),
        lambda iz, ia: next_r(get(iz, ia, 0)),
        c,
        y,
    )
    for iz, ia, ir in NODES:
        n = node(iz, ia, ir)
        d[n] = (1.0 + C1) * d[n] + C2 * kind(iz, ia, ir) * (b[n] - y[n])
        x[n] = d[n, 0:8, 0:HALF]

    def near(iz, ia, ir):
        return d[node(iz, ia, ir), :, 0:HALF]

    mid_apply(
        near,
        lambda ia, ir: next_z(near(0, ia, ir)),
        lambda iz, ir: next_a(get(iz, 0, ir))[:, 0:HALF],
        lambda iz, ia: next_r(near(iz, ia, 0)),
        [{e: v[:, 0:HALF] for e, v in t.items()} for t in c],
        y2,
    )
    inner = lane % ER > 0
    for iz, ia, ir in NODES:
        n = node(iz, ia, ir)
        r = b[n, :, 0:HALF] - y2[n]
        r = r if ir else jnp.where(inner, r, 0.0)
        y2[n] = r
        res[n] = r[0:8]

    def gather(v, prev):
        return v[0] + v[1] * float(J31[1, 0]) + v[2] * float(J31[2, 0]) + prev(v[1] * float(J31[1, 1]) + v[2] * float(J31[2, 1]))

    planes = []
    for iz in range(3):
        lines = [gather([y2[node(iz, ia, ir)] for ir in range(3)], prev_r) for ia in range(3)]
        planes.append(gather(lines, prev_a))
    vertex = jnp.where(inner, gather(planes, prev_z), 0.0)
    coarse[0] = lroll(vertex, -32)[:, 0:GROUP]


def vertex_solve(s0, s1, s2, b):
    shape = b.shape
    inner = (lane_iota(shape) % ER) > 0

    def pair(v, f):
        return v + f(v)

    edge_z = 0.5 * pair(pair(s0, prev_a), prev_r)
    edge_a = 0.5 * pair(pair(s1, prev_z), prev_r)
    edge_r = 0.5 * pair(pair(s2, prev_z), prev_a)
    back_z, back_a, back_r = prev_z(edge_z), prev_a(edge_a), prev_r(edge_r)
    middle = edge_z + back_z + edge_a + back_a + edge_r + back_r

    def operate(q):
        y = middle * q - edge_z * next_z(q) - back_z * prev_z(q)
        y = y - edge_a * next_a(q) - back_a * prev_a(q)
        y = y - edge_r * next_r(q) - back_r * prev_r(q)
        return jnp.where(inner, y, 0.0)

    def total(v):
        return jnp.sum(jnp.sum(v, axis=0, keepdims=True), axis=1, keepdims=True)

    e = jnp.zeros(shape, jnp.float32)
    r = b
    q = b
    rr = total(r * r)
    for _ in range(ITERS):
        y = operate(q)
        alpha = rr / total(q * y)
        e = e + alpha * q
        r = r - alpha * y
        rn = total(r * r)
        q = r + (rn / rr) * q
        rr = rn
    return e


def k_fifth(whole, res, xm, inv3, c_in, x, rho, inv, ghost, kron, x_out, q, m1, m2, lift, dm, rm, xs, g):
    e = vertex_solve(whole[1], whole[2], whole[3], whole[0])
    lanes = e.shape[1]
    e = pltpu.roll(e, (lanes + 32 - GROUP * lax.axis_index("row")) % lanes, 1)
    corner = {}
    for cz in range(2):
        for ca in range(2):
            for cr in range(2):
                v = next_z(e) if cz else e
                corner[cz, ca, cr] = lroll(v, -(ca * ER + cr))[0:8, 0:HALF]

    def three(a, b):
        return [a] + [a * float(J31[i, 0]) + b * float(J31[i, 1]) for i in (1, 2)]

    along_r = {(cz, ca): three(corner[cz, ca, 0], corner[cz, ca, 1]) for cz in range(2) for ca in range(2)}
    along_ra = {cz: [three(along_r[cz, 0][ir], along_r[cz, 1][ir]) for ir in range(3)] for cz in range(2)}
    beyond_a = {ir: three(along_r[0, 1][ir], along_r[1, 1][ir]) for ir in range(3)}
    for ia in range(3):
        for ir in range(3):
            for iz, v in enumerate(three(along_ra[0][ir][ia], along_ra[1][ir][ia])):
                lift[node(iz, ia, ir)] = v

    c = [{e_: c_in[4 * k + i] for i, e_ in enumerate([(0, 0), (0, 1), (1, 0), (1, 1)])} for k in range(3)]

    def kind(iz, ia, ir):
        return inv3[(end(iz) * 2 + end(ia)) * 2 + end(ir)]

    def get_lift(iz, ia, ir):
        return lift[node(iz, ia, ir)]

    def get_d(iz, ia, ir):
        return dm[node(iz, ia, ir)]

    mid_apply(
        get_lift,
        lambda ia, ir: along_ra[1][ir][ia],
        lambda iz, ir: beyond_a[ir][iz],
        lambda iz, ia: next_r(get_lift(iz, ia, 0)),
        c,
        rm,
    )
    for iz, ia, ir in NODES:
        n = node(iz, ia, ir)
        r = kind(iz, ia, ir) * (res[n] - rm[n])
        dm[n] = r * (1.0 / THETA)
        lift[n] = lift[n] + xm[n] + ((1.0 + C1) / THETA + C2) * r
    mid_apply(
        get_d,
        lambda ia, ir: next_z(get_d(0, ia, ir)),
        lambda iz, ir: next_a(get_d(iz, 0, ir)),
        lambda iz, ia: next_r(get_d(iz, ia, 0)),
        c,
        rm,
    )
    for iz, ia, ir in NODES:
        n = node(iz, ia, ir)
        lift[n] = lift[n] - C2 * kind(iz, ia, ir) * rm[n]
    for iz in range(4):
        for ia in range(4):
            for ir in range(4):
                v = lift[node(iz % 3, ia % 3, ir % 3)]
                v = lroll(v, -(ia // 3 * ER + ir // 3))
                v = next_z(v) if iz == 3 else v
                n = (iz * 4 + ia) * 4 + ir
                xs[n * 8 : (n + 1) * 8, :] = v
    low = lane_iota((64, HALF)) < GROUP
    cols = []
    for h in range(2):
        one = xs[pl.ds(2 + 2 * h, 64, stride=8), :]
        two = xs[pl.ds(3 + 2 * h, 64, stride=8), :]
        cols.append(jnp.where(low, lroll(one, -32), lroll(two, 32)))
    xe = jnp.concatenate(cols, axis=1)
    raised = jnp.dot(kron[...], xe, preferred_element_type=jnp.float32, precision=lax.Precision.HIGHEST)
    g[...] = raised.reshape(8, 8, 8, 256)
    for iz, ia, sl in every_fine():
        x_out[iz, ia, :, sl] = x[iz, ia, :, sl] + g[iz, ia, :, sl]
    masks = radial_masks()
    fine_apply(g, q, rho, halves(ghost), -1.0)
    for iz, ia, sl in every_fine():
        q[iz, ia, :, sl] = radial_add(q[iz, ia, :, sl], masks)
    sum_inside(q)
    send_z(q, lambda iz, ia, h: inv[iz, ia, :, half_of(h)], m1, m2)


FINE = (8, 8, 8, 256)


def call(body, outs, scratch=(), name=None, far=0):
    shapes = [jax.ShapeDtypeStruct(s, jnp.float32) for s in outs]
    specs = dict(in_specs=[pl.BlockSpec(memory_space=pltpu.HBM)] * far) if far else {}
    return pl.pallas_call(
        body,
        out_shape=shapes,
        scratch_shapes=[pltpu.VMEM(s, jnp.float32) for s in scratch] + ([pltpu.SemaphoreType.DMA((far,))] if far else []),
        **specs,
        compiler_params=pltpu.CompilerParams(vmem_limit_bytes=32 * 1024 * 1024),
        name=name,
    )


def per_device(gz, row, rhs, stretch):
    mate_row = [(i, i ^ 1) for i in range(row)]
    other_row = [(i, (((i + 1) ^ 1) - 1) % row) for i in range(row)]
    mate_gz = [(i, i ^ 1) for i in range(gz)]
    other_gz = [(i, (((i + 1) ^ 1) - 1) % gz) for i in range(gz)]

    def swap_a(m1, m2):
        return lax.ppermute(m1, "row", mate_row), lax.ppermute(m2, "row", other_row)

    def swap_z(m1, m2):
        return lax.ppermute(m1, "gz", mate_gz), lax.ppermute(m2, "gz", other_gz)

    def message(entries):
        return (entries, 8, HALF)

    stretch = jnp.pad(stretch, ((0, 5), (0, 0)))
    ghosts = (6, 8, HALF)
    q, g, m1, m2 = call(k_first, [FINE, FINE, message(FIRST), message(FIRST)], [(8, 256), FINE], name="first", far=2)(rhs, stretch)
    z1, z2 = swap_z(m1, m2)
    m1, m2 = call(k_first_a, [message(FIRST), message(FIRST)], name="first_a")(q, g, stretch, z1, z2)
    r1, r2 = swap_a(m1, m2)
    inv, d, y = call(k_first_mean, [FINE, FINE, FINE], name="first_mean")(q, g, stretch, z1, z2)
    faces = (8, 2, 8, HALF)
    inv, x, rho, block, ghost = call(k_first_done, [FINE, FINE, FINE, (56, 256), ghosts], [faces, FINE], name="first_done")(
        rhs, q, g, inv, d, y, stretch, jnp.asarray(RESTRICT), z1, z2, r1, r2
    )

    rows = gz * EZ
    blocks = [block] + [lax.ppermute(block, "gz", [(i, (i + k) % gz) for i in range(gz)]) for k in range(1, gz)]
    column_ = call(functools.partial(k_column, rows), [(PACKED, rows, HALF)], [(56 * rows, HALF)], name="column")(*blocks)[0]
    r1, r2 = swap_a(column_, column_)
    cube, wide = (27, 8, HALF), (27, rows, 2 * HALF)
    coarse, res, xm, inv3, c3 = call(
        k_mid,
        [(4, rows, GROUP), cube, cube, (8, 8, HALF), (12, 8, HALF)],
        [wide, wide, wide, (27, rows, HALF)],
        name="mid",
    )(column_, r1, r2)

    bit = 1
    while bit < row:
        size = 2 if bit == 1 or bit * 2 >= row else 4
        digit = (lax.axis_index("row") // bit) % size
        parts = [coarse] + [lax.ppermute(coarse, "row", [(i, i ^ (k * bit)) for i in range(row)]) for k in range(1, size)]
        ordered = []
        for place in range(size):
            v = parts[place]
            for m in range(1, size):
                v = jnp.where(digit == m, parts[place ^ m], v)
            ordered.append(v)
        coarse = jnp.concatenate(ordered, 2)
        bit *= size

    x, q, m1, m2 = call(k_fifth, [FINE, FINE, message(8), message(8)], [cube, cube, cube, (512, HALF), FINE], name="fifth")(
        coarse, res, xm, inv3, c3, x, rho, inv, ghost, jnp.asarray(KRON73)
    )
    z1, z2 = swap_z(m1, m2)
    m1, m2 = call(k_later_a, [message(LATER), message(LATER)], name="later_a")(q, inv, z1, z2)
    r1, r2 = swap_a(m1, m2)
    d, y = call(k_later_mean, [FINE, FINE], name="later_mean")(q, inv, ghost, z1, z2)
    return call(k_last, [FINE], [faces, FINE], name="last")(q, inv, d, y, x, ghost, z1, z2, r1, r2)[0]


def solution(mesh):
    gz, row = mesh.shape["gz"], mesh.shape["row"]
    return jax.shard_map(
        functools.partial(per_device, gz, row),
        mesh=mesh,
        in_specs=(P(None, None, None, ("gz", "row")), P(None, ("gz", "row"))),
        out_specs=P(None, None, None, ("gz", "row")),
        check_vma=False,
    )
```

```python
import functools

import jax
import jax.numpy as jnp
import numpy as np
from jax import lax
from jax.experimental import pallas as pl
from jax.experimental.pallas import tpu as pltpu
from jax.sharding import PartitionSpec as P

ITERS = 5
EZ = 4
EA = 4
ER = 16
HALF = 128
GROUP = EA * ER

THETA = 2.2
DELTA = 1.8
RHO = DELTA / THETA
RHO2 = 1.0 / (2.0 * THETA / DELTA - RHO)
C1 = RHO2 * RHO
C2 = 2.0 * RHO2 / DELTA


def points_of(order):
    return -np.cos(np.pi * np.arange(order + 1) / order)


def tables_of(order):
    x = points_of(order)
    n = order + 1
    dist = x[:, None] - x[None, :] + np.eye(n)
    bary = 1.0 / np.prod(dist, axis=1)
    off = bary[None, :] / bary[:, None] / dist * (1.0 - np.eye(n))
    deriv = off - np.diag(off.sum(axis=1))
    place = np.arange(n)
    run = np.ones(n)
    for j in range(1, order // 2 + 1):
        b = 1.0 if 2 * j == order else 2.0
        run = run - b / (4.0 * j * j - 1.0) * np.cos(2.0 * j * place * np.pi / order)
    ends = np.where((place == 0) | (place == order), 1.0, 2.0)
    w = ends / order * run
    k = deriv.T @ np.diag(w) @ deriv
    return w, k


def interp_of(fine, coarse):
    x, y = points_of(fine), points_of(coarse)
    cols = []
    for j in range(coarse + 1):
        v = np.ones(fine + 1)
        for k in range(coarse + 1):
            if k != j:
                v = v * (x - y[k]) / (y[j] - y[k])
        cols.append(v)
    return np.stack(cols, axis=1)


W7, K7 = tables_of(7)
W3, K3 = tables_of(3)
J73 = interp_of(7, 3)
J31 = interp_of(3, 1)


def halves_of(table):
    high = table.astype(jnp.bfloat16)
    return high, (table - high.astype(np.float64)).astype(jnp.bfloat16)


KRON_HIGH, KRON_LOW = halves_of(np.kron(np.kron(J73, J73), J73))
KRON73 = np.concatenate([KRON_HIGH, KRON_HIGH, KRON_LOW], axis=1)


def weighted_sum(coefs, vals):
    total = None
    for c, v in zip(coefs, vals):
        term = v * float(c)
        total = term if total is None else total + term
    return total


def along(table, vals):
    rows, cols = table.shape
    half = cols // 2
    even = [vals[j] + vals[cols - 1 - j] for j in range(half)]
    odd = [vals[j] - vals[cols - 1 - j] for j in range(half)]
    out = [None] * rows
    for i in range(rows // 2):
        e = weighted_sum([(table[i, j] + table[i, cols - 1 - j]) / 2 for j in range(half)], even)
        o = weighted_sum([(table[i, j] - table[i, cols - 1 - j]) / 2 for j in range(half)], odd)
        out[i] = e + o
        out[rows - 1 - i] = e - o
    return out


def pair_of(v):
    high = v.astype(jnp.bfloat16)
    return high, (v - high.astype(jnp.float32)).astype(jnp.bfloat16)


def sub_iota(shape=(8, HALF)):
    return lax.broadcasted_iota(jnp.int32, shape, len(shape) - 2)


def lane_iota(shape=(8, HALF)):
    return lax.broadcasted_iota(jnp.int32, shape, len(shape) - 1)


def column(values):
    it = sub_iota()
    out = jnp.full((8, HALF), float(values[0]), jnp.float32)
    for i in range(1, 8):
        out = jnp.where(it == i, float(values[i]), out)
    return out


def lroll(v, shift):
    n = v.shape[-1]
    shift = shift % n
    return v if shift == 0 else pltpu.roll(v, shift, v.ndim - 1)


def sroll(v, shift):
    n = v.shape[-2]
    shift = shift % n
    return v if shift == 0 else pltpu.roll(v, shift, v.ndim - 2)


def half_of(h):
    return slice(h * HALF, (h + 1) * HALF)


def radial_masks():
    sub, lane = sub_iota(), lane_iota()
    r = lane % ER
    low = (sub == 0) & (r > 0)
    high = (sub == 7) & (r < ER - 1)
    wall = ((sub == 0) & (r == 0)) | ((sub == 7) & (r == ER - 1))
    return low, high, wall


def radial_add(v, masks):
    below = lroll(sroll(v, 1), 1)
    above = lroll(sroll(v, 7), HALF - 1)
    return v + jnp.where(masks[0], below, jnp.where(masks[1], above, 0.0))


def radial_columns():
    return [column([K7[i, (i - s) % 8] for i in range(8)]) for s in range(8)]


def radial_apply(rolls, v):
    total = rolls[0] * v
    for s in range(1, 8):
        total = total + rolls[s] * sroll(v, s)
    return total


def fine_apply(src, dst, base, s_half, sign):
    rolls = radial_columns()
    wr = column(W7)
    for h in range(len(s_half)):
        sl = half_of(h)
        s0, s1, s2 = [v * sign for v in stretch_rows(s_half[h])]
        s0, s1 = s0 * wr, s1 * wr
        for iz in range(8):
            vals = [src[iz, ia, :, sl] for ia in range(8)]
            part_a = along(K7, vals)
            s1z = s1 * float(W7[iz])
            s2z = s2 * float(W7[iz])
            for ia in range(8):
                part = part_a[ia] * s1z + radial_apply(rolls, vals[ia]) * (s2z * float(W7[ia]))
                dst[iz, ia, :, sl] = part if base is None else base[iz, ia, :, sl] + part
        for ia in range(8):
            vals = [src[iz, ia, :, sl] for iz in range(8)]
            part_z = along(K7, vals)
            s0a = s0 * float(W7[ia])
            for iz in range(8):
                dst[iz, ia, :, sl] = dst[iz, ia, :, sl] + part_z[iz] * s0a


def diag_at(s_ref, h, iz, ia, wr, kr):
    sl = half_of(h)
    s0, s1, s2 = (jnp.broadcast_to(s_ref[c : c + 1, sl], (8, HALF)) for c in range(3))
    ends = s0 * float(K7[iz, iz] * W7[ia]) + s1 * float(W7[iz] * K7[ia, ia])
    return ends * wr + s2 * (kr * float(W7[iz] * W7[ia]))


def pack_a(plane, slot):
    place = (lane_iota() // ER) % EA
    out = []
    for i in range(4):
        parts = [plane(0, i), plane(1, i), plane(0, i + 4), plane(1, i + 4)]
        parts = [lroll(v, (s - slot) * ER) for s, v in enumerate(parts)]
        out.append(jnp.where(place == 0, parts[0], jnp.where(place == 1, parts[1], jnp.where(place == 2, parts[2], parts[3]))))
    return out


def unpack_a(msg, slot, h, iz):
    s = h + 2 * (iz // 4)
    return lroll(msg[iz % 4], (slot - s) * ER)


def pack_z(plane, upper):
    low = lane_iota() < GROUP
    out = []
    for i in range(4):
        a, b = plane(i), plane(i + 4)
        out.append(jnp.where(low, lroll(a, GROUP) if upper else a, b if upper else lroll(b, GROUP)))
    return out


def unpack_z(msg, ia, upper):
    m = msg[ia % 4]
    return lroll(m, GROUP) if (ia < 4) == upper else m


def parity(axis):
    return lax.axis_index(axis) % 2 == 0


def choose(flag, a, b):
    return [jnp.where(flag, x, y) for x, y in zip(a, b)]


def got(axis, r1, r2, lo, hi):
    even = parity(axis)
    one = [r1[i] for i in range(lo, hi)]
    two = [r2[i] for i in range(lo, hi)]
    return choose(even, two, one), choose(even, one, two)


def post(axis, lower, upper, m1, m2, start):
    even = parity(axis)
    for i, (lo, up) in enumerate(zip(lower, upper)):
        m1[start + i] = jnp.where(even, up, lo)
        m2[start + i] = jnp.where(even, lo, up)


def place_of():
    return (lane_iota() // ER) % EA


def every_fine():
    for h in range(2):
        for iz in range(8):
            for ia in range(8):
                yield iz, ia, half_of(h)


def join_a(y, iz, h, left, right):
    place, sl = place_of(), half_of(h)
    lo, hi = y[iz, 0, :, sl], y[iz, 7, :, sl]
    y[iz, 0, :, sl] = lo + jnp.where(place > 0, lroll(hi, ER), left)
    y[iz, 7, :, sl] = hi + jnp.where(place < EA - 1, lroll(lo, HALF - ER), right)


def join_z(y, ia, beyond):
    low = lane_iota() < GROUP
    lo0, lo1 = y[0, ia, :, half_of(0)], y[0, ia, :, half_of(1)]
    hi0, hi1 = y[7, ia, :, half_of(0)], y[7, ia, :, half_of(1)]
    up0, up1 = lroll(hi0, GROUP), lroll(hi1, GROUP)
    dn0, dn1 = lroll(lo0, GROUP), lroll(lo1, GROUP)
    y[0, ia, :, half_of(0)] = lo0 + jnp.where(low, beyond, up0)
    y[0, ia, :, half_of(1)] = lo1 + jnp.where(low, up0, up1)
    y[7, ia, :, half_of(0)] = hi0 + jnp.where(low, dn0, dn1)
    y[7, ia, :, half_of(1)] = hi1 + jnp.where(low, dn1, beyond)


def sum_inside(y):
    for iz in range(8):
        for h in range(2):
            join_a(y, iz, h, 0.0, 0.0)
    for ia in range(8):
        join_z(y, ia, 0.0)


FIRST, LATER = 17, 9


def faces_z(q, inverse):
    top_q = pack_z(lambda ia: q[7, ia, :, half_of(1)], True)
    bottom_q = pack_z(lambda ia: q[0, ia, :, half_of(0)], False)

    def behind(ia, h):
        nodes = range(7) if h else range(1, 8)
        row = K7[7 if h else 0] / THETA
        return weighted_sum([row[j] for j in nodes], [inverse(j, ia, h) * q[j, ia, :, half_of(h)] for j in nodes])

    top_t = pack_z(lambda ia: behind(ia, 1), True)
    bottom_t = pack_z(lambda ia: behind(ia, 0), False)
    return bottom_q + bottom_t, top_q + top_t


def edge_lines(f, ia, h):
    slot = lane_iota() // ER
    source = (EA - 1 if ia else 0) + (EA if h else 0)
    out = None
    for j in range(1, 8):
        v = lroll(f[7 - j if h else j, ia, :, half_of(h)], (j - 1 - source) * ER)
        out = v if out is None else jnp.where(slot == j - 1, v, out)
    return out


def k_first(rhs_any, s_any, q, g, m1, m2, s_ref, rhs, sems):
    copy_s = pltpu.make_async_copy(s_any, s_ref, sems.at[0])
    copy_rhs = pltpu.make_async_copy(rhs_any, rhs, sems.at[1])
    copy_s.start()
    copy_rhs.start()
    masks = radial_masks()
    wr, kr = column(W7), column(np.diag(K7))
    copy_s.wait()
    for iz, ia, sl in every_fine():
        g[iz, ia, :, sl] = radial_add(diag_at(s_ref, sl.start // HALF, iz, ia, wr, kr), masks)
    sum_inside(g)
    copy_rhs.wait()
    for iz, ia, sl in every_fine():
        q[iz, ia, :, sl] = radial_add(rhs[iz, ia, :, sl], masks)
    sum_inside(q)
    bottom, top = faces_z(q, lambda iz, ia, h: jnp.where(masks[2], 0.0, 1.0 / g[iz, ia, :, half_of(h)]))
    post("gz", bottom, top, m1, m2, 0)
    post(
        "gz",
        pack_z(lambda ia: g[0, ia, :, half_of(0)], False),
        pack_z(lambda ia: g[7, ia, :, half_of(1)], True),
        m1,
        m2,
        8,
    )
    lines = [[edge_lines(f, ia, h) for f in (q, g) for ia in (0, 7)] for h in range(2)]
    post("gz", lines[0], lines[1], m1, m2, 12)
    even = parity("gz")
    top, bottom = lroll(s_ref[:, half_of(1)], GROUP), s_ref[:, half_of(0)]
    m1[16] = jnp.where(even, top, bottom)
    m2[16] = jnp.where(even, bottom, top)


def with_z(f, beyond, iz, ia, h):
    v = f[iz, ia, :, half_of(h)]
    low = lane_iota() < GROUP
    if iz == 0 and h == 0:
        v = v + jnp.where(low, beyond[ia], 0.0)
    if iz == 7 and h == 1:
        v = v + jnp.where(low, 0.0, beyond[ia])
    return v


def both_z(below, above, ia):
    return jnp.where(lane_iota() < GROUP, unpack_z(below, ia, False), unpack_z(above, ia, True))


def from_z(z1, z2, start):
    below, above = got("gz", z1, z2, start, start + 4)
    return [both_z(below, above, ia) for ia in range(8)]


def send_a(q, qz, inverse, m1, m2):
    full = lambda iz, ia, h: with_z(q, qz, iz, ia, h)
    post("row", pack_a(lambda h, iz: full(iz, 0, h), 0), pack_a(lambda h, iz: full(iz, 7, h), EA - 1), m1, m2, 0)
    left, right = {}, {}
    for h in range(2):
        for iz in range(8):
            scaled = [inverse(iz, ia, h) * full(iz, ia, h) for ia in range(8)]
            left[h, iz] = weighted_sum(K7[0, 1:] / THETA, scaled[1:])
            right[h, iz] = weighted_sum(K7[7, :7] / THETA, scaled[:7])
    post("row", pack_a(lambda h, iz: left[h, iz], 0), pack_a(lambda h, iz: right[h, iz], EA - 1), m1, m2, 4)


def k_first_a(q, g, s_ref, z1, z2, m1, m2):
    wall = radial_masks()[2]
    gz = from_z(z1, z2, 8)
    full = lambda iz, ia, h: with_z(g, gz, iz, ia, h)
    send_a(q, from_z(z1, z2, 0), lambda iz, ia, h: jnp.where(wall, 0.0, 1.0 / full(iz, ia, h)), m1, m2)
    post("row", pack_a(lambda h, iz: full(iz, 0, h), 0), pack_a(lambda h, iz: full(iz, 7, h), EA - 1), m1, m2, 8)
    below, above = got("gz", z1, z2, 12, 16)
    post("row", [below[0], below[2], above[0], above[2]], [below[1], below[3], above[1], above[3]], m1, m2, 12)
    s_below, s_above = got("gz", z1, z2, 16, 17)
    s_z = jnp.where(lane_iota() < GROUP, s_below[0], lroll(s_above[0], GROUP))
    place = place_of()
    even = parity("row")

    def stretch_of(slot):
        parts = [s_ref[:, half_of(0)], s_ref[:, half_of(1)], s_z]
        parts = [lroll(v, (s - slot) * ER) for s, v in enumerate(parts)]
        return jnp.where(place == 0, parts[0], jnp.where(place == 1, parts[1], parts[2]))

    to_left, to_right = stretch_of(0), stretch_of(EA - 1)
    m1[16] = jnp.where(even, to_right, to_left)
    m2[16] = jnp.where(even, to_left, to_right)


def complete(f, fz, r1, r2, start, put):
    place = place_of()
    left, right = got("row", r1, r2, start, start + 4)
    for h in range(2):
        for iz in range(8):
            for ia in range(8):
                v = with_z(f, fz, iz, ia, h)
                if ia == 0:
                    v = v + jnp.where(place == 0, unpack_a(left, 0, h, iz), 0.0)
                if ia == 7:
                    v = v + jnp.where(place == EA - 1, unpack_a(right, EA - 1, h, iz), 0.0)
                put(iz, ia, h, v)


def halves(ghost):
    return [ghost[4], ghost[5]]


def stretch_rows(v):
    return [jnp.broadcast_to(v[k : k + 1], (8, HALF)) for k in range(3)]


def meanwhile(q, qz, inverse, ghost, d, y):
    place = place_of()
    for iz, ia, sl in every_fine():
        h = sl.start // HALF
        v = inverse(iz, ia, h) * with_z(q, qz, iz, ia, h) * (1.0 / THETA)
        if ia == 0:
            v = jnp.where(place == 0, 0.0, v)
        if ia == 7:
            v = jnp.where(place == EA - 1, 0.0, v)
        d[iz, ia, :, sl] = v
    fine_apply(d, y, None, ghost, 1.0)


def k_first_mean(q, g, s_ref, z1, z2, inv, d, y):
    wall = radial_masks()[2]
    gz = from_z(z1, z2, 8)
    for iz, ia, sl in every_fine():
        inv[iz, ia, :, sl] = jnp.where(wall, 0.0, 1.0 / with_z(g, gz, iz, ia, sl.start // HALF))
    meanwhile(q, from_z(z1, z2, 0), lambda iz, ia, h: inv[iz, ia, :, half_of(h)], [s_ref[:, half_of(0)], s_ref[:, half_of(1)]], d, y)


def k_later_mean(q, inv, ghost, qz, d, y):
    meanwhile(q, qz, lambda iz, ia, h: inv[iz, ia, :, half_of(h)], halves(ghost), d, y)


def with_face(d, face):
    def whole(iz, ia, h):
        v = d[iz, ia, :, half_of(h)]
        if ia == 0:
            v = jnp.where(place_of() == 0, face[iz, h], v)
        if ia == 7:
            v = jnp.where(place_of() == EA - 1, face[iz, h], v)
        return v

    return whole


def edge_faces(q, qz, r1, r2, put):
    place = place_of()
    left, right = got("row", r1, r2, 0, 4)
    for h in range(2):
        for iz in range(8):
            low = with_z(q, qz, iz, 0, h) + jnp.where(place == 0, unpack_a(left, 0, h, iz), 0.0)
            high = with_z(q, qz, iz, 7, h) + jnp.where(place == EA - 1, unpack_a(right, EA - 1, h, iz), 0.0)
            put(iz, h, low, high)


def add_beyond(d, y0, y, face, s_own, s_n, s_z, s_m, t_left, t_right, t_z):
    place, low = place_of(), lane_iota() < GROUP
    wr, rolls = column(W7), radial_columns()
    w0, k00 = float(W7[0]), float(K7[0, 0])
    first, last = place == 0, place == EA - 1
    k_face = [jnp.where(last, float(K7[ia, 7]), float(K7[ia, 0])) for ia in range(8)]
    t_edge = []
    for h in range(2):
        sl = half_of(h)
        s0, s1, s2 = s_n[h]
        o0, o1, o2 = s_own[h]
        vals = [face[iz, h] for iz in range(8)]
        part_z = along(K7, vals)
        for iz in range(8):
            t = jnp.where(last, unpack_a(t_right, EA - 1, h, iz), unpack_a(t_left, 0, h, iz))
            if (h, iz) in ((0, 0), (1, 7)):
                t_edge.append(t)
            wz = float(W7[iz])
            part_z_w, part_r = w0 * wr * part_z[iz], (w0 * wz) * radial_apply(rolls, vals[iz])
            beyond = (s1 * wr) * (vals[iz] * k00 + t) * wz + s0 * part_z_w + s2 * part_r
            inside = o0 * part_z_w + o2 * part_r
            lines = (o1 * wr) * (vals[iz] * wz)
            for ia in range(1, 7):
                y[iz, ia, :, sl] = y0[iz, ia, :, sl] + lines * k_face[ia]
            lo = y0[iz, 0, :, sl] + lines * k_face[0] + jnp.where(first, inside, 0.0)
            hi = y0[iz, 7, :, sl] + lines * k_face[7] + jnp.where(last, inside, 0.0)
            y[iz, 0, :, sl] = lo + jnp.where(first, beyond, lroll(hi, ER))
            y[iz, 7, :, sl] = hi + jnp.where(last, beyond, lroll(lo, HALF - ER))
    t_a = jnp.where(low, t_edge[0], t_edge[1])
    vals = [jnp.where(low, d(0, ia, 0), d(7, ia, 1)) for ia in range(8)]
    part_a = along(K7, vals)
    s0, s1, s2 = s_z
    beyond = []
    for ia in range(8):
        wa = float(W7[ia])
        beyond.append((s0 * wr) * (vals[ia] * k00 + t_z[ia]) * wa + w0 * (s1 * wr * part_a[ia] + s2 * wa * radial_apply(rolls, vals[ia])))
    edge = jnp.where(place == EA - 1, vals[7], vals[0])
    edge_t = jnp.where(place == EA - 1, t_z[7], t_z[0])
    s0, s1, s2 = s_m
    corner = w0 * wr * (s0 * (edge * k00 + edge_t) + s1 * (edge * k00 + t_a)) + (w0 * w0) * s2 * radial_apply(rolls, edge)
    lo = beyond[0] + jnp.where(place > 0, lroll(beyond[7], ER), corner)
    hi = beyond[7] + jnp.where(place < EA - 1, lroll(beyond[0], -ER), corner)
    beyond[0], beyond[7] = lo, hi
    for ia in range(8):
        join_z(y, ia, beyond[ia])


def k_first_done(rhs, q, g, inv0, d, y0, s_ref, table, z1, z2, r1, r2, inv, x, rho, mid, up, down, ghost, face, y):
    masks = radial_masks()
    place, low = place_of(), lane_iota() < GROUP
    first, last = place == 0, place == EA - 1
    for iz in range(8):
        for h in range(2):
            for ia in range(1, 7):
                inv[iz, ia, :, half_of(h)] = inv0[iz, ia, :, half_of(h)]
    gz, qz = from_z(z1, z2, 8), from_z(z1, z2, 0)
    g_left, g_right = got("row", r1, r2, 8, 12)
    for iz in range(8):
        for h in range(2):
            v = with_z(g, gz, iz, 0, h) + jnp.where(first, unpack_a(g_left, 0, h, iz), 0.0)
            inv[iz, 0, :, half_of(h)] = jnp.where(masks[2], 0.0, 1.0 / v)
            v = with_z(g, gz, iz, 7, h) + jnp.where(last, unpack_a(g_right, EA - 1, h, iz), 0.0)
            inv[iz, 7, :, half_of(h)] = jnp.where(masks[2], 0.0, 1.0 / v)

    def put_face(iz, h, lo, hi):
        lo, hi = inv[iz, 0, :, half_of(h)] * lo, inv[iz, 7, :, half_of(h)] * hi
        face[iz, h] = jnp.where(first, lo, jnp.where(last, hi, 0.0)) * (1.0 / THETA)

    edge_faces(q, qz, r1, r2, put_face)
    below, above = got("gz", z1, z2, 16, 17)
    left, right = got("row", r1, r2, 16, 17)
    ghost[2] = jnp.where(low, below[0], lroll(above[0], GROUP))
    ghost[4] = s_ref[:, half_of(0)]
    ghost[5] = s_ref[:, half_of(1)]
    for k, s in ((0, 0), (1, 1), (3, 2)):
        ghost[k] = jnp.where(place == EA - 1, lroll(right[0], (EA - 1 - s) * ER), lroll(left[0], -s * ER))
    z_lines = got("gz", z1, z2, 12, 16)
    a_lines = got("row", r1, r2, 12, 16)
    slot = lane_iota() // ER
    weight = jnp.zeros((8, HALF), jnp.float32)
    for j in range(1, 8):
        weight = jnp.where(slot == j - 1, float(K7[0, j] / THETA), weight)
    t_edge = [[None, None], [None, None]]
    for side in range(2):
        for end in range(2):
            qs = z_lines[end][side] + a_lines[side][2 * end]
            gs = z_lines[end][2 + side] + a_lines[side][2 * end + 1]
            v = jnp.where(masks[2] | (slot == 7), 0.0, weight * qs / gs)
            for shift in (64, 32, 16):
                v = v + lroll(v, shift)
            t_edge[side][end] = v
    t_z = from_z(z1, z2, 4)
    t_z[0] = jnp.where(place == 0, jnp.where(low, t_edge[0][0], t_edge[0][1]), t_z[0])
    t_z[7] = jnp.where(place == EA - 1, jnp.where(low, t_edge[1][0], t_edge[1][1]), t_z[7])
    t_left, t_right = got("row", r1, r2, 4, 8)
    s_n, s_z, s_m = [stretch_rows(ghost[0]), stretch_rows(ghost[1])], stretch_rows(ghost[2]), stretch_rows(ghost[3])
    s_own = [stretch_rows(v) for v in halves(ghost)]
    whole = with_face(d, face)
    add_beyond(whole, y0, y, face, s_own, s_n, s_z, s_m, t_left, t_right, t_z)

    def put_x(iz, ia, h, v):
        sl = half_of(h)
        r = v - radial_add(y[iz, ia, :, sl], masks)
        x[iz, ia, :, sl] = (1.0 + C1) * whole(iz, ia, h) + C2 * inv[iz, ia, :, sl] * r

    complete(q, qz, r1, r2, 0, put_x)
    fine_apply(x, rho, rhs, halves(ghost), -1.0)
    for iz, ia, sl in every_fine():
        y[iz, ia, :, sl] = jnp.where(masks[2], 0.0, rho[iz, ia, :, sl])
    high, low_part = pair_of(y[...].reshape(512, 256))
    sums = jnp.dot(table[...], high, preferred_element_type=jnp.float32)
    sums = sums[0:112] + sums[112:224] + jnp.dot(table[0:112, :], low_part, preferred_element_type=jnp.float32)
    inner = lane_iota((56, HALF)) % ER > 0
    for h in range(2):
        sl = half_of(h)
        mid[:, sl] = sums[0:56, sl] + jnp.where(inner, lroll(sums[56:112, sl], 1), 0.0)
    mid[48:56, :] = s_ref[...]
    up[0:56, :] = mid[...]
    down[0:56, :] = mid[...]
    for iz, ia, sl in every_fine():
        y[iz, ia, :, sl] = radial_add(rho[iz, ia, :, sl], masks)
    sum_inside(y)
    bottom, top = faces_z(y, lambda iz, ia, h: inv[iz, ia, :, half_of(h)])
    for i in range(8):
        up[56 + 8 * (i // 2) : 64 + 8 * (i // 2), half_of(i % 2)] = top[i]
        down[56 + 8 * (i // 2) : 64 + 8 * (i // 2), half_of(i % 2)] = bottom[i]


def k_last(q, inv, d, y0, x, ghost, qz, tz, r1, r2, out, face, y):
    masks = radial_masks()
    place = place_of()
    first, last = place == 0, place == EA - 1

    def put_face(iz, h, lo, hi):
        lo, hi = inv[iz, 0, :, half_of(h)] * lo, inv[iz, 7, :, half_of(h)] * hi
        face[iz, h] = jnp.where(first, lo, jnp.where(last, hi, 0.0)) * (1.0 / THETA)

    edge_faces(q, qz, r1, r2, put_face)
    t_z = [tz[ia] for ia in range(8)]
    left, right = got("row", r1, r2, 8, 9)
    t_z[0] = t_z[0] + jnp.where(first, lroll(left[0], -(EA - 1) * ER), 0.0)
    t_z[7] = t_z[7] + jnp.where(last, lroll(right[0], (EA - 1) * ER), 0.0)
    t_left, t_right = got("row", r1, r2, 4, 8)
    s_n, s_z, s_m = [stretch_rows(ghost[0]), stretch_rows(ghost[1])], stretch_rows(ghost[2]), stretch_rows(ghost[3])
    s_own = [stretch_rows(v) for v in halves(ghost)]
    whole = with_face(d, face)
    add_beyond(whole, y0, y, face, s_own, s_n, s_z, s_m, t_left, t_right, t_z)

    def put_out(iz, ia, h, v):
        sl = half_of(h)
        r = v - radial_add(y[iz, ia, :, sl], masks)
        out[iz, ia, :, sl] = x[iz, ia, :, sl] + (1.0 + C1) * whole(iz, ia, h) + C2 * inv[iz, ia, :, sl] * r

    complete(q, qz, r1, r2, 0, put_out)


NODES = [(iz, ia, ir) for iz in range(3) for ia in range(3) for ir in range(3)]


def node(iz, ia, ir):
    return (iz * 3 + ia) * 3 + ir


def restrict_rows():
    picks = [(iz, ia, ir) for iz, ia, ir in NODES]
    picks += [(iz, 3, ir) for iz in range(3) for ir in range(3)]
    picks += [(3, ia, ir) for ia in range(3) for ir in range(3)]
    picks += [(3, 3, ir) for ir in range(3)]
    out = np.zeros((112, 512))
    for i, (iz, ia, ir) in enumerate(picks):
        out[i] = np.kron(np.kron(J73[:, iz], J73[:, ia]), J73[:, ir])
        if ir == 0:
            out[56 + i] = np.kron(np.kron(J73[:, iz], J73[:, ia]), J73[:, 3])
    return np.concatenate(halves_of(out), axis=0)


RESTRICT = restrict_rows()
PACKED = 17


def prev_z(v):
    return sroll(v, 1)


def prev_a(v):
    return lroll(v, ER)


def prev_r(v):
    return lroll(v, 1)


def next_z(v):
    return sroll(v, -1)


def next_a(v):
    return lroll(v, -ER)


def next_r(v):
    return lroll(v, -1)


def mid_coefs(s):
    prev = (prev_z, prev_a, prev_r)
    out = []
    for direction in range(3):
        one, two = [k for k in range(3) if k != direction]
        table = {}
        for e1 in range(2):
            v = s[direction] * float(W3[e1])
            v = v + prev[one](v) if e1 == 0 else v
            for e2 in range(2):
                u = v * float(W3[e2])
                table[e1, e2] = u + prev[two](u) if e2 == 0 else u
        out.append(table)
    return out


def mid_inverse(c, inner):
    out = {}
    for ez in range(2):
        for ea in range(2):
            for er in range(2):
                total = None
                for v, e, prev in ((c[0][ea, er], ez, prev_z), (c[1][ez, er], ea, prev_a), (c[2][ez, ea], er, prev_r)):
                    term = v * float(K3[1, 1]) if e else (v + prev(v)) * float(K3[0, 0])
                    total = term if total is None else total + term
                value = 1.0 / total
                out[ez, ea, er] = value if er else jnp.where(inner, value, 0.0)
    return out


def end(i):
    return 0 if i == 0 else 1


def mid_apply(get, nz, na, nr, c, acc):
    for ia in range(3):
        for ir in range(3):
            part = along(K3, [get(0, ia, ir), get(1, ia, ir), get(2, ia, ir), nz(ia, ir)])
            part = [v * c[0][end(ia), end(ir)] for v in part]
            acc[node(0, ia, ir)] = part[0] + prev_z(part[3])
            acc[node(1, ia, ir)] = part[1]
            acc[node(2, ia, ir)] = part[2]
    for iz in range(3):
        for ir in range(3):
            part = along(K3, [get(iz, 0, ir), get(iz, 1, ir), get(iz, 2, ir), na(iz, ir)])
            part = [v * c[1][end(iz), end(ir)] for v in part]
            acc[node(iz, 0, ir)] = acc[node(iz, 0, ir)] + part[0] + prev_a(part[3])
            acc[node(iz, 1, ir)] = acc[node(iz, 1, ir)] + part[1]
            acc[node(iz, 2, ir)] = acc[node(iz, 2, ir)] + part[2]
    for iz in range(3):
        for ia in range(3):
            part = along(K3, [get(iz, ia, 0), get(iz, ia, 1), get(iz, ia, 2), nr(iz, ia)])
            part = [v * c[2][end(iz), end(ia)] for v in part]
            acc[node(iz, ia, 0)] = acc[node(iz, ia, 0)] + part[0] + prev_r(part[3])
            acc[node(iz, ia, 1)] = acc[node(iz, ia, 1)] + part[1]
            acc[node(iz, ia, 2)] = acc[node(iz, ia, 2)] + part[2]


def k_column(rows, *refs):
    blocks, out, wide = refs[:-2], refs[-2], refs[-1]
    for k, block in enumerate(blocks):
        for z in range(EZ):
            v = block[0:56, half_of(z // 2)]
            wide[pl.ds((2 - EZ * k + z) % rows, 56, stride=rows), :] = lroll(v, GROUP) if z % 2 else v

    def entry(i):
        return wide[i * rows : (i + 1) * rows, :]

    shape = (rows, HALF)
    lane = lane_iota(shape)
    own, face = {}, {}
    for iz, ia, ir in NODES:
        v = entry(node(iz, ia, ir))
        own[iz, ia, ir] = v + prev_z(entry(36 + ia * 3 + ir)) if iz == 0 else v
    for iz in range(3):
        for ir in range(3):
            v = entry(27 + iz * 3 + ir)
            v = v + prev_z(entry(45 + ir)) if iz == 0 else v
            face[iz * 3 + ir] = v
            own[iz, 0, ir] = own[iz, 0, ir] + jnp.where(lane >= ER, prev_a(v), 0.0)
    flat = [own[n] for n in NODES] + [entry(48 + k) for k in range(3)]
    for p in range(15):
        out[p] = jnp.where(lane < GROUP, flat[2 * p], lroll(flat[2 * p + 1], GROUP))
    for p in range(2):
        v = None
        for slot, i in enumerate(range(8 * p, min(9, 8 * p + 8))):
            moved = lroll(face[i], (slot - (EA - 1)) * ER)
            v = moved if v is None else jnp.where(lane // ER == slot, moved, v)
        out[15 + p] = v


def k_mid(own, r1, r2, coarse, res, x, inv_out, c_out, far, b, d, y, y2):
    rows = own.shape[1]
    even = parity("row")
    lane = lane_iota((rows, HALF))

    def sides(i):
        one, two = r1[i], r2[i]
        return jnp.where(even, two, one), jnp.where(even, one, two)

    def halo(i):
        p, base = i // 2, GROUP * (i % 2)
        left, right = sides(p)
        left, right = lroll(left, 96 - base), lroll(right, 96 - base)
        mine = lroll(own[p], 32 - base)
        first = jnp.where(lane < 32, left, jnp.where(lane < 96, mine, right))
        return first, jnp.where(lane < 32, right, left)

    for iz, ia, ir in NODES:
        n = node(iz, ia, ir)
        first, second = halo(n)
        if ia == 0:
            i = iz * 3 + ir
            left, _ = sides(15 + i // 8)
            slot = i % 8
            from_left = lroll(left, 32 - slot * ER)
            to_right = lroll(own[15 + i // 8], 96 - slot * ER)
            first = first + jnp.where((lane >= 32) & (lane < 48), from_left, jnp.where((lane >= 96) & (lane < 112), to_right, 0.0))
        b[n, :, 0:HALF] = first
        b[n, :, HALF:] = second
    s = []
    for k in range(3):
        first, second = halo(27 + k)
        second = jnp.where((lane >= 32) & (lane < 96), 1.0, second)
        coarse[1 + k] = lroll(first, -32)[:, 0:GROUP]
        s.append(jnp.concatenate([first, second], axis=1))
        for layer, (lower, upper) in enumerate(((1, 6), (0, 7))):
            lo, hi = first[lower : lower + 1], first[upper : upper + 1]
            low, place = lane[0:1] < GROUP, ((lane // ER) % EA)[0:1]
            far[layer, k : k + 1] = jnp.where(low, lroll(lo, -32), lroll(hi, 32))
            left = jnp.where(low, lroll(lo, -16), lroll(hi, 48))
            right = jnp.where(low, lroll(lo, -48), lroll(hi, 16))
            far[2 + layer, k : k + 1] = jnp.where(place == EA - 1, right, left)

    inner = lane_iota((rows, 2 * HALF)) % ER > 0
    c = mid_coefs(s)
    inverse = mid_inverse(c, inner)
    for i, e in enumerate([(ez, ea, er) for ez in range(2) for ea in range(2) for er in range(2)]):
        inv_out[i] = inverse[e][:, 0:HALF]
    for k in range(3):
        for i, e in enumerate([(0, 0), (0, 1), (1, 0), (1, 1)]):
            c_out[4 * k + i] = c[k][e][:, 0:HALF]

    def kind(iz, ia, ir):
        return inverse[end(iz), end(ia), end(ir)]

    def get(iz, ia, ir):
        return d[node(iz, ia, ir)]

    for iz, ia, ir in NODES:
        n = node(iz, ia, ir)
        d[n] = kind(iz, ia, ir) * b[n] * (1.0 / THETA)
    mid_apply(
        get,
        lambda ia, ir: next_z(get(0, ia, ir)),
        lambda iz, ir: next_a(get(iz, 0, ir)),
        lambda iz, ia: next_r(get(iz, ia, 0)),
        c,
        y,
    )
    for iz, ia, ir in NODES:
        n = node(iz, ia, ir)
        d[n] = (1.0 + C1) * d[n] + C2 * kind(iz, ia, ir) * (b[n] - y[n])
        x[n] = d[n, :, 0:HALF]

    def near(iz, ia, ir):
        return d[node(iz, ia, ir), :, 0:HALF]

    mid_apply(
        near,
        lambda ia, ir: next_z(near(0, ia, ir)),
        lambda iz, ir: next_a(get(iz, 0, ir))[:, 0:HALF],
        lambda iz, ia: next_r(near(iz, ia, 0)),
        [{e: v[:, 0:HALF] for e, v in t.items()} for t in c],
        y2,
    )
    inner = lane % ER > 0
    for iz, ia, ir in NODES:
        n = node(iz, ia, ir)
        r = b[n, :, 0:HALF] - y2[n]
        r = r if ir else jnp.where(inner, r, 0.0)
        y2[n] = r
        res[n] = r

    def gather(v, prev):
        return v[0] + v[1] * float(J31[1, 0]) + v[2] * float(J31[2, 0]) + prev(v[1] * float(J31[1, 1]) + v[2] * float(J31[2, 1]))

    planes = []
    for iz in range(3):
        lines = [gather([y2[node(iz, ia, ir)] for ir in range(3)], prev_r) for ia in range(3)]
        planes.append(gather(lines, prev_a))
    vertex = jnp.where(inner, gather(planes, prev_z), 0.0)
    coarse[0] = lroll(vertex, -32)[:, 0:GROUP]


def k_far(far, inv):
    masks, place = radial_masks(), place_of()
    wr, kr = column(W7), column(np.diag(K7))
    near, next_, near_n, next_n = [stretch_rows(far[i]) for i in range(4)]

    def diag(s, iz, ia):
        return (s[0] * float(K7[iz, iz] * W7[ia]) + s[1] * float(W7[iz] * K7[ia, ia])) * wr + s[2] * (kr * float(W7[iz] * W7[ia]))

    for j in range(1, 8):

        def whole(s, t, ia):
            v = diag(s, j, ia)
            return radial_add(v + diag(t, 0, ia) if j == 7 else v, masks)

        line = [whole(near, next_, ia) for ia in range(8)]
        beyond = whole(near_n, next_n, 0)
        lo = line[0] + jnp.where(place > 0, lroll(line[7], ER), beyond)
        hi = line[7] + jnp.where(place < EA - 1, lroll(line[0], -ER), beyond)
        line[0], line[7] = lo, hi
        for ia in range(8):
            inv[j - 1, ia] = jnp.where(masks[2], 0.0, 1.0 / line[ia])


def vertex_solve(s0, s1, s2, b):
    shape = b.shape
    inner = (lane_iota(shape) % ER) > 0

    def pair(v, f):
        return v + f(v)

    edge_z = 0.5 * pair(pair(s0, prev_a), prev_r)
    edge_a = 0.5 * pair(pair(s1, prev_z), prev_r)
    edge_r = 0.5 * pair(pair(s2, prev_z), prev_a)
    back_z, back_a, back_r = prev_z(edge_z), prev_a(edge_a), prev_r(edge_r)
    middle = edge_z + back_z + edge_a + back_a + edge_r + back_r

    def operate(q):
        y = middle * q - edge_z * next_z(q) - back_z * prev_z(q)
        y = y - edge_a * next_a(q) - back_a * prev_a(q)
        y = y - edge_r * next_r(q) - back_r * prev_r(q)
        return jnp.where(inner, y, 0.0)

    def total(v):
        return jnp.sum(jnp.sum(v, axis=0, keepdims=True), axis=1, keepdims=True)

    e = jnp.zeros(shape, jnp.float32)
    r = b
    q = b
    rr = total(r * r)
    for _ in range(ITERS):
        y = operate(q)
        alpha = rr / total(q * y)
        e = e + alpha * q
        r = r - alpha * y
        rn = total(r * r)
        q = r + (rn / rr) * q
        rr = rn
    return e


def k_fifth(
    whole, res, xm, inv3, c_in, x, rho, inv, ghost, kron, far, inv_far, from_below, from_above, x_out, q, qz, tz, m1, m2, lift, dm, rm, xs, g, gf, yf
):
    e = vertex_solve(whole[1], whole[2], whole[3], whole[0])
    rows, lanes = e.shape
    e = pltpu.roll(e, (lanes + 32 - GROUP * lax.axis_index("row")) % lanes, 1)
    corner = {}
    for cz in range(2):
        for ca in range(2):
            for cr in range(2):
                v = next_z(e) if cz else e
                corner[cz, ca, cr] = lroll(v, -(ca * ER + cr))[:, 0:HALF]

    def three(a, b):
        return [a] + [a * float(J31[i, 0]) + b * float(J31[i, 1]) for i in (1, 2)]

    along_r = {(cz, ca): three(corner[cz, ca, 0], corner[cz, ca, 1]) for cz in range(2) for ca in range(2)}
    along_ra = {cz: [three(along_r[cz, 0][ir], along_r[cz, 1][ir]) for ir in range(3)] for cz in range(2)}
    beyond_a = {ir: three(along_r[0, 1][ir], along_r[1, 1][ir]) for ir in range(3)}
    for ia in range(3):
        for ir in range(3):
            for iz, v in enumerate(three(along_ra[0][ir][ia], along_ra[1][ir][ia])):
                lift[node(iz, ia, ir)] = v

    c = [{e_: c_in[4 * k + i] for i, e_ in enumerate([(0, 0), (0, 1), (1, 0), (1, 1)])} for k in range(3)]

    def kind(iz, ia, ir):
        return inv3[(end(iz) * 2 + end(ia)) * 2 + end(ir)]

    def get_lift(iz, ia, ir):
        return lift[node(iz, ia, ir)]

    def get_d(iz, ia, ir):
        return dm[node(iz, ia, ir)]

    mid_apply(
        get_lift,
        lambda ia, ir: along_ra[1][ir][ia],
        lambda iz, ir: beyond_a[ir][iz],
        lambda iz, ia: next_r(get_lift(iz, ia, 0)),
        c,
        rm,
    )
    for iz, ia, ir in NODES:
        n = node(iz, ia, ir)
        r = kind(iz, ia, ir) * (res[n] - rm[n])
        dm[n] = r * (1.0 / THETA)
        lift[n] = lift[n] + xm[n] + ((1.0 + C1) / THETA + C2) * r
    mid_apply(
        get_d,
        lambda ia, ir: next_z(get_d(0, ia, ir)),
        lambda iz, ir: next_a(get_d(iz, 0, ir)),
        lambda iz, ia: next_r(get_d(iz, ia, 0)),
        c,
        rm,
    )
    for iz, ia, ir in NODES:
        n = node(iz, ia, ir)
        lift[n] = lift[n] - C2 * kind(iz, ia, ir) * rm[n]
    for iz in range(4):
        for ia in range(4):
            for ir in range(4):
                v = lift[node(iz % 3, ia % 3, ir % 3)]
                v = lroll(v, -(ia // 3 * ER + ir // 3))
                v = next_z(v) if iz == 3 else v
                n = (iz * 4 + ia) * 4 + ir
                xs[n * rows : (n + 1) * rows, :] = v
    low = lane_iota((64, HALF)) < GROUP
    cols = []
    for h in range(2):
        one = xs[pl.ds(2 + 2 * h, 64, stride=rows), :]
        two = xs[pl.ds(3 + 2 * h, 64, stride=rows), :]
        cols.append(jnp.where(low, lroll(one, -32), lroll(two, 32)))
    for lower, upper in ((1, 6), (0, 7)):
        one = xs[pl.ds(lower, 64, stride=rows), :]
        one = jnp.concatenate([one[48:64], one[32:48], one[16:32], one[0:16]], axis=0)
        two = xs[pl.ds(upper, 64, stride=rows), :]
        cols.append(jnp.where(low, lroll(one, -32), lroll(two, 32)))
    high, low_part = pair_of(jnp.concatenate(cols, axis=1))
    raised = jnp.dot(kron[...], jnp.concatenate([high, low_part, high], axis=0), preferred_element_type=jnp.float32)
    g[...] = raised[:, 0:256].reshape(8, 8, 8, 256)
    gf[...] = raised[:, 256:512].reshape(8, 8, 8, 256)
    for iz, ia, sl in every_fine():
        x_out[iz, ia, :, sl] = x[iz, ia, :, sl] + g[iz, ia, :, sl]
    masks = radial_masks()
    fine_apply(g, q, rho, halves(ghost), -1.0)
    for iz, ia, sl in every_fine():
        q[iz, ia, :, sl] = radial_add(q[iz, ia, :, sl], masks)
    sum_inside(q)

    fine_apply(gf, yf, None, [far[0]], 1.0)
    s0, s1, s2 = stretch_rows(far[1])
    wr, rolls, place = column(W7), radial_columns(), place_of()
    second = half_of(1)
    part_a = along(K7, [gf[0, ia, :, second] for ia in range(8)])
    for ia in range(8):
        part_z = weighted_sum(K7[0], [gf[j, ia, :, second] for j in range(8)])
        part_r = radial_apply(rolls, gf[0, ia, :, second])
        v = s0 * wr * part_z * float(W7[ia]) + (s1 * wr * part_a[ia] + s2 * part_r * float(W7[ia])) * float(W7[0])
        yf[7, ia] = yf[7, ia] + v
    for j in range(8):
        line = [radial_add(yf[j, ia], masks) for ia in range(8)]
        lo = line[0] + jnp.where(place > 0, lroll(line[7], ER), 0.0)
        hi = line[7] + jnp.where(place < EA - 1, lroll(line[0], -ER), 0.0)
        line[0], line[7] = lo, hi
        for ia in range(8):
            if j:
                line[ia] = inv_far[j - 1, ia] * line[ia] * float(K7[0, j] / THETA)
            yf[j, ia] = line[ia]

    def entries(block, start):
        out = []
        for i in range(start, start + 4):
            out.append(block[56 + 8 * (i // 2) : 64 + 8 * (i // 2), half_of(i % 2)])
        return out

    q_below, q_above, t_below, t_above = entries(from_below, 0), entries(from_above, 0), entries(from_below, 4), entries(from_above, 4)
    for ia in range(8):
        qz[ia] = both_z(q_below, q_above, ia) - yf[0, ia]
        total = yf[1, ia]
        for j in range(2, 8):
            total = total + yf[j, ia]
        tz[ia] = both_z(t_below, t_above, ia) - total
    send_a(q, qz, lambda iz, ia, h: inv[iz, ia, :, half_of(h)], m1, m2)
    post("row", [tz[0]], [tz[7]], m1, m2, 8)


FINE = (8, 8, 8, 256)


def call(body, outs, scratch=(), name=None, far=0):
    shapes = [jax.ShapeDtypeStruct(s, jnp.float32) for s in outs]
    specs = dict(in_specs=[pl.BlockSpec(memory_space=pltpu.HBM)] * far) if far else {}
    return pl.pallas_call(
        body,
        out_shape=shapes,
        scratch_shapes=[pltpu.VMEM(s, jnp.float32) for s in scratch] + ([pltpu.SemaphoreType.DMA((far,))] if far else []),
        **specs,
        compiler_params=pltpu.CompilerParams(vmem_limit_bytes=32 * 1024 * 1024),
        name=name,
    )


def per_device(gz, row, rhs, stretch):
    mate_row = [(i, i ^ 1) for i in range(row)]
    other_row = [(i, (((i + 1) ^ 1) - 1) % row) for i in range(row)]
    mate_gz = [(i, i ^ 1) for i in range(gz)]
    other_gz = [(i, (((i + 1) ^ 1) - 1) % gz) for i in range(gz)]

    def swap_a(m1, m2):
        return lax.ppermute(m1, "row", mate_row), lax.ppermute(m2, "row", other_row)

    def swap_z(m1, m2):
        return lax.ppermute(m1, "gz", mate_gz), lax.ppermute(m2, "gz", other_gz)

    def message(entries):
        return (entries, 8, HALF)

    stretch = jnp.pad(stretch, ((0, 5), (0, 0)))
    ghosts = (6, 8, HALF)
    q, g, m1, m2 = call(k_first, [FINE, FINE, message(FIRST), message(FIRST)], [(8, 256), FINE], name="first", far=2)(rhs, stretch)
    z1, z2 = swap_z(m1, m2)
    m1, m2 = call(k_first_a, [message(FIRST), message(FIRST)], name="first_a")(q, g, stretch, z1, z2)
    r1, r2 = swap_a(m1, m2)
    inv, d, y = call(k_first_mean, [FINE, FINE, FINE], name="first_mean")(q, g, stretch, z1, z2)
    faces = (8, 2, 8, HALF)
    inv, x, rho, block, up, down, ghost = call(k_first_done, [FINE, FINE, FINE, (56, 256), (88, 256), (88, 256), ghosts], [faces, FINE], name="first_done")(
        rhs, q, g, inv, d, y, stretch, jnp.asarray(RESTRICT), z1, z2, r1, r2
    )

    rows = gz * EZ
    blocks = [block] + [
        lax.ppermute(up if k == 1 else down if k == gz - 1 else block, "gz", [(i, (i + k) % gz) for i in range(gz)]) for k in range(1, gz)
    ]
    column_ = call(functools.partial(k_column, rows), [(PACKED, rows, HALF)], [(56 * rows, HALF)], name="column")(*blocks)[0]
    r1, r2 = swap_a(column_, column_)
    cube, wide = (27, rows, HALF), (27, rows, 2 * HALF)
    coarse, res, xm, inv3, c3, far = call(
        k_mid,
        [(4, rows, GROUP), cube, cube, (8, rows, HALF), (12, rows, HALF), (4, 8, HALF)],
        [wide, wide, wide, (27, rows, HALF)],
        name="mid",
    )(column_, r1, r2)

    inv_far = call(k_far, [(7, 8, 8, HALF)], name="far")(far)[0]

    bit = 1
    while bit < row:
        size = 2 if bit == 1 or bit * 2 >= row else 4
        digit = (lax.axis_index("row") // bit) % size
        parts = [coarse] + [lax.ppermute(coarse, "row", [(i, i ^ (k * bit)) for i in range(row)]) for k in range(1, size)]
        ordered = []
        for place in range(size):
            v = parts[place]
            for m in range(1, size):
                v = jnp.where(digit == m, parts[place ^ m], v)
            ordered.append(v)
        coarse = jnp.concatenate(ordered, 2)
        bit *= size

    line = (8, 8, HALF)
    x, q, qz, tz, m1, m2 = call(
        k_fifth,
        [FINE, FINE, line, line, message(LATER), message(LATER)],
        [cube, cube, cube, (64 * rows, HALF), FINE, FINE, (8, 8, 8, HALF)],
        name="fifth",
    )(coarse, res, xm, inv3, c3, x, rho, inv, ghost, jnp.asarray(KRON73), far, inv_far, blocks[1], blocks[gz - 1])
    r1, r2 = swap_a(m1, m2)
    d, y = call(k_later_mean, [FINE, FINE], name="later_mean")(q, inv, ghost, qz)
    return call(k_last, [FINE], [faces, FINE], name="last")(q, inv, d, y, x, ghost, qz, tz, r1, r2)[0]


def solution(mesh):
    gz, row = mesh.shape["gz"], mesh.shape["row"]
    return jax.shard_map(
        functools.partial(per_device, gz, row),
        mesh=mesh,
        in_specs=(P(None, None, None, ("gz", "row")), P(None, ("gz", "row"))),
        out_specs=P(None, None, None, ("gz", "row")),
        check_vma=False,
    )
```

```python
import functools

import jax
import jax.numpy as jnp
import numpy as np
from jax import lax
from jax.experimental import pallas as pl
from jax.experimental.pallas import tpu as pltpu
from jax.sharding import PartitionSpec as P

ITERS = 5
EZ = 4
EA = 4
ER = 16
HALF = 128
GROUP = EA * ER

THETA = 2.2
DELTA = 1.8
RHO = DELTA / THETA
RHO2 = 1.0 / (2.0 * THETA / DELTA - RHO)
C1 = RHO2 * RHO
C2 = 2.0 * RHO2 / DELTA


def points_of(order):
    return -np.cos(np.pi * np.arange(order + 1) / order)


def tables_of(order):
    x = points_of(order)
    n = order + 1
    dist = x[:, None] - x[None, :] + np.eye(n)
    bary = 1.0 / np.prod(dist, axis=1)
    off = bary[None, :] / bary[:, None] / dist * (1.0 - np.eye(n))
    deriv = off - np.diag(off.sum(axis=1))
    place = np.arange(n)
    run = np.ones(n)
    for j in range(1, order // 2 + 1):
        b = 1.0 if 2 * j == order else 2.0
        run = run - b / (4.0 * j * j - 1.0) * np.cos(2.0 * j * place * np.pi / order)
    ends = np.where((place == 0) | (place == order), 1.0, 2.0)
    w = ends / order * run
    k = deriv.T @ np.diag(w) @ deriv
    return w, k


def interp_of(fine, coarse):
    x, y = points_of(fine), points_of(coarse)
    cols = []
    for j in range(coarse + 1):
        v = np.ones(fine + 1)
        for k in range(coarse + 1):
            if k != j:
                v = v * (x - y[k]) / (y[j] - y[k])
        cols.append(v)
    return np.stack(cols, axis=1)


W7, K7 = tables_of(7)
W3, K3 = tables_of(3)
J73 = interp_of(7, 3)
J31 = interp_of(3, 1)


def halves_of(table):
    high = table.astype(jnp.bfloat16)
    return high, (table - high.astype(np.float64)).astype(jnp.bfloat16)


KRON_HIGH, KRON_LOW = halves_of(np.kron(np.kron(J73, J73), J73))
KRON73 = np.concatenate([KRON_HIGH, KRON_HIGH, KRON_LOW], axis=1)


def weighted_sum(coefs, vals):
    total = None
    for c, v in zip(coefs, vals):
        term = v * float(c)
        total = term if total is None else total + term
    return total


def along(table, vals):
    rows, cols = table.shape
    half = cols // 2
    even = [vals[j] + vals[cols - 1 - j] for j in range(half)]
    odd = [vals[j] - vals[cols - 1 - j] for j in range(half)]
    out = [None] * rows
    for i in range(rows // 2):
        e = weighted_sum([(table[i, j] + table[i, cols - 1 - j]) / 2 for j in range(half)], even)
        o = weighted_sum([(table[i, j] - table[i, cols - 1 - j]) / 2 for j in range(half)], odd)
        out[i] = e + o
        out[rows - 1 - i] = e - o
    return out


def pair_of(v):
    high = v.astype(jnp.bfloat16)
    return high, (v - high.astype(jnp.float32)).astype(jnp.bfloat16)


def sub_iota(shape=(8, HALF)):
    return lax.broadcasted_iota(jnp.int32, shape, len(shape) - 2)


def lane_iota(shape=(8, HALF)):
    return lax.broadcasted_iota(jnp.int32, shape, len(shape) - 1)


def column(values):
    it = sub_iota()
    out = jnp.full((8, HALF), float(values[0]), jnp.float32)
    for i in range(1, 8):
        out = jnp.where(it == i, float(values[i]), out)
    return out


def lroll(v, shift):
    n = v.shape[-1]
    shift = shift % n
    return v if shift == 0 else pltpu.roll(v, shift, v.ndim - 1)


def sroll(v, shift):
    n = v.shape[-2]
    shift = shift % n
    return v if shift == 0 else pltpu.roll(v, shift, v.ndim - 2)


def half_of(h):
    return slice(h * HALF, (h + 1) * HALF)


def radial_masks():
    sub, lane = sub_iota(), lane_iota()
    r = lane % ER
    low = (sub == 0) & (r > 0)
    high = (sub == 7) & (r < ER - 1)
    wall = ((sub == 0) & (r == 0)) | ((sub == 7) & (r == ER - 1))
    return low, high, wall


def radial_add(v, masks):
    below = lroll(sroll(v, 1), 1)
    above = lroll(sroll(v, 7), HALF - 1)
    return v + jnp.where(masks[0], below, jnp.where(masks[1], above, 0.0))


def radial_columns():
    return [column([K7[i, (i - s) % 8] for i in range(8)]) for s in range(8)]


def radial_apply(rolls, v):
    total = rolls[0] * v
    for s in range(1, 8):
        total = total + rolls[s] * sroll(v, s)
    return total


def fine_apply(src, dst, base, s_half, sign):
    rolls = radial_columns()
    wr = column(W7)
    for h in range(len(s_half)):
        sl = half_of(h)
        s0, s1, s2 = [v * sign for v in stretch_rows(s_half[h])]
        s0, s1 = s0 * wr, s1 * wr
        for iz in range(8):
            vals = [src[iz, ia, :, sl] for ia in range(8)]
            part_a = along(K7, vals)
            s1z = s1 * float(W7[iz])
            s2z = s2 * float(W7[iz])
            for ia in range(8):
                part = part_a[ia] * s1z + radial_apply(rolls, vals[ia]) * (s2z * float(W7[ia]))
                dst[iz, ia, :, sl] = part if base is None else base[iz, ia, :, sl] + part
        for ia in range(8):
            vals = [src[iz, ia, :, sl] for iz in range(8)]
            part_z = along(K7, vals)
            s0a = s0 * float(W7[ia])
            for iz in range(8):
                dst[iz, ia, :, sl] = dst[iz, ia, :, sl] + part_z[iz] * s0a


def diag_at(s_ref, h, iz, ia, wr, kr):
    sl = half_of(h)
    s0, s1, s2 = (jnp.broadcast_to(s_ref[c : c + 1, sl], (8, HALF)) for c in range(3))
    ends = s0 * float(K7[iz, iz] * W7[ia]) + s1 * float(W7[iz] * K7[ia, ia])
    return ends * wr + s2 * (kr * float(W7[iz] * W7[ia]))


def pack_a(plane, slot):
    place = (lane_iota() // ER) % EA
    out = []
    for i in range(4):
        parts = [plane(0, i), plane(1, i), plane(0, i + 4), plane(1, i + 4)]
        parts = [lroll(v, (s - slot) * ER) for s, v in enumerate(parts)]
        out.append(jnp.where(place == 0, parts[0], jnp.where(place == 1, parts[1], jnp.where(place == 2, parts[2], parts[3]))))
    return out


def unpack_a(msg, slot, h, iz):
    s = h + 2 * (iz // 4)
    return lroll(msg[iz % 4], (slot - s) * ER)


def pack_z(plane, upper):
    low = lane_iota() < GROUP
    out = []
    for i in range(4):
        a, b = plane(i), plane(i + 4)
        out.append(jnp.where(low, lroll(a, GROUP) if upper else a, b if upper else lroll(b, GROUP)))
    return out


def unpack_z(msg, ia, upper):
    m = msg[ia % 4]
    return lroll(m, GROUP) if (ia < 4) == upper else m


def parity(axis):
    return lax.axis_index(axis) % 2 == 0


def choose(flag, a, b):
    return [jnp.where(flag, x, y) for x, y in zip(a, b)]


def got(axis, r1, r2, lo, hi):
    even = parity(axis)
    one = [r1[i] for i in range(lo, hi)]
    two = [r2[i] for i in range(lo, hi)]
    return choose(even, two, one), choose(even, one, two)


def post(axis, lower, upper, m1, m2, start):
    even = parity(axis)
    for i, (lo, up) in enumerate(zip(lower, upper)):
        m1[start + i] = jnp.where(even, up, lo)
        m2[start + i] = jnp.where(even, lo, up)


def place_of():
    return (lane_iota() // ER) % EA


def every_fine():
    for h in range(2):
        for iz in range(8):
            for ia in range(8):
                yield iz, ia, half_of(h)


def join_a(y, iz, h, left, right):
    place, sl = place_of(), half_of(h)
    lo, hi = y[iz, 0, :, sl], y[iz, 7, :, sl]
    y[iz, 0, :, sl] = lo + jnp.where(place > 0, lroll(hi, ER), left)
    y[iz, 7, :, sl] = hi + jnp.where(place < EA - 1, lroll(lo, HALF - ER), right)


def join_z(y, ia, beyond):
    low = lane_iota() < GROUP
    lo0, lo1 = y[0, ia, :, half_of(0)], y[0, ia, :, half_of(1)]
    hi0, hi1 = y[7, ia, :, half_of(0)], y[7, ia, :, half_of(1)]
    up0, up1 = lroll(hi0, GROUP), lroll(hi1, GROUP)
    dn0, dn1 = lroll(lo0, GROUP), lroll(lo1, GROUP)
    y[0, ia, :, half_of(0)] = lo0 + jnp.where(low, beyond, up0)
    y[0, ia, :, half_of(1)] = lo1 + jnp.where(low, up0, up1)
    y[7, ia, :, half_of(0)] = hi0 + jnp.where(low, dn0, dn1)
    y[7, ia, :, half_of(1)] = hi1 + jnp.where(low, dn1, beyond)


def sum_inside(y):
    for iz in range(8):
        for h in range(2):
            join_a(y, iz, h, 0.0, 0.0)
    for ia in range(8):
        join_z(y, ia, 0.0)


FIRST, LATER = 17, 9


def faces_z(q, inverse):
    top_q = pack_z(lambda ia: q[7, ia, :, half_of(1)], True)
    bottom_q = pack_z(lambda ia: q[0, ia, :, half_of(0)], False)

    def behind(ia, h):
        nodes = range(7) if h else range(1, 8)
        row = K7[7 if h else 0] / THETA
        return weighted_sum([row[j] for j in nodes], [inverse(j, ia, h) * q[j, ia, :, half_of(h)] for j in nodes])

    top_t = pack_z(lambda ia: behind(ia, 1), True)
    bottom_t = pack_z(lambda ia: behind(ia, 0), False)
    return bottom_q + bottom_t, top_q + top_t


def edge_lines(f, ia, h):
    slot = lane_iota() // ER
    source = (EA - 1 if ia else 0) + (EA if h else 0)
    out = None
    for j in range(1, 8):
        v = lroll(f[7 - j if h else j, ia, :, half_of(h)], (j - 1 - source) * ER)
        out = v if out is None else jnp.where(slot == j - 1, v, out)
    return out


def k_first(rhs_any, s_any, q, g, m1, m2, s_ref, rhs, sems):
    copy_s = pltpu.make_async_copy(s_any, s_ref, sems.at[0])
    copy_rhs = pltpu.make_async_copy(rhs_any, rhs, sems.at[1])
    copy_s.start()
    copy_rhs.start()
    masks = radial_masks()
    wr, kr = column(W7), column(np.diag(K7))
    copy_s.wait()
    for iz, ia, sl in every_fine():
        g[iz, ia, :, sl] = radial_add(diag_at(s_ref, sl.start // HALF, iz, ia, wr, kr), masks)
    sum_inside(g)
    copy_rhs.wait()
    for iz, ia, sl in every_fine():
        q[iz, ia, :, sl] = radial_add(rhs[iz, ia, :, sl], masks)
    sum_inside(q)
    bottom, top = faces_z(q, lambda iz, ia, h: jnp.where(masks[2], 0.0, 1.0 / g[iz, ia, :, half_of(h)]))
    post("gz", bottom, top, m1, m2, 0)
    post(
        "gz",
        pack_z(lambda ia: g[0, ia, :, half_of(0)], False),
        pack_z(lambda ia: g[7, ia, :, half_of(1)], True),
        m1,
        m2,
        8,
    )
    lines = [[edge_lines(f, ia, h) for f in (q, g) for ia in (0, 7)] for h in range(2)]
    post("gz", lines[0], lines[1], m1, m2, 12)
    even = parity("gz")
    top, bottom = lroll(s_ref[:, half_of(1)], GROUP), s_ref[:, half_of(0)]
    m1[16] = jnp.where(even, top, bottom)
    m2[16] = jnp.where(even, bottom, top)


def with_z(f, beyond, iz, ia, h):
    v = f[iz, ia, :, half_of(h)]
    low = lane_iota() < GROUP
    if iz == 0 and h == 0:
        v = v + jnp.where(low, beyond[ia], 0.0)
    if iz == 7 and h == 1:
        v = v + jnp.where(low, 0.0, beyond[ia])
    return v


def both_z(below, above, ia):
    return jnp.where(lane_iota() < GROUP, unpack_z(below, ia, False), unpack_z(above, ia, True))


def from_z(z1, z2, start):
    below, above = got("gz", z1, z2, start, start + 4)
    return [both_z(below, above, ia) for ia in range(8)]


def send_a(q, qz, inverse, m1, m2):
    full = lambda iz, ia, h: with_z(q, qz, iz, ia, h)
    post("row", pack_a(lambda h, iz: full(iz, 0, h), 0), pack_a(lambda h, iz: full(iz, 7, h), EA - 1), m1, m2, 0)
    left, right = {}, {}
    for h in range(2):
        for iz in range(8):
            scaled = [inverse(iz, ia, h) * full(iz, ia, h) for ia in range(8)]
            left[h, iz] = weighted_sum(K7[0, 1:] / THETA, scaled[1:])
            right[h, iz] = weighted_sum(K7[7, :7] / THETA, scaled[:7])
    post("row", pack_a(lambda h, iz: left[h, iz], 0), pack_a(lambda h, iz: right[h, iz], EA - 1), m1, m2, 4)


def k_first_a(q, g, s_ref, z1, z2, m1, m2):
    wall = radial_masks()[2]
    gz = from_z(z1, z2, 8)
    full = lambda iz, ia, h: with_z(g, gz, iz, ia, h)
    send_a(q, from_z(z1, z2, 0), lambda iz, ia, h: jnp.where(wall, 0.0, 1.0 / full(iz, ia, h)), m1, m2)
    post("row", pack_a(lambda h, iz: full(iz, 0, h), 0), pack_a(lambda h, iz: full(iz, 7, h), EA - 1), m1, m2, 8)
    below, above = got("gz", z1, z2, 12, 16)
    post("row", [below[0], below[2], above[0], above[2]], [below[1], below[3], above[1], above[3]], m1, m2, 12)
    s_below, s_above = got("gz", z1, z2, 16, 17)
    s_z = jnp.where(lane_iota() < GROUP, s_below[0], lroll(s_above[0], GROUP))
    place = place_of()
    even = parity("row")

    def stretch_of(slot):
        parts = [s_ref[:, half_of(0)], s_ref[:, half_of(1)], s_z]
        parts = [lroll(v, (s - slot) * ER) for s, v in enumerate(parts)]
        return jnp.where(place == 0, parts[0], jnp.where(place == 1, parts[1], parts[2]))

    to_left, to_right = stretch_of(0), stretch_of(EA - 1)
    m1[16] = jnp.where(even, to_right, to_left)
    m2[16] = jnp.where(even, to_left, to_right)


def complete(f, fz, r1, r2, start, put):
    place = place_of()
    left, right = got("row", r1, r2, start, start + 4)
    for h in range(2):
        for iz in range(8):
            for ia in range(8):
                v = with_z(f, fz, iz, ia, h)
                if ia == 0:
                    v = v + jnp.where(place == 0, unpack_a(left, 0, h, iz), 0.0)
                if ia == 7:
                    v = v + jnp.where(place == EA - 1, unpack_a(right, EA - 1, h, iz), 0.0)
                put(iz, ia, h, v)


def halves(ghost):
    return [ghost[4], ghost[5]]


def stretch_rows(v):
    return [jnp.broadcast_to(v[k : k + 1], (8, HALF)) for k in range(3)]


def meanwhile(q, qz, inverse, ghost, d, y):
    place = place_of()
    for iz, ia, sl in every_fine():
        h = sl.start // HALF
        v = inverse(iz, ia, h) * with_z(q, qz, iz, ia, h) * (1.0 / THETA)
        if ia == 0:
            v = jnp.where(place == 0, 0.0, v)
        if ia == 7:
            v = jnp.where(place == EA - 1, 0.0, v)
        d[iz, ia, :, sl] = v
    fine_apply(d, y, None, ghost, 1.0)


def k_first_mean(q, g, s_ref, z1, z2, inv, d, y):
    wall = radial_masks()[2]
    gz = from_z(z1, z2, 8)
    for iz, ia, sl in every_fine():
        inv[iz, ia, :, sl] = jnp.where(wall, 0.0, 1.0 / with_z(g, gz, iz, ia, sl.start // HALF))
    meanwhile(q, from_z(z1, z2, 0), lambda iz, ia, h: inv[iz, ia, :, half_of(h)], [s_ref[:, half_of(0)], s_ref[:, half_of(1)]], d, y)


def k_later_mean(q, inv, ghost, qz, d, y):
    meanwhile(q, qz, lambda iz, ia, h: inv[iz, ia, :, half_of(h)], halves(ghost), d, y)


def with_face(d, face):
    def whole(iz, ia, h):
        v = d[iz, ia, :, half_of(h)]
        if ia == 0:
            v = jnp.where(place_of() == 0, face[iz, h], v)
        if ia == 7:
            v = jnp.where(place_of() == EA - 1, face[iz, h], v)
        return v

    return whole


def edge_faces(q, qz, r1, r2, put):
    place = place_of()
    left, right = got("row", r1, r2, 0, 4)
    for h in range(2):
        for iz in range(8):
            low = with_z(q, qz, iz, 0, h) + jnp.where(place == 0, unpack_a(left, 0, h, iz), 0.0)
            high = with_z(q, qz, iz, 7, h) + jnp.where(place == EA - 1, unpack_a(right, EA - 1, h, iz), 0.0)
            put(iz, h, low, high)


def add_beyond(d, y0, y, face, s_own, s_n, s_z, s_m, t_left, t_right, t_z):
    place, low = place_of(), lane_iota() < GROUP
    wr, rolls = column(W7), radial_columns()
    w0, k00 = float(W7[0]), float(K7[0, 0])
    first, last = place == 0, place == EA - 1
    k_face = [jnp.where(last, float(K7[ia, 7]), float(K7[ia, 0])) for ia in range(8)]
    t_edge = []
    for h in range(2):
        sl = half_of(h)
        s0, s1, s2 = s_n[h]
        o0, o1, o2 = s_own[h]
        vals = [face[iz, h] for iz in range(8)]
        part_z = along(K7, vals)
        for iz in range(8):
            t = jnp.where(last, unpack_a(t_right, EA - 1, h, iz), unpack_a(t_left, 0, h, iz))
            if (h, iz) in ((0, 0), (1, 7)):
                t_edge.append(t)
            wz = float(W7[iz])
            part_z_w, part_r = w0 * wr * part_z[iz], (w0 * wz) * radial_apply(rolls, vals[iz])
            beyond = (s1 * wr) * (vals[iz] * k00 + t) * wz + s0 * part_z_w + s2 * part_r
            inside = o0 * part_z_w + o2 * part_r
            lines = (o1 * wr) * (vals[iz] * wz)
            for ia in range(1, 7):
                y[iz, ia, :, sl] = y0[iz, ia, :, sl] + lines * k_face[ia]
            lo = y0[iz, 0, :, sl] + lines * k_face[0] + jnp.where(first, inside, 0.0)
            hi = y0[iz, 7, :, sl] + lines * k_face[7] + jnp.where(last, inside, 0.0)
            y[iz, 0, :, sl] = lo + jnp.where(first, beyond, lroll(hi, ER))
            y[iz, 7, :, sl] = hi + jnp.where(last, beyond, lroll(lo, HALF - ER))
    t_a = jnp.where(low, t_edge[0], t_edge[1])
    vals = [jnp.where(low, d(0, ia, 0), d(7, ia, 1)) for ia in range(8)]
    part_a = along(K7, vals)
    s0, s1, s2 = s_z
    beyond = []
    for ia in range(8):
        wa = float(W7[ia])
        beyond.append((s0 * wr) * (vals[ia] * k00 + t_z[ia]) * wa + w0 * (s1 * wr * part_a[ia] + s2 * wa * radial_apply(rolls, vals[ia])))
    edge = jnp.where(place == EA - 1, vals[7], vals[0])
    edge_t = jnp.where(place == EA - 1, t_z[7], t_z[0])
    s0, s1, s2 = s_m
    corner = w0 * wr * (s0 * (edge * k00 + edge_t) + s1 * (edge * k00 + t_a)) + (w0 * w0) * s2 * radial_apply(rolls, edge)
    lo = beyond[0] + jnp.where(place > 0, lroll(beyond[7], ER), corner)
    hi = beyond[7] + jnp.where(place < EA - 1, lroll(beyond[0], -ER), corner)
    beyond[0], beyond[7] = lo, hi
    for ia in range(8):
        join_z(y, ia, beyond[ia])


def k_first_done(rhs, q, g, inv0, d, y0, s_ref, table, z1, z2, r1, r2, inv, x, rho, mid, up, down, ghost, face, y):
    masks = radial_masks()
    place, low = place_of(), lane_iota() < GROUP
    first, last = place == 0, place == EA - 1
    for iz in range(8):
        for h in range(2):
            for ia in range(1, 7):
                inv[iz, ia, :, half_of(h)] = inv0[iz, ia, :, half_of(h)]
    gz, qz = from_z(z1, z2, 8), from_z(z1, z2, 0)
    g_left, g_right = got("row", r1, r2, 8, 12)
    for iz in range(8):
        for h in range(2):
            v = with_z(g, gz, iz, 0, h) + jnp.where(first, unpack_a(g_left, 0, h, iz), 0.0)
            inv[iz, 0, :, half_of(h)] = jnp.where(masks[2], 0.0, 1.0 / v)
            v = with_z(g, gz, iz, 7, h) + jnp.where(last, unpack_a(g_right, EA - 1, h, iz), 0.0)
            inv[iz, 7, :, half_of(h)] = jnp.where(masks[2], 0.0, 1.0 / v)

    def put_face(iz, h, lo, hi):
        lo, hi = inv[iz, 0, :, half_of(h)] * lo, inv[iz, 7, :, half_of(h)] * hi
        face[iz, h] = jnp.where(first, lo, jnp.where(last, hi, 0.0)) * (1.0 / THETA)

    edge_faces(q, qz, r1, r2, put_face)
    below, above = got("gz", z1, z2, 16, 17)
    left, right = got("row", r1, r2, 16, 17)
    ghost[2] = jnp.where(low, below[0], lroll(above[0], GROUP))
    ghost[4] = s_ref[:, half_of(0)]
    ghost[5] = s_ref[:, half_of(1)]
    for k, s in ((0, 0), (1, 1), (3, 2)):
        ghost[k] = jnp.where(place == EA - 1, lroll(right[0], (EA - 1 - s) * ER), lroll(left[0], -s * ER))
    z_lines = got("gz", z1, z2, 12, 16)
    a_lines = got("row", r1, r2, 12, 16)
    slot = lane_iota() // ER
    weight = jnp.zeros((8, HALF), jnp.float32)
    for j in range(1, 8):
        weight = jnp.where(slot == j - 1, float(K7[0, j] / THETA), weight)
    t_edge = [[None, None], [None, None]]
    for side in range(2):
        for end in range(2):
            qs = z_lines[end][side] + a_lines[side][2 * end]
            gs = z_lines[end][2 + side] + a_lines[side][2 * end + 1]
            v = jnp.where(masks[2] | (slot == 7), 0.0, weight * qs / gs)
            for shift in (64, 32, 16):
                v = v + lroll(v, shift)
            t_edge[side][end] = v
    t_z = from_z(z1, z2, 4)
    t_z[0] = jnp.where(place == 0, jnp.where(low, t_edge[0][0], t_edge[0][1]), t_z[0])
    t_z[7] = jnp.where(place == EA - 1, jnp.where(low, t_edge[1][0], t_edge[1][1]), t_z[7])
    t_left, t_right = got("row", r1, r2, 4, 8)
    s_n, s_z, s_m = [stretch_rows(ghost[0]), stretch_rows(ghost[1])], stretch_rows(ghost[2]), stretch_rows(ghost[3])
    s_own = [stretch_rows(v) for v in halves(ghost)]
    whole = with_face(d, face)
    add_beyond(whole, y0, y, face, s_own, s_n, s_z, s_m, t_left, t_right, t_z)

    def put_x(iz, ia, h, v):
        sl = half_of(h)
        r = v - radial_add(y[iz, ia, :, sl], masks)
        x[iz, ia, :, sl] = (1.0 + C1) * whole(iz, ia, h) + C2 * inv[iz, ia, :, sl] * r

    complete(q, qz, r1, r2, 0, put_x)
    fine_apply(x, rho, rhs, halves(ghost), -1.0)
    for iz, ia, sl in every_fine():
        y[iz, ia, :, sl] = jnp.where(masks[2], 0.0, rho[iz, ia, :, sl])
    high, low_part = pair_of(y[...].reshape(512, 256))
    sums = jnp.dot(table[...], high, preferred_element_type=jnp.float32)
    sums = sums[0:112] + sums[112:224] + jnp.dot(table[0:112, :], low_part, preferred_element_type=jnp.float32)
    inner = lane_iota((56, HALF)) % ER > 0
    for h in range(2):
        sl = half_of(h)
        mid[:, sl] = sums[0:56, sl] + jnp.where(inner, lroll(sums[56:112, sl], 1), 0.0)
    mid[48:56, :] = s_ref[...]
    for iz, ia, sl in every_fine():
        y[iz, ia, :, sl] = radial_add(rho[iz, ia, :, sl], masks)
    sum_inside(y)
    bottom, top = faces_z(y, lambda iz, ia, h: inv[iz, ia, :, half_of(h)])
    for i in range(8):
        up[i] = top[i]
        down[i] = bottom[i]


def k_last(q, inv, d, y0, x, ghost, qz, tz, r1, r2, out, face, y):
    masks = radial_masks()
    place = place_of()
    first, last = place == 0, place == EA - 1

    def put_face(iz, h, lo, hi):
        lo, hi = inv[iz, 0, :, half_of(h)] * lo, inv[iz, 7, :, half_of(h)] * hi
        face[iz, h] = jnp.where(first, lo, jnp.where(last, hi, 0.0)) * (1.0 / THETA)

    edge_faces(q, qz, r1, r2, put_face)
    t_z = [tz[ia] for ia in range(8)]
    left, right = got("row", r1, r2, 8, 9)
    t_z[0] = t_z[0] + jnp.where(first, lroll(left[0], -(EA - 1) * ER), 0.0)
    t_z[7] = t_z[7] + jnp.where(last, lroll(right[0], (EA - 1) * ER), 0.0)
    t_left, t_right = got("row", r1, r2, 4, 8)
    s_n, s_z, s_m = [stretch_rows(ghost[0]), stretch_rows(ghost[1])], stretch_rows(ghost[2]), stretch_rows(ghost[3])
    s_own = [stretch_rows(v) for v in halves(ghost)]
    whole = with_face(d, face)
    add_beyond(whole, y0, y, face, s_own, s_n, s_z, s_m, t_left, t_right, t_z)

    def put_out(iz, ia, h, v):
        sl = half_of(h)
        r = v - radial_add(y[iz, ia, :, sl], masks)
        out[iz, ia, :, sl] = x[iz, ia, :, sl] + (1.0 + C1) * whole(iz, ia, h) + C2 * inv[iz, ia, :, sl] * r

    complete(q, qz, r1, r2, 0, put_out)


NODES = [(iz, ia, ir) for iz in range(3) for ia in range(3) for ir in range(3)]


def node(iz, ia, ir):
    return (iz * 3 + ia) * 3 + ir


def restrict_rows():
    picks = [(iz, ia, ir) for iz, ia, ir in NODES]
    picks += [(iz, 3, ir) for iz in range(3) for ir in range(3)]
    picks += [(3, ia, ir) for ia in range(3) for ir in range(3)]
    picks += [(3, 3, ir) for ir in range(3)]
    out = np.zeros((112, 512))
    for i, (iz, ia, ir) in enumerate(picks):
        out[i] = np.kron(np.kron(J73[:, iz], J73[:, ia]), J73[:, ir])
        if ir == 0:
            out[56 + i] = np.kron(np.kron(J73[:, iz], J73[:, ia]), J73[:, 3])
    return np.concatenate(halves_of(out), axis=0)


RESTRICT = restrict_rows()
PACKED = 17


def prev_z(v):
    return sroll(v, 1)


def prev_a(v):
    return lroll(v, ER)


def prev_r(v):
    return lroll(v, 1)


def next_z(v):
    return sroll(v, -1)


def next_a(v):
    return lroll(v, -ER)


def next_r(v):
    return lroll(v, -1)


def mid_coefs(s):
    prev = (prev_z, prev_a, prev_r)
    out = []
    for direction in range(3):
        one, two = [k for k in range(3) if k != direction]
        table = {}
        for e1 in range(2):
            v = s[direction] * float(W3[e1])
            v = v + prev[one](v) if e1 == 0 else v
            for e2 in range(2):
                u = v * float(W3[e2])
                table[e1, e2] = u + prev[two](u) if e2 == 0 else u
        out.append(table)
    return out


def mid_inverse(c, inner):
    out = {}
    for ez in range(2):
        for ea in range(2):
            for er in range(2):
                total = None
                for v, e, prev in ((c[0][ea, er], ez, prev_z), (c[1][ez, er], ea, prev_a), (c[2][ez, ea], er, prev_r)):
                    term = v * float(K3[1, 1]) if e else (v + prev(v)) * float(K3[0, 0])
                    total = term if total is None else total + term
                value = 1.0 / total
                out[ez, ea, er] = value if er else jnp.where(inner, value, 0.0)
    return out


def end(i):
    return 0 if i == 0 else 1


def mid_apply(get, nz, na, nr, c, acc):
    for ia in range(3):
        for ir in range(3):
            part = along(K3, [get(0, ia, ir), get(1, ia, ir), get(2, ia, ir), nz(ia, ir)])
            part = [v * c[0][end(ia), end(ir)] for v in part]
            acc[node(0, ia, ir)] = part[0] + prev_z(part[3])
            acc[node(1, ia, ir)] = part[1]
            acc[node(2, ia, ir)] = part[2]
    for iz in range(3):
        for ir in range(3):
            part = along(K3, [get(iz, 0, ir), get(iz, 1, ir), get(iz, 2, ir), na(iz, ir)])
            part = [v * c[1][end(iz), end(ir)] for v in part]
            acc[node(iz, 0, ir)] = acc[node(iz, 0, ir)] + part[0] + prev_a(part[3])
            acc[node(iz, 1, ir)] = acc[node(iz, 1, ir)] + part[1]
            acc[node(iz, 2, ir)] = acc[node(iz, 2, ir)] + part[2]
    for iz in range(3):
        for ia in range(3):
            part = along(K3, [get(iz, ia, 0), get(iz, ia, 1), get(iz, ia, 2), nr(iz, ia)])
            part = [v * c[2][end(iz), end(ia)] for v in part]
            acc[node(iz, ia, 0)] = acc[node(iz, ia, 0)] + part[0] + prev_r(part[3])
            acc[node(iz, ia, 1)] = acc[node(iz, ia, 1)] + part[1]
            acc[node(iz, ia, 2)] = acc[node(iz, ia, 2)] + part[2]


def k_column(rows, *refs):
    up_in, down_in, *blocks, out, up, down, wide = refs
    up[...] = up_in[...]
    down[...] = down_in[...]
    for k, block in enumerate(blocks):
        for z in range(EZ):
            v = block[:, half_of(z // 2)]
            wide[pl.ds((2 - EZ * k + z) % rows, 56, stride=rows), :] = lroll(v, GROUP) if z % 2 else v

    def entry(i):
        return wide[i * rows : (i + 1) * rows, :]

    shape = (rows, HALF)
    lane = lane_iota(shape)
    own, face = {}, {}
    for iz, ia, ir in NODES:
        v = entry(node(iz, ia, ir))
        own[iz, ia, ir] = v + prev_z(entry(36 + ia * 3 + ir)) if iz == 0 else v
    for iz in range(3):
        for ir in range(3):
            v = entry(27 + iz * 3 + ir)
            v = v + prev_z(entry(45 + ir)) if iz == 0 else v
            face[iz * 3 + ir] = v
            own[iz, 0, ir] = own[iz, 0, ir] + jnp.where(lane >= ER, prev_a(v), 0.0)
    flat = [own[n] for n in NODES] + [entry(48 + k) for k in range(3)]
    for p in range(15):
        out[p] = jnp.where(lane < GROUP, flat[2 * p], lroll(flat[2 * p + 1], GROUP))
    for p in range(2):
        v = None
        for slot, i in enumerate(range(8 * p, min(9, 8 * p + 8))):
            moved = lroll(face[i], (slot - (EA - 1)) * ER)
            v = moved if v is None else jnp.where(lane // ER == slot, moved, v)
        out[15 + p] = v


def k_mid(own, r1, r2, below, above, coarse, res, x, inv_out, c_out, far, b, d, y, y2):
    rows = own.shape[1]
    even = parity("row")
    lane = lane_iota((rows, HALF))

    def sides(i):
        one, two = r1[i], r2[i]
        return jnp.where(even, two, one), jnp.where(even, one, two)

    def halo(i):
        p, base = i // 2, GROUP * (i % 2)
        left, right = sides(p)
        left, right = lroll(left, 96 - base), lroll(right, 96 - base)
        mine = lroll(own[p], 32 - base)
        first = jnp.where(lane < 32, left, jnp.where(lane < 96, mine, right))
        return first, jnp.where(lane < 32, right, left)

    for iz, ia, ir in NODES:
        n = node(iz, ia, ir)
        first, second = halo(n)
        if ia == 0:
            i = iz * 3 + ir
            left, _ = sides(15 + i // 8)
            slot = i % 8
            from_left = lroll(left, 32 - slot * ER)
            to_right = lroll(own[15 + i // 8], 96 - slot * ER)
            first = first + jnp.where((lane >= 32) & (lane < 48), from_left, jnp.where((lane >= 96) & (lane < 112), to_right, 0.0))
        b[n, :, 0:HALF] = first
        b[n, :, HALF:] = second
    s = []
    for k in range(3):
        first, second = halo(27 + k)
        second = jnp.where((lane >= 32) & (lane < 96), 1.0, second)
        coarse[1 + k] = lroll(first, -32)[:, 0:GROUP]
        s.append(jnp.concatenate([first, second], axis=1))
        for layer, (lower, upper) in enumerate(((1, 6), (0, 7))):
            lo, hi = first[lower : lower + 1], first[upper : upper + 1]
            low, place = lane[0:1] < GROUP, ((lane // ER) % EA)[0:1]
            far[layer, k : k + 1] = jnp.where(low, lroll(lo, -32), lroll(hi, 32))
            left = jnp.where(low, lroll(lo, -16), lroll(hi, 48))
            right = jnp.where(low, lroll(lo, -48), lroll(hi, 16))
            far[2 + layer, k : k + 1] = jnp.where(place == EA - 1, right, left)

    inner = lane_iota((rows, 2 * HALF)) % ER > 0
    c = mid_coefs(s)
    inverse = mid_inverse(c, inner)
    for i, e in enumerate([(ez, ea, er) for ez in range(2) for ea in range(2) for er in range(2)]):
        inv_out[i] = inverse[e][:, 0:HALF]
    for k in range(3):
        for i, e in enumerate([(0, 0), (0, 1), (1, 0), (1, 1)]):
            c_out[4 * k + i] = c[k][e][:, 0:HALF]

    def kind(iz, ia, ir):
        return inverse[end(iz), end(ia), end(ir)]

    def get(iz, ia, ir):
        return d[node(iz, ia, ir)]

    for iz, ia, ir in NODES:
        n = node(iz, ia, ir)
        d[n] = kind(iz, ia, ir) * b[n] * (1.0 / THETA)
    mid_apply(
        get,
        lambda ia, ir: next_z(get(0, ia, ir)),
        lambda iz, ir: next_a(get(iz, 0, ir)),
        lambda iz, ia: next_r(get(iz, ia, 0)),
        c,
        y,
    )
    for iz, ia, ir in NODES:
        n = node(iz, ia, ir)
        d[n] = (1.0 + C1) * d[n] + C2 * kind(iz, ia, ir) * (b[n] - y[n])
        x[n] = d[n, :, 0:HALF]

    def near(iz, ia, ir):
        return d[node(iz, ia, ir), :, 0:HALF]

    mid_apply(
        near,
        lambda ia, ir: next_z(near(0, ia, ir)),
        lambda iz, ir: next_a(get(iz, 0, ir))[:, 0:HALF],
        lambda iz, ia: next_r(near(iz, ia, 0)),
        [{e: v[:, 0:HALF] for e, v in t.items()} for t in c],
        y2,
    )
    inner = lane % ER > 0
    for iz, ia, ir in NODES:
        n = node(iz, ia, ir)
        r = b[n, :, 0:HALF] - y2[n]
        r = r if ir else jnp.where(inner, r, 0.0)
        y2[n] = r
        res[n] = r

    def gather(v, prev):
        return v[0] + v[1] * float(J31[1, 0]) + v[2] * float(J31[2, 0]) + prev(v[1] * float(J31[1, 1]) + v[2] * float(J31[2, 1]))

    planes = []
    for iz in range(3):
        lines = [gather([y2[node(iz, ia, ir)] for ir in range(3)], prev_r) for ia in range(3)]
        planes.append(gather(lines, prev_a))
    vertex = jnp.where(inner, gather(planes, prev_z), 0.0)
    coarse[0] = lroll(vertex, -32)[:, 0:GROUP]


def k_far(far, inv):
    masks, place = radial_masks(), place_of()
    wr, kr = column(W7), column(np.diag(K7))
    near, next_, near_n, next_n = [stretch_rows(far[i]) for i in range(4)]

    def diag(s, iz, ia):
        return (s[0] * float(K7[iz, iz] * W7[ia]) + s[1] * float(W7[iz] * K7[ia, ia])) * wr + s[2] * (kr * float(W7[iz] * W7[ia]))

    for j in range(1, 8):

        def whole(s, t, ia):
            v = diag(s, j, ia)
            return radial_add(v + diag(t, 0, ia) if j == 7 else v, masks)

        line = [whole(near, next_, ia) for ia in range(8)]
        beyond = whole(near_n, next_n, 0)
        lo = line[0] + jnp.where(place > 0, lroll(line[7], ER), beyond)
        hi = line[7] + jnp.where(place < EA - 1, lroll(line[0], -ER), beyond)
        line[0], line[7] = lo, hi
        for ia in range(8):
            inv[j - 1, ia] = jnp.where(masks[2], 0.0, 1.0 / line[ia])


def vertex_solve(s0, s1, s2, b):
    shape = b.shape
    inner = (lane_iota(shape) % ER) > 0

    def pair(v, f):
        return v + f(v)

    edge_z = 0.5 * pair(pair(s0, prev_a), prev_r)
    edge_a = 0.5 * pair(pair(s1, prev_z), prev_r)
    edge_r = 0.5 * pair(pair(s2, prev_z), prev_a)
    back_z, back_a, back_r = prev_z(edge_z), prev_a(edge_a), prev_r(edge_r)
    middle = edge_z + back_z + edge_a + back_a + edge_r + back_r

    def operate(q):
        y = middle * q - edge_z * next_z(q) - back_z * prev_z(q)
        y = y - edge_a * next_a(q) - back_a * prev_a(q)
        y = y - edge_r * next_r(q) - back_r * prev_r(q)
        return jnp.where(inner, y, 0.0)

    def total(v):
        return jnp.sum(jnp.sum(v, axis=0, keepdims=True), axis=1, keepdims=True)

    e = jnp.zeros(shape, jnp.float32)
    r = b
    q = b
    rr = total(r * r)
    for _ in range(ITERS):
        y = operate(q)
        alpha = rr / total(q * y)
        e = e + alpha * q
        r = r - alpha * y
        rn = total(r * r)
        q = r + (rn / rr) * q
        rr = rn
    return e


def k_fifth(
    whole, res, xm, inv3, c_in, x, rho, inv, ghost, kron, far, inv_far, from_below, from_above, x_out, q, qz, tz, m1, m2, lift, dm, rm, xs, g, gf, yf
):
    e = vertex_solve(whole[1], whole[2], whole[3], whole[0])
    rows, lanes = e.shape
    e = pltpu.roll(e, (lanes + 32 - GROUP * lax.axis_index("row")) % lanes, 1)
    corner = {}
    for cz in range(2):
        for ca in range(2):
            for cr in range(2):
                v = next_z(e) if cz else e
                corner[cz, ca, cr] = lroll(v, -(ca * ER + cr))[:, 0:HALF]

    def three(a, b):
        return [a] + [a * float(J31[i, 0]) + b * float(J31[i, 1]) for i in (1, 2)]

    along_r = {(cz, ca): three(corner[cz, ca, 0], corner[cz, ca, 1]) for cz in range(2) for ca in range(2)}
    along_ra = {cz: [three(along_r[cz, 0][ir], along_r[cz, 1][ir]) for ir in range(3)] for cz in range(2)}
    beyond_a = {ir: three(along_r[0, 1][ir], along_r[1, 1][ir]) for ir in range(3)}
    for ia in range(3):
        for ir in range(3):
            for iz, v in enumerate(three(along_ra[0][ir][ia], along_ra[1][ir][ia])):
                lift[node(iz, ia, ir)] = v

    c = [{e_: c_in[4 * k + i] for i, e_ in enumerate([(0, 0), (0, 1), (1, 0), (1, 1)])} for k in range(3)]

    def kind(iz, ia, ir):
        return inv3[(end(iz) * 2 + end(ia)) * 2 + end(ir)]

    def get_lift(iz, ia, ir):
        return lift[node(iz, ia, ir)]

    def get_d(iz, ia, ir):
        return dm[node(iz, ia, ir)]

    mid_apply(
        get_lift,
        lambda ia, ir: along_ra[1][ir][ia],
        lambda iz, ir: beyond_a[ir][iz],
        lambda iz, ia: next_r(get_lift(iz, ia, 0)),
        c,
        rm,
    )
    for iz, ia, ir in NODES:
        n = node(iz, ia, ir)
        r = kind(iz, ia, ir) * (res[n] - rm[n])
        dm[n] = r * (1.0 / THETA)
        lift[n] = lift[n] + xm[n] + ((1.0 + C1) / THETA + C2) * r
    mid_apply(
        get_d,
        lambda ia, ir: next_z(get_d(0, ia, ir)),
        lambda iz, ir: next_a(get_d(iz, 0, ir)),
        lambda iz, ia: next_r(get_d(iz, ia, 0)),
        c,
        rm,
    )
    for iz, ia, ir in NODES:
        n = node(iz, ia, ir)
        lift[n] = lift[n] - C2 * kind(iz, ia, ir) * rm[n]
    for iz in range(4):
        for ia in range(4):
            for ir in range(4):
                v = lift[node(iz % 3, ia % 3, ir % 3)]
                v = lroll(v, -(ia // 3 * ER + ir // 3))
                v = next_z(v) if iz == 3 else v
                n = (iz * 4 + ia) * 4 + ir
                xs[n * rows : (n + 1) * rows, :] = v
    low = lane_iota((64, HALF)) < GROUP
    cols = []
    for h in range(2):
        one = xs[pl.ds(2 + 2 * h, 64, stride=rows), :]
        two = xs[pl.ds(3 + 2 * h, 64, stride=rows), :]
        cols.append(jnp.where(low, lroll(one, -32), lroll(two, 32)))
    for lower, upper in ((1, 6), (0, 7)):
        one = xs[pl.ds(lower, 64, stride=rows), :]
        one = jnp.concatenate([one[48:64], one[32:48], one[16:32], one[0:16]], axis=0)
        two = xs[pl.ds(upper, 64, stride=rows), :]
        cols.append(jnp.where(low, lroll(one, -32), lroll(two, 32)))
    high, low_part = pair_of(jnp.concatenate(cols, axis=1))
    raised = jnp.dot(kron[...], jnp.concatenate([high, low_part, high], axis=0), preferred_element_type=jnp.float32)
    g[...] = raised[:, 0:256].reshape(8, 8, 8, 256)
    gf[...] = raised[:, 256:512].reshape(8, 8, 8, 256)
    for iz, ia, sl in every_fine():
        x_out[iz, ia, :, sl] = x[iz, ia, :, sl] + g[iz, ia, :, sl]
    masks = radial_masks()
    fine_apply(g, q, rho, halves(ghost), -1.0)
    for iz, ia, sl in every_fine():
        q[iz, ia, :, sl] = radial_add(q[iz, ia, :, sl], masks)
    sum_inside(q)

    fine_apply(gf, yf, None, [far[0]], 1.0)
    s0, s1, s2 = stretch_rows(far[1])
    wr, rolls, place = column(W7), radial_columns(), place_of()
    second = half_of(1)
    part_a = along(K7, [gf[0, ia, :, second] for ia in range(8)])
    for ia in range(8):
        part_z = weighted_sum(K7[0], [gf[j, ia, :, second] for j in range(8)])
        part_r = radial_apply(rolls, gf[0, ia, :, second])
        v = s0 * wr * part_z * float(W7[ia]) + (s1 * wr * part_a[ia] + s2 * part_r * float(W7[ia])) * float(W7[0])
        yf[7, ia] = yf[7, ia] + v
    for j in range(8):
        line = [radial_add(yf[j, ia], masks) for ia in range(8)]
        lo = line[0] + jnp.where(place > 0, lroll(line[7], ER), 0.0)
        hi = line[7] + jnp.where(place < EA - 1, lroll(line[0], -ER), 0.0)
        line[0], line[7] = lo, hi
        for ia in range(8):
            if j:
                line[ia] = inv_far[j - 1, ia] * line[ia] * float(K7[0, j] / THETA)
            yf[j, ia] = line[ia]

    q_below, q_above = [from_below[i] for i in range(4)], [from_above[i] for i in range(4)]
    t_below, t_above = [from_below[i] for i in range(4, 8)], [from_above[i] for i in range(4, 8)]
    for ia in range(8):
        qz[ia] = both_z(q_below, q_above, ia) - yf[0, ia]
        total = yf[1, ia]
        for j in range(2, 8):
            total = total + yf[j, ia]
        tz[ia] = both_z(t_below, t_above, ia) - total
    send_a(q, qz, lambda iz, ia, h: inv[iz, ia, :, half_of(h)], m1, m2)
    post("row", [tz[0]], [tz[7]], m1, m2, 8)


FINE = (8, 8, 8, 256)


def call(body, outs, scratch=(), name=None, far=0):
    shapes = [jax.ShapeDtypeStruct(s, jnp.float32) for s in outs]
    specs = dict(in_specs=[pl.BlockSpec(memory_space=pltpu.HBM)] * far) if far else {}
    return pl.pallas_call(
        body,
        out_shape=shapes,
        scratch_shapes=[pltpu.VMEM(s, jnp.float32) for s in scratch] + ([pltpu.SemaphoreType.DMA((far,))] if far else []),
        **specs,
        compiler_params=pltpu.CompilerParams(vmem_limit_bytes=32 * 1024 * 1024),
        name=name,
    )


def per_device(gz, row, rhs, stretch):
    mate_row = [(i, i ^ 1) for i in range(row)]
    other_row = [(i, (((i + 1) ^ 1) - 1) % row) for i in range(row)]
    mate_gz = [(i, i ^ 1) for i in range(gz)]
    other_gz = [(i, (((i + 1) ^ 1) - 1) % gz) for i in range(gz)]

    def swap_a(m1, m2):
        return lax.ppermute(m1, "row", mate_row), lax.ppermute(m2, "row", other_row)

    def swap_z(m1, m2):
        return lax.ppermute(m1, "gz", mate_gz), lax.ppermute(m2, "gz", other_gz)

    def message(entries):
        return (entries, 8, HALF)

    stretch = jnp.pad(stretch, ((0, 5), (0, 0)))
    ghosts = (6, 8, HALF)
    q, g, m1, m2 = call(k_first, [FINE, FINE, message(FIRST), message(FIRST)], [(8, 256), FINE], name="first", far=2)(rhs, stretch)
    z1, z2 = swap_z(m1, m2)
    m1, m2 = call(k_first_a, [message(FIRST), message(FIRST)], name="first_a")(q, g, stretch, z1, z2)
    r1, r2 = swap_a(m1, m2)
    inv, d, y = call(k_first_mean, [FINE, FINE, FINE], name="first_mean")(q, g, stretch, z1, z2)
    faces = (8, 2, 8, HALF)
    inv, x, rho, block, up, down, ghost = call(k_first_done, [FINE, FINE, FINE, (56, 256), message(8), message(8), ghosts], [faces, FINE], name="first_done")(
        rhs, q, g, inv, d, y, stretch, jnp.asarray(RESTRICT), z1, z2, r1, r2
    )

    rows = gz * EZ
    blocks = {0: block}
    for k in sorted(range(1, gz), key=lambda k: -min(k, gz - k)):
        blocks[k] = lax.ppermute(block, "gz", [(i, (i + k) % gz) for i in range(gz)])
    blocks = [blocks[k] for k in range(gz)]
    face = (8, 8, HALF)
    column_, up, down = call(functools.partial(k_column, rows), [(PACKED, rows, HALF), face, face], [(56 * rows, HALF)], name="column")(
        up, down, *blocks
    )
    r1, r2 = swap_a(column_, column_)
    below = lax.ppermute(up, "gz", [(i, (i + 1) % gz) for i in range(gz)])
    above = lax.ppermute(down, "gz", [(i, (i - 1) % gz) for i in range(gz)])
    cube, wide = (27, rows, HALF), (27, rows, 2 * HALF)
    coarse, res, xm, inv3, c3, far = call(
        k_mid,
        [(4, rows, GROUP), cube, cube, (8, rows, HALF), (12, rows, HALF), (4, 8, HALF)],
        [wide, wide, wide, (27, rows, HALF)],
        name="mid",
    )(column_, r1, r2, below, above)

    inv_far = call(k_far, [(7, 8, 8, HALF)], name="far")(far)[0]

    bit = 1
    while bit < row:
        size = 2 if bit == 1 or bit * 2 >= row else 4
        digit = (lax.axis_index("row") // bit) % size
        parts = [coarse] + [lax.ppermute(coarse, "row", [(i, i ^ (k * bit)) for i in range(row)]) for k in range(1, size)]
        ordered = []
        for place in range(size):
            v = parts[place]
            for m in range(1, size):
                v = jnp.where(digit == m, parts[place ^ m], v)
            ordered.append(v)
        coarse = jnp.concatenate(ordered, 2)
        bit *= size

    line = (8, 8, HALF)
    x, q, qz, tz, m1, m2 = call(
        k_fifth,
        [FINE, FINE, line, line, message(LATER), message(LATER)],
        [cube, cube, cube, (64 * rows, HALF), FINE, FINE, (8, 8, 8, HALF)],
        name="fifth",
    )(coarse, res, xm, inv3, c3, x, rho, inv, ghost, jnp.asarray(KRON73), far, inv_far, below, above)
    r1, r2 = swap_a(m1, m2)
    d, y = call(k_later_mean, [FINE, FINE], name="later_mean")(q, inv, ghost, qz)
    return call(k_last, [FINE], [faces, FINE], name="last")(q, inv, d, y, x, ghost, qz, tz, r1, r2)[0]


def solution(mesh):
    gz, row = mesh.shape["gz"], mesh.shape["row"]
    return jax.shard_map(
        functools.partial(per_device, gz, row),
        mesh=mesh,
        in_specs=(P(None, None, None, ("gz", "row")), P(None, ("gz", "row"))),
        out_specs=P(None, None, None, ("gz", "row")),
        check_vma=False,
    )
```

```python
import functools

import jax
import jax.numpy as jnp
import numpy as np
from jax import lax
from jax.experimental import pallas as pl
from jax.experimental.pallas import tpu as pltpu
from jax.sharding import PartitionSpec as P

ITERS = 5
EZ = 4
EA = 4
ER = 16
HALF = 128
GROUP = EA * ER

THETA = 2.2
DELTA = 1.8
RHO = DELTA / THETA
RHO2 = 1.0 / (2.0 * THETA / DELTA - RHO)
C1 = RHO2 * RHO
C2 = 2.0 * RHO2 / DELTA


def points_of(order):
    return -np.cos(np.pi * np.arange(order + 1) / order)


def tables_of(order):
    x = points_of(order)
    n = order + 1
    dist = x[:, None] - x[None, :] + np.eye(n)
    bary = 1.0 / np.prod(dist, axis=1)
    off = bary[None, :] / bary[:, None] / dist * (1.0 - np.eye(n))
    deriv = off - np.diag(off.sum(axis=1))
    place = np.arange(n)
    run = np.ones(n)
    for j in range(1, order // 2 + 1):
        b = 1.0 if 2 * j == order else 2.0
        run = run - b / (4.0 * j * j - 1.0) * np.cos(2.0 * j * place * np.pi / order)
    ends = np.where((place == 0) | (place == order), 1.0, 2.0)
    w = ends / order * run
    k = deriv.T @ np.diag(w) @ deriv
    return w, k


def interp_of(fine, coarse):
    x, y = points_of(fine), points_of(coarse)
    cols = []
    for j in range(coarse + 1):
        v = np.ones(fine + 1)
        for k in range(coarse + 1):
            if k != j:
                v = v * (x - y[k]) / (y[j] - y[k])
        cols.append(v)
    return np.stack(cols, axis=1)


W7, K7 = tables_of(7)
W3, K3 = tables_of(3)
J73 = interp_of(7, 3)
J31 = interp_of(3, 1)


def halves_of(table):
    high = table.astype(jnp.bfloat16)
    return high, (table - high.astype(np.float64)).astype(jnp.bfloat16)


KRON_HIGH, KRON_LOW = halves_of(np.kron(np.kron(J73, J73), J73))
KRON73 = np.concatenate([KRON_HIGH, KRON_HIGH, KRON_LOW], axis=1)


def weighted_sum(coefs, vals):
    total = None
    for c, v in zip(coefs, vals):
        term = v * float(c)
        total = term if total is None else total + term
    return total


def along(table, vals):
    rows, cols = table.shape
    half = cols // 2
    even = [vals[j] + vals[cols - 1 - j] for j in range(half)]
    odd = [vals[j] - vals[cols - 1 - j] for j in range(half)]
    out = [None] * rows
    for i in range(rows // 2):
        e = weighted_sum([(table[i, j] + table[i, cols - 1 - j]) / 2 for j in range(half)], even)
        o = weighted_sum([(table[i, j] - table[i, cols - 1 - j]) / 2 for j in range(half)], odd)
        out[i] = e + o
        out[rows - 1 - i] = e - o
    return out


def pair_of(v):
    high = v.astype(jnp.bfloat16)
    return high, (v - high.astype(jnp.float32)).astype(jnp.bfloat16)


def sub_iota(shape=(8, HALF)):
    return lax.broadcasted_iota(jnp.int32, shape, len(shape) - 2)


def lane_iota(shape=(8, HALF)):
    return lax.broadcasted_iota(jnp.int32, shape, len(shape) - 1)


def column(values):
    it = sub_iota()
    out = jnp.full((8, HALF), float(values[0]), jnp.float32)
    for i in range(1, 8):
        out = jnp.where(it == i, float(values[i]), out)
    return out


def lroll(v, shift):
    n = v.shape[-1]
    shift = shift % n
    return v if shift == 0 else pltpu.roll(v, shift, v.ndim - 1)


def sroll(v, shift):
    n = v.shape[-2]
    shift = shift % n
    return v if shift == 0 else pltpu.roll(v, shift, v.ndim - 2)


def half_of(h):
    return slice(h * HALF, (h + 1) * HALF)


def radial_masks():
    sub, lane = sub_iota(), lane_iota()
    r = lane % ER
    low = (sub == 0) & (r > 0)
    high = (sub == 7) & (r < ER - 1)
    wall = ((sub == 0) & (r == 0)) | ((sub == 7) & (r == ER - 1))
    return low, high, wall


def radial_add(v, masks):
    below = lroll(sroll(v, 1), 1)
    above = lroll(sroll(v, 7), HALF - 1)
    return v + jnp.where(masks[0], below, jnp.where(masks[1], above, 0.0))


def radial_columns():
    return [column([K7[i, (i - s) % 8] for i in range(8)]) for s in range(8)]


def radial_apply(rolls, v):
    total = rolls[0] * v
    for s in range(1, 8):
        total = total + rolls[s] * sroll(v, s)
    return total


def fine_apply(src, dst, base, s_half, sign):
    rolls = radial_columns()
    wr = column(W7)
    for h in range(len(s_half)):
        sl = half_of(h)
        s0, s1, s2 = [v * sign for v in stretch_rows(s_half[h])]
        s0, s1 = s0 * wr, s1 * wr
        for iz in range(8):
            vals = [src[iz, ia, :, sl] for ia in range(8)]
            part_a = along(K7, vals)
            s1z = s1 * float(W7[iz])
            s2z = s2 * float(W7[iz])
            for ia in range(8):
                part = part_a[ia] * s1z + radial_apply(rolls, vals[ia]) * (s2z * float(W7[ia]))
                dst[iz, ia, :, sl] = part if base is None else base[iz, ia, :, sl] + part
        for ia in range(8):
            vals = [src[iz, ia, :, sl] for iz in range(8)]
            part_z = along(K7, vals)
            s0a = s0 * float(W7[ia])
            for iz in range(8):
                dst[iz, ia, :, sl] = dst[iz, ia, :, sl] + part_z[iz] * s0a


def diag_at(s_ref, h, iz, ia, wr, kr):
    sl = half_of(h)
    s0, s1, s2 = (jnp.broadcast_to(s_ref[c : c + 1, sl], (8, HALF)) for c in range(3))
    ends = s0 * float(K7[iz, iz] * W7[ia]) + s1 * float(W7[iz] * K7[ia, ia])
    return ends * wr + s2 * (kr * float(W7[iz] * W7[ia]))


def pack_a(plane, slot):
    place = (lane_iota() // ER) % EA
    out = []
    for i in range(4):
        parts = [plane(0, i), plane(1, i), plane(0, i + 4), plane(1, i + 4)]
        parts = [lroll(v, (s - slot) * ER) for s, v in enumerate(parts)]
        out.append(jnp.where(place == 0, parts[0], jnp.where(place == 1, parts[1], jnp.where(place == 2, parts[2], parts[3]))))
    return out


def unpack_a(msg, slot, h, iz):
    s = h + 2 * (iz // 4)
    return lroll(msg[iz % 4], (slot - s) * ER)


def pack_z(plane, upper):
    low = lane_iota() < GROUP
    out = []
    for i in range(4):
        a, b = plane(i), plane(i + 4)
        out.append(jnp.where(low, lroll(a, GROUP) if upper else a, b if upper else lroll(b, GROUP)))
    return out


def unpack_z(msg, ia, upper):
    m = msg[ia % 4]
    return lroll(m, GROUP) if (ia < 4) == upper else m


def parity(axis):
    return lax.axis_index(axis) % 2 == 0


def choose(flag, a, b):
    return [jnp.where(flag, x, y) for x, y in zip(a, b)]


def got(axis, r1, r2, lo, hi):
    even = parity(axis)
    one = [r1[i] for i in range(lo, hi)]
    two = [r2[i] for i in range(lo, hi)]
    return choose(even, two, one), choose(even, one, two)


def post(axis, lower, upper, m1, m2, start):
    even = parity(axis)
    for i, (lo, up) in enumerate(zip(lower, upper)):
        m1[start + i] = jnp.where(even, up, lo)
        m2[start + i] = jnp.where(even, lo, up)


def place_of():
    return (lane_iota() // ER) % EA


def every_fine():
    for h in range(2):
        for iz in range(8):
            for ia in range(8):
                yield iz, ia, half_of(h)


def join_a(y, iz, h, left, right):
    place, sl = place_of(), half_of(h)
    lo, hi = y[iz, 0, :, sl], y[iz, 7, :, sl]
    y[iz, 0, :, sl] = lo + jnp.where(place > 0, lroll(hi, ER), left)
    y[iz, 7, :, sl] = hi + jnp.where(place < EA - 1, lroll(lo, HALF - ER), right)


def join_z(y, ia, beyond):
    low = lane_iota() < GROUP
    lo0, lo1 = y[0, ia, :, half_of(0)], y[0, ia, :, half_of(1)]
    hi0, hi1 = y[7, ia, :, half_of(0)], y[7, ia, :, half_of(1)]
    up0, up1 = lroll(hi0, GROUP), lroll(hi1, GROUP)
    dn0, dn1 = lroll(lo0, GROUP), lroll(lo1, GROUP)
    y[0, ia, :, half_of(0)] = lo0 + jnp.where(low, beyond, up0)
    y[0, ia, :, half_of(1)] = lo1 + jnp.where(low, up0, up1)
    y[7, ia, :, half_of(0)] = hi0 + jnp.where(low, dn0, dn1)
    y[7, ia, :, half_of(1)] = hi1 + jnp.where(low, dn1, beyond)


def sum_inside(y):
    for iz in range(8):
        for h in range(2):
            join_a(y, iz, h, 0.0, 0.0)
    for ia in range(8):
        join_z(y, ia, 0.0)


FIRST, LATER = 17, 9


def faces_z(q, inverse):
    top_q = pack_z(lambda ia: q[7, ia, :, half_of(1)], True)
    bottom_q = pack_z(lambda ia: q[0, ia, :, half_of(0)], False)

    def behind(ia, h):
        nodes = range(7) if h else range(1, 8)
        row = K7[7 if h else 0] / THETA
        return weighted_sum([row[j] for j in nodes], [inverse(j, ia, h) * q[j, ia, :, half_of(h)] for j in nodes])

    top_t = pack_z(lambda ia: behind(ia, 1), True)
    bottom_t = pack_z(lambda ia: behind(ia, 0), False)
    return bottom_q + bottom_t, top_q + top_t


def edge_lines(f, ia, h):
    slot = lane_iota() // ER
    source = (EA - 1 if ia else 0) + (EA if h else 0)
    out = None
    for j in range(1, 8):
        v = lroll(f[7 - j if h else j, ia, :, half_of(h)], (j - 1 - source) * ER)
        out = v if out is None else jnp.where(slot == j - 1, v, out)
    return out


def k_diag(s_ref, g):
    masks = radial_masks()
    wr, kr = column(W7), column(np.diag(K7))
    for iz, ia, sl in every_fine():
        g[iz, ia, :, sl] = radial_add(diag_at(s_ref, sl.start // HALF, iz, ia, wr, kr), masks)
    sum_inside(g)


def k_first(rhs, s_ref, g, q, m1, m2):
    masks = radial_masks()
    for iz, ia, sl in every_fine():
        q[iz, ia, :, sl] = radial_add(rhs[iz, ia, :, sl], masks)
    sum_inside(q)
    bottom, top = faces_z(q, lambda iz, ia, h: jnp.where(masks[2], 0.0, 1.0 / g[iz, ia, :, half_of(h)]))
    post("gz", bottom, top, m1, m2, 0)
    post(
        "gz",
        pack_z(lambda ia: g[0, ia, :, half_of(0)], False),
        pack_z(lambda ia: g[7, ia, :, half_of(1)], True),
        m1,
        m2,
        8,
    )
    lines = [[edge_lines(f, ia, h) for f in (q, g) for ia in (0, 7)] for h in range(2)]
    post("gz", lines[0], lines[1], m1, m2, 12)
    even = parity("gz")
    top, bottom = lroll(s_ref[:, half_of(1)], GROUP), s_ref[:, half_of(0)]
    m1[16] = jnp.where(even, top, bottom)
    m2[16] = jnp.where(even, bottom, top)


def with_z(f, beyond, iz, ia, h):
    v = f[iz, ia, :, half_of(h)]
    low = lane_iota() < GROUP
    if iz == 0 and h == 0:
        v = v + jnp.where(low, beyond[ia], 0.0)
    if iz == 7 and h == 1:
        v = v + jnp.where(low, 0.0, beyond[ia])
    return v


def both_z(below, above, ia):
    return jnp.where(lane_iota() < GROUP, unpack_z(below, ia, False), unpack_z(above, ia, True))


def from_z(z1, z2, start):
    below, above = got("gz", z1, z2, start, start + 4)
    return [both_z(below, above, ia) for ia in range(8)]


def send_a(q, qz, inverse, m1, m2):
    full = lambda iz, ia, h: with_z(q, qz, iz, ia, h)
    post("row", pack_a(lambda h, iz: full(iz, 0, h), 0), pack_a(lambda h, iz: full(iz, 7, h), EA - 1), m1, m2, 0)
    left, right = {}, {}
    for h in range(2):
        for iz in range(8):
            scaled = [inverse(iz, ia, h) * full(iz, ia, h) for ia in range(8)]
            left[h, iz] = weighted_sum(K7[0, 1:] / THETA, scaled[1:])
            right[h, iz] = weighted_sum(K7[7, :7] / THETA, scaled[:7])
    post("row", pack_a(lambda h, iz: left[h, iz], 0), pack_a(lambda h, iz: right[h, iz], EA - 1), m1, m2, 4)


def k_first_a(q, g, s_ref, z1, z2, m1, m2):
    wall = radial_masks()[2]
    gz = from_z(z1, z2, 8)
    full = lambda iz, ia, h: with_z(g, gz, iz, ia, h)
    send_a(q, from_z(z1, z2, 0), lambda iz, ia, h: jnp.where(wall, 0.0, 1.0 / full(iz, ia, h)), m1, m2)
    post("row", pack_a(lambda h, iz: full(iz, 0, h), 0), pack_a(lambda h, iz: full(iz, 7, h), EA - 1), m1, m2, 8)
    below, above = got("gz", z1, z2, 12, 16)
    post("row", [below[0], below[2], above[0], above[2]], [below[1], below[3], above[1], above[3]], m1, m2, 12)
    s_below, s_above = got("gz", z1, z2, 16, 17)
    s_z = jnp.where(lane_iota() < GROUP, s_below[0], lroll(s_above[0], GROUP))
    place = place_of()
    even = parity("row")

    def stretch_of(slot):
        parts = [s_ref[:, half_of(0)], s_ref[:, half_of(1)], s_z]
        parts = [lroll(v, (s - slot) * ER) for s, v in enumerate(parts)]
        return jnp.where(place == 0, parts[0], jnp.where(place == 1, parts[1], parts[2]))

    to_left, to_right = stretch_of(0), stretch_of(EA - 1)
    m1[16] = jnp.where(even, to_right, to_left)
    m2[16] = jnp.where(even, to_left, to_right)


def complete(f, fz, r1, r2, start, put):
    place = place_of()
    left, right = got("row", r1, r2, start, start + 4)
    for h in range(2):
        for iz in range(8):
            for ia in range(8):
                v = with_z(f, fz, iz, ia, h)
                if ia == 0:
                    v = v + jnp.where(place == 0, unpack_a(left, 0, h, iz), 0.0)
                if ia == 7:
                    v = v + jnp.where(place == EA - 1, unpack_a(right, EA - 1, h, iz), 0.0)
                put(iz, ia, h, v)


def halves(ghost):
    return [ghost[4], ghost[5]]


def stretch_rows(v):
    return [jnp.broadcast_to(v[k : k + 1], (8, HALF)) for k in range(3)]


def meanwhile(q, qz, inverse, ghost, d, y):
    place = place_of()
    for iz, ia, sl in every_fine():
        h = sl.start // HALF
        v = inverse(iz, ia, h) * with_z(q, qz, iz, ia, h) * (1.0 / THETA)
        if ia == 0:
            v = jnp.where(place == 0, 0.0, v)
        if ia == 7:
            v = jnp.where(place == EA - 1, 0.0, v)
        d[iz, ia, :, sl] = v
    fine_apply(d, y, None, ghost, 1.0)


def k_first_mean(q, g, s_ref, z1, z2, inv, d, y):
    wall = radial_masks()[2]
    gz = from_z(z1, z2, 8)
    for iz, ia, sl in every_fine():
        inv[iz, ia, :, sl] = jnp.where(wall, 0.0, 1.0 / with_z(g, gz, iz, ia, sl.start // HALF))
    meanwhile(q, from_z(z1, z2, 0), lambda iz, ia, h: inv[iz, ia, :, half_of(h)], [s_ref[:, half_of(0)], s_ref[:, half_of(1)]], d, y)


def k_later_mean(q, inv, ghost, qz, d, y):
    meanwhile(q, qz, lambda iz, ia, h: inv[iz, ia, :, half_of(h)], halves(ghost), d, y)


def with_face(d, face):
    def whole(iz, ia, h):
        v = d[iz, ia, :, half_of(h)]
        if ia == 0:
            v = jnp.where(place_of() == 0, face[iz, h], v)
        if ia == 7:
            v = jnp.where(place_of() == EA - 1, face[iz, h], v)
        return v

    return whole


def edge_faces(q, qz, r1, r2, put):
    place = place_of()
    left, right = got("row", r1, r2, 0, 4)
    for h in range(2):
        for iz in range(8):
            low = with_z(q, qz, iz, 0, h) + jnp.where(place == 0, unpack_a(left, 0, h, iz), 0.0)
            high = with_z(q, qz, iz, 7, h) + jnp.where(place == EA - 1, unpack_a(right, EA - 1, h, iz), 0.0)
            put(iz, h, low, high)


def add_beyond(d, y0, y, face, s_own, s_n, s_z, s_m, t_left, t_right, t_z):
    place, low = place_of(), lane_iota() < GROUP
    wr, rolls = column(W7), radial_columns()
    w0, k00 = float(W7[0]), float(K7[0, 0])
    first, last = place == 0, place == EA - 1
    k_face = [jnp.where(last, float(K7[ia, 7]), float(K7[ia, 0])) for ia in range(8)]
    t_edge = []
    for h in range(2):
        sl = half_of(h)
        s0, s1, s2 = s_n[h]
        o0, o1, o2 = s_own[h]
        vals = [face[iz, h] for iz in range(8)]
        part_z = along(K7, vals)
        for iz in range(8):
            t = jnp.where(last, unpack_a(t_right, EA - 1, h, iz), unpack_a(t_left, 0, h, iz))
            if (h, iz) in ((0, 0), (1, 7)):
                t_edge.append(t)
            wz = float(W7[iz])
            part_z_w, part_r = w0 * wr * part_z[iz], (w0 * wz) * radial_apply(rolls, vals[iz])
            beyond = (s1 * wr) * (vals[iz] * k00 + t) * wz + s0 * part_z_w + s2 * part_r
            inside = o0 * part_z_w + o2 * part_r
            lines = (o1 * wr) * (vals[iz] * wz)
            for ia in range(1, 7):
                y[iz, ia, :, sl] = y0[iz, ia, :, sl] + lines * k_face[ia]
            lo = y0[iz, 0, :, sl] + lines * k_face[0] + jnp.where(first, inside, 0.0)
            hi = y0[iz, 7, :, sl] + lines * k_face[7] + jnp.where(last, inside, 0.0)
            y[iz, 0, :, sl] = lo + jnp.where(first, beyond, lroll(hi, ER))
            y[iz, 7, :, sl] = hi + jnp.where(last, beyond, lroll(lo, HALF - ER))
    t_a = jnp.where(low, t_edge[0], t_edge[1])
    vals = [jnp.where(low, d(0, ia, 0), d(7, ia, 1)) for ia in range(8)]
    part_a = along(K7, vals)
    s0, s1, s2 = s_z
    beyond = []
    for ia in range(8):
        wa = float(W7[ia])
        beyond.append((s0 * wr) * (vals[ia] * k00 + t_z[ia]) * wa + w0 * (s1 * wr * part_a[ia] + s2 * wa * radial_apply(rolls, vals[ia])))
    edge = jnp.where(place == EA - 1, vals[7], vals[0])
    edge_t = jnp.where(place == EA - 1, t_z[7], t_z[0])
    s0, s1, s2 = s_m
    corner = w0 * wr * (s0 * (edge * k00 + edge_t) + s1 * (edge * k00 + t_a)) + (w0 * w0) * s2 * radial_apply(rolls, edge)
    lo = beyond[0] + jnp.where(place > 0, lroll(beyond[7], ER), corner)
    hi = beyond[7] + jnp.where(place < EA - 1, lroll(beyond[0], -ER), corner)
    beyond[0], beyond[7] = lo, hi
    for ia in range(8):
        join_z(y, ia, beyond[ia])


def k_first_done(rhs, q, g, inv0, d, y0, s_ref, table, z1, z2, r1, r2, inv, x, rho, mid, up, down, ghost, face, y):
    masks = radial_masks()
    place, low = place_of(), lane_iota() < GROUP
    first, last = place == 0, place == EA - 1
    for iz in range(8):
        for h in range(2):
            for ia in range(1, 7):
                inv[iz, ia, :, half_of(h)] = inv0[iz, ia, :, half_of(h)]
    gz, qz = from_z(z1, z2, 8), from_z(z1, z2, 0)
    g_left, g_right = got("row", r1, r2, 8, 12)
    for iz in range(8):
        for h in range(2):
            v = with_z(g, gz, iz, 0, h) + jnp.where(first, unpack_a(g_left, 0, h, iz), 0.0)
            inv[iz, 0, :, half_of(h)] = jnp.where(masks[2], 0.0, 1.0 / v)
            v = with_z(g, gz, iz, 7, h) + jnp.where(last, unpack_a(g_right, EA - 1, h, iz), 0.0)
            inv[iz, 7, :, half_of(h)] = jnp.where(masks[2], 0.0, 1.0 / v)

    def put_face(iz, h, lo, hi):
        lo, hi = inv[iz, 0, :, half_of(h)] * lo, inv[iz, 7, :, half_of(h)] * hi
        face[iz, h] = jnp.where(first, lo, jnp.where(last, hi, 0.0)) * (1.0 / THETA)

    edge_faces(q, qz, r1, r2, put_face)
    below, above = got("gz", z1, z2, 16, 17)
    left, right = got("row", r1, r2, 16, 17)
    ghost[2] = jnp.where(low, below[0], lroll(above[0], GROUP))
    ghost[4] = s_ref[:, half_of(0)]
    ghost[5] = s_ref[:, half_of(1)]
    for k, s in ((0, 0), (1, 1), (3, 2)):
        ghost[k] = jnp.where(place == EA - 1, lroll(right[0], (EA - 1 - s) * ER), lroll(left[0], -s * ER))
    z_lines = got("gz", z1, z2, 12, 16)
    a_lines = got("row", r1, r2, 12, 16)
    slot = lane_iota() // ER
    weight = jnp.zeros((8, HALF), jnp.float32)
    for j in range(1, 8):
        weight = jnp.where(slot == j - 1, float(K7[0, j] / THETA), weight)
    t_edge = [[None, None], [None, None]]
    for side in range(2):
        for end in range(2):
            qs = z_lines[end][side] + a_lines[side][2 * end]
            gs = z_lines[end][2 + side] + a_lines[side][2 * end + 1]
            v = jnp.where(masks[2] | (slot == 7), 0.0, weight * qs / gs)
            for shift in (64, 32, 16):
                v = v + lroll(v, shift)
            t_edge[side][end] = v
    t_z = from_z(z1, z2, 4)
    t_z[0] = jnp.where(place == 0, jnp.where(low, t_edge[0][0], t_edge[0][1]), t_z[0])
    t_z[7] = jnp.where(place == EA - 1, jnp.where(low, t_edge[1][0], t_edge[1][1]), t_z[7])
    t_left, t_right = got("row", r1, r2, 4, 8)
    s_n, s_z, s_m = [stretch_rows(ghost[0]), stretch_rows(ghost[1])], stretch_rows(ghost[2]), stretch_rows(ghost[3])
    s_own = [stretch_rows(v) for v in halves(ghost)]
    whole = with_face(d, face)
    add_beyond(whole, y0, y, face, s_own, s_n, s_z, s_m, t_left, t_right, t_z)

    def put_x(iz, ia, h, v):
        sl = half_of(h)
        r = v - radial_add(y[iz, ia, :, sl], masks)
        x[iz, ia, :, sl] = (1.0 + C1) * whole(iz, ia, h) + C2 * inv[iz, ia, :, sl] * r

    complete(q, qz, r1, r2, 0, put_x)
    fine_apply(x, rho, rhs, halves(ghost), -1.0)
    for iz, ia, sl in every_fine():
        y[iz, ia, :, sl] = jnp.where(masks[2], 0.0, rho[iz, ia, :, sl])
    high, low_part = pair_of(y[...].reshape(512, 256))
    sums = jnp.dot(table[...], high, preferred_element_type=jnp.float32)
    sums = sums[0:112] + sums[112:224] + jnp.dot(table[0:112, :], low_part, preferred_element_type=jnp.float32)
    inner = lane_iota((56, HALF)) % ER > 0
    for h in range(2):
        sl = half_of(h)
        mid[:, sl] = sums[0:56, sl] + jnp.where(inner, lroll(sums[56:112, sl], 1), 0.0)
    mid[48:56, :] = s_ref[...]
    up[0:56, :] = mid[...]
    down[0:56, :] = mid[...]
    for iz, ia, sl in every_fine():
        y[iz, ia, :, sl] = radial_add(rho[iz, ia, :, sl], masks)
    sum_inside(y)
    bottom, top = faces_z(y, lambda iz, ia, h: inv[iz, ia, :, half_of(h)])
    for i in range(8):
        up[56 + 8 * (i // 2) : 64 + 8 * (i // 2), half_of(i % 2)] = top[i]
        down[56 + 8 * (i // 2) : 64 + 8 * (i // 2), half_of(i % 2)] = bottom[i]


def k_last(q, inv, d, y0, x, ghost, qz, tz, r1, r2, out, face, y):
    masks = radial_masks()
    place = place_of()
    first, last = place == 0, place == EA - 1

    def put_face(iz, h, lo, hi):
        lo, hi = inv[iz, 0, :, half_of(h)] * lo, inv[iz, 7, :, half_of(h)] * hi
        face[iz, h] = jnp.where(first, lo, jnp.where(last, hi, 0.0)) * (1.0 / THETA)

    edge_faces(q, qz, r1, r2, put_face)
    t_z = [tz[ia] for ia in range(8)]
    left, right = got("row", r1, r2, 8, 9)
    t_z[0] = t_z[0] + jnp.where(first, lroll(left[0], -(EA - 1) * ER), 0.0)
    t_z[7] = t_z[7] + jnp.where(last, lroll(right[0], (EA - 1) * ER), 0.0)
    t_left, t_right = got("row", r1, r2, 4, 8)
    s_n, s_z, s_m = [stretch_rows(ghost[0]), stretch_rows(ghost[1])], stretch_rows(ghost[2]), stretch_rows(ghost[3])
    s_own = [stretch_rows(v) for v in halves(ghost)]
    whole = with_face(d, face)
    add_beyond(whole, y0, y, face, s_own, s_n, s_z, s_m, t_left, t_right, t_z)

    def put_out(iz, ia, h, v):
        sl = half_of(h)
        r = v - radial_add(y[iz, ia, :, sl], masks)
        out[iz, ia, :, sl] = x[iz, ia, :, sl] + (1.0 + C1) * whole(iz, ia, h) + C2 * inv[iz, ia, :, sl] * r

    complete(q, qz, r1, r2, 0, put_out)


NODES = [(iz, ia, ir) for iz in range(3) for ia in range(3) for ir in range(3)]


def node(iz, ia, ir):
    return (iz * 3 + ia) * 3 + ir


def restrict_rows():
    picks = [(iz, ia, ir) for iz, ia, ir in NODES]
    picks += [(iz, 3, ir) for iz in range(3) for ir in range(3)]
    picks += [(3, ia, ir) for ia in range(3) for ir in range(3)]
    picks += [(3, 3, ir) for ir in range(3)]
    out = np.zeros((112, 512))
    for i, (iz, ia, ir) in enumerate(picks):
        out[i] = np.kron(np.kron(J73[:, iz], J73[:, ia]), J73[:, ir])
        if ir == 0:
            out[56 + i] = np.kron(np.kron(J73[:, iz], J73[:, ia]), J73[:, 3])
    return np.concatenate(halves_of(out), axis=0)


RESTRICT = restrict_rows()
PACKED = 17


def prev_z(v):
    return sroll(v, 1)


def prev_a(v):
    return lroll(v, ER)


def prev_r(v):
    return lroll(v, 1)


def next_z(v):
    return sroll(v, -1)


def next_a(v):
    return lroll(v, -ER)


def next_r(v):
    return lroll(v, -1)


def mid_coefs(s):
    prev = (prev_z, prev_a, prev_r)
    out = []
    for direction in range(3):
        one, two = [k for k in range(3) if k != direction]
        table = {}
        for e1 in range(2):
            v = s[direction] * float(W3[e1])
            v = v + prev[one](v) if e1 == 0 else v
            for e2 in range(2):
                u = v * float(W3[e2])
                table[e1, e2] = u + prev[two](u) if e2 == 0 else u
        out.append(table)
    return out


def mid_inverse(c, inner):
    out = {}
    for ez in range(2):
        for ea in range(2):
            for er in range(2):
                total = None
                for v, e, prev in ((c[0][ea, er], ez, prev_z), (c[1][ez, er], ea, prev_a), (c[2][ez, ea], er, prev_r)):
                    term = v * float(K3[1, 1]) if e else (v + prev(v)) * float(K3[0, 0])
                    total = term if total is None else total + term
                value = 1.0 / total
                out[ez, ea, er] = value if er else jnp.where(inner, value, 0.0)
    return out


def end(i):
    return 0 if i == 0 else 1


def mid_apply(get, nz, na, nr, c, acc):
    for ia in range(3):
        for ir in range(3):
            part = along(K3, [get(0, ia, ir), get(1, ia, ir), get(2, ia, ir), nz(ia, ir)])
            part = [v * c[0][end(ia), end(ir)] for v in part]
            acc[node(0, ia, ir)] = part[0] + prev_z(part[3])
            acc[node(1, ia, ir)] = part[1]
            acc[node(2, ia, ir)] = part[2]
    for iz in range(3):
        for ir in range(3):
            part = along(K3, [get(iz, 0, ir), get(iz, 1, ir), get(iz, 2, ir), na(iz, ir)])
            part = [v * c[1][end(iz), end(ir)] for v in part]
            acc[node(iz, 0, ir)] = acc[node(iz, 0, ir)] + part[0] + prev_a(part[3])
            acc[node(iz, 1, ir)] = acc[node(iz, 1, ir)] + part[1]
            acc[node(iz, 2, ir)] = acc[node(iz, 2, ir)] + part[2]
    for iz in range(3):
        for ia in range(3):
            part = along(K3, [get(iz, ia, 0), get(iz, ia, 1), get(iz, ia, 2), nr(iz, ia)])
            part = [v * c[2][end(iz), end(ia)] for v in part]
            acc[node(iz, ia, 0)] = acc[node(iz, ia, 0)] + part[0] + prev_r(part[3])
            acc[node(iz, ia, 1)] = acc[node(iz, ia, 1)] + part[1]
            acc[node(iz, ia, 2)] = acc[node(iz, ia, 2)] + part[2]


def k_column(rows, *refs):
    blocks, out, wide = refs[:-2], refs[-2], refs[-1]
    for k, block in enumerate(blocks):
        for z in range(EZ):
            v = block[0:56, half_of(z // 2)]
            wide[pl.ds((2 - EZ * k + z) % rows, 56, stride=rows), :] = lroll(v, GROUP) if z % 2 else v

    def entry(i):
        return wide[i * rows : (i + 1) * rows, :]

    shape = (rows, HALF)
    lane = lane_iota(shape)
    own, face = {}, {}
    for iz, ia, ir in NODES:
        v = entry(node(iz, ia, ir))
        own[iz, ia, ir] = v + prev_z(entry(36 + ia * 3 + ir)) if iz == 0 else v
    for iz in range(3):
        for ir in range(3):
            v = entry(27 + iz * 3 + ir)
            v = v + prev_z(entry(45 + ir)) if iz == 0 else v
            face[iz * 3 + ir] = v
            own[iz, 0, ir] = own[iz, 0, ir] + jnp.where(lane >= ER, prev_a(v), 0.0)
    flat = [own[n] for n in NODES] + [entry(48 + k) for k in range(3)]
    for p in range(15):
        out[p] = jnp.where(lane < GROUP, flat[2 * p], lroll(flat[2 * p + 1], GROUP))
    for p in range(2):
        v = None
        for slot, i in enumerate(range(8 * p, min(9, 8 * p + 8))):
            moved = lroll(face[i], (slot - (EA - 1)) * ER)
            v = moved if v is None else jnp.where(lane // ER == slot, moved, v)
        out[15 + p] = v


def k_mid(own, r1, r2, coarse, res, x, inv_out, c_out, far, b, d, y, y2):
    rows = own.shape[1]
    even = parity("row")
    lane = lane_iota((rows, HALF))

    def sides(i):
        one, two = r1[i], r2[i]
        return jnp.where(even, two, one), jnp.where(even, one, two)

    def halo(i):
        p, base = i // 2, GROUP * (i % 2)
        left, right = sides(p)
        left, right = lroll(left, 96 - base), lroll(right, 96 - base)
        mine = lroll(own[p], 32 - base)
        first = jnp.where(lane < 32, left, jnp.where(lane < 96, mine, right))
        return first, jnp.where(lane < 32, right, left)

    for iz, ia, ir in NODES:
        n = node(iz, ia, ir)
        first, second = halo(n)
        if ia == 0:
            i = iz * 3 + ir
            left, _ = sides(15 + i // 8)
            slot = i % 8
            from_left = lroll(left, 32 - slot * ER)
            to_right = lroll(own[15 + i // 8], 96 - slot * ER)
            first = first + jnp.where((lane >= 32) & (lane < 48), from_left, jnp.where((lane >= 96) & (lane < 112), to_right, 0.0))
        b[n, :, 0:HALF] = first
        b[n, :, HALF:] = second
    s = []
    for k in range(3):
        first, second = halo(27 + k)
        second = jnp.where((lane >= 32) & (lane < 96), 1.0, second)
        coarse[1 + k] = lroll(first, -32)[:, 0:GROUP]
        s.append(jnp.concatenate([first, second], axis=1))
        for layer, (lower, upper) in enumerate(((1, 6), (0, 7))):
            lo, hi = first[lower : lower + 1], first[upper : upper + 1]
            low, place = lane[0:1] < GROUP, ((lane // ER) % EA)[0:1]
            far[layer, k : k + 1] = jnp.where(low, lroll(lo, -32), lroll(hi, 32))
            left = jnp.where(low, lroll(lo, -16), lroll(hi, 48))
            right = jnp.where(low, lroll(lo, -48), lroll(hi, 16))
            far[2 + layer, k : k + 1] = jnp.where(place == EA - 1, right, left)

    inner = lane_iota((rows, 2 * HALF)) % ER > 0
    c = mid_coefs(s)
    inverse = mid_inverse(c, inner)
    for i, e in enumerate([(ez, ea, er) for ez in range(2) for ea in range(2) for er in range(2)]):
        inv_out[i] = inverse[e][:, 0:HALF]
    for k in range(3):
        for i, e in enumerate([(0, 0), (0, 1), (1, 0), (1, 1)]):
            c_out[4 * k + i] = c[k][e][:, 0:HALF]

    def kind(iz, ia, ir):
        return inverse[end(iz), end(ia), end(ir)]

    def get(iz, ia, ir):
        return d[node(iz, ia, ir)]

    for iz, ia, ir in NODES:
        n = node(iz, ia, ir)
        d[n] = kind(iz, ia, ir) * b[n] * (1.0 / THETA)
    mid_apply(
        get,
        lambda ia, ir: next_z(get(0, ia, ir)),
        lambda iz, ir: next_a(get(iz, 0, ir)),
        lambda iz, ia: next_r(get(iz, ia, 0)),
        c,
        y,
    )
    for iz, ia, ir in NODES:
        n = node(iz, ia, ir)
        d[n] = (1.0 + C1) * d[n] + C2 * kind(iz, ia, ir) * (b[n] - y[n])
        x[n] = d[n, :, 0:HALF]

    def near(iz, ia, ir):
        return d[node(iz, ia, ir), :, 0:HALF]

    mid_apply(
        near,
        lambda ia, ir: next_z(near(0, ia, ir)),
        lambda iz, ir: next_a(get(iz, 0, ir))[:, 0:HALF],
        lambda iz, ia: next_r(near(iz, ia, 0)),
        [{e: v[:, 0:HALF] for e, v in t.items()} for t in c],
        y2,
    )
    inner = lane % ER > 0
    for iz, ia, ir in NODES:
        n = node(iz, ia, ir)
        r = b[n, :, 0:HALF] - y2[n]
        r = r if ir else jnp.where(inner, r, 0.0)
        y2[n] = r
        res[n] = r

    def gather(v, prev):
        return v[0] + v[1] * float(J31[1, 0]) + v[2] * float(J31[2, 0]) + prev(v[1] * float(J31[1, 1]) + v[2] * float(J31[2, 1]))

    planes = []
    for iz in range(3):
        lines = [gather([y2[node(iz, ia, ir)] for ir in range(3)], prev_r) for ia in range(3)]
        planes.append(gather(lines, prev_a))
    vertex = jnp.where(inner, gather(planes, prev_z), 0.0)
    coarse[0] = lroll(vertex, -32)[:, 0:GROUP]


def k_far(far, inv):
    masks, place = radial_masks(), place_of()
    wr, kr = column(W7), column(np.diag(K7))
    near, next_, near_n, next_n = [stretch_rows(far[i]) for i in range(4)]

    def diag(s, iz, ia):
        return (s[0] * float(K7[iz, iz] * W7[ia]) + s[1] * float(W7[iz] * K7[ia, ia])) * wr + s[2] * (kr * float(W7[iz] * W7[ia]))

    for j in range(1, 8):

        def whole(s, t, ia):
            v = diag(s, j, ia)
            return radial_add(v + diag(t, 0, ia) if j == 7 else v, masks)

        line = [whole(near, next_, ia) for ia in range(8)]
        beyond = whole(near_n, next_n, 0)
        lo = line[0] + jnp.where(place > 0, lroll(line[7], ER), beyond)
        hi = line[7] + jnp.where(place < EA - 1, lroll(line[0], -ER), beyond)
        line[0], line[7] = lo, hi
        for ia in range(8):
            inv[j - 1, ia] = jnp.where(masks[2], 0.0, 1.0 / line[ia])


def vertex_solve(s0, s1, s2, b):
    shape = b.shape
    inner = (lane_iota(shape) % ER) > 0

    def pair(v, f):
        return v + f(v)

    edge_z = 0.5 * pair(pair(s0, prev_a), prev_r)
    edge_a = 0.5 * pair(pair(s1, prev_z), prev_r)
    edge_r = 0.5 * pair(pair(s2, prev_z), prev_a)
    back_z, back_a, back_r = prev_z(edge_z), prev_a(edge_a), prev_r(edge_r)
    middle = edge_z + back_z + edge_a + back_a + edge_r + back_r

    def operate(q):
        y = middle * q - edge_z * next_z(q) - back_z * prev_z(q)
        y = y - edge_a * next_a(q) - back_a * prev_a(q)
        y = y - edge_r * next_r(q) - back_r * prev_r(q)
        return jnp.where(inner, y, 0.0)

    def total(v):
        return jnp.sum(jnp.sum(v, axis=0, keepdims=True), axis=1, keepdims=True)

    e = jnp.zeros(shape, jnp.float32)
    r = b
    q = b
    rr = total(r * r)
    for _ in range(ITERS):
        y = operate(q)
        alpha = rr / total(q * y)
        e = e + alpha * q
        r = r - alpha * y
        rn = total(r * r)
        q = r + (rn / rr) * q
        rr = rn
    return e


def k_fifth(
    whole, res, xm, inv3, c_in, x, rho, inv, ghost, kron, far, inv_far, from_below, from_above, x_out, q, qz, tz, m1, m2, lift, dm, rm, xs, g, gf, yf
):
    e = vertex_solve(whole[1], whole[2], whole[3], whole[0])
    rows, lanes = e.shape
    e = pltpu.roll(e, (lanes + 32 - GROUP * lax.axis_index("row")) % lanes, 1)
    corner = {}
    for cz in range(2):
        for ca in range(2):
            for cr in range(2):
                v = next_z(e) if cz else e
                corner[cz, ca, cr] = lroll(v, -(ca * ER + cr))[:, 0:HALF]

    def three(a, b):
        return [a] + [a * float(J31[i, 0]) + b * float(J31[i, 1]) for i in (1, 2)]

    along_r = {(cz, ca): three(corner[cz, ca, 0], corner[cz, ca, 1]) for cz in range(2) for ca in range(2)}
    along_ra = {cz: [three(along_r[cz, 0][ir], along_r[cz, 1][ir]) for ir in range(3)] for cz in range(2)}
    beyond_a = {ir: three(along_r[0, 1][ir], along_r[1, 1][ir]) for ir in range(3)}
    for ia in range(3):
        for ir in range(3):
            for iz, v in enumerate(three(along_ra[0][ir][ia], along_ra[1][ir][ia])):
                lift[node(iz, ia, ir)] = v

    c = [{e_: c_in[4 * k + i] for i, e_ in enumerate([(0, 0), (0, 1), (1, 0), (1, 1)])} for k in range(3)]

    def kind(iz, ia, ir):
        return inv3[(end(iz) * 2 + end(ia)) * 2 + end(ir)]

    def get_lift(iz, ia, ir):
        return lift[node(iz, ia, ir)]

    def get_d(iz, ia, ir):
        return dm[node(iz, ia, ir)]

    mid_apply(
        get_lift,
        lambda ia, ir: along_ra[1][ir][ia],
        lambda iz, ir: beyond_a[ir][iz],
        lambda iz, ia: next_r(get_lift(iz, ia, 0)),
        c,
        rm,
    )
    for iz, ia, ir in NODES:
        n = node(iz, ia, ir)
        r = kind(iz, ia, ir) * (res[n] - rm[n])
        dm[n] = r * (1.0 / THETA)
        lift[n] = lift[n] + xm[n] + ((1.0 + C1) / THETA + C2) * r
    mid_apply(
        get_d,
        lambda ia, ir: next_z(get_d(0, ia, ir)),
        lambda iz, ir: next_a(get_d(iz, 0, ir)),
        lambda iz, ia: next_r(get_d(iz, ia, 0)),
        c,
        rm,
    )
    for iz, ia, ir in NODES:
        n = node(iz, ia, ir)
        lift[n] = lift[n] - C2 * kind(iz, ia, ir) * rm[n]
    for iz in range(4):
        for ia in range(4):
            for ir in range(4):
                v = lift[node(iz % 3, ia % 3, ir % 3)]
                v = lroll(v, -(ia // 3 * ER + ir // 3))
                v = next_z(v) if iz == 3 else v
                n = (iz * 4 + ia) * 4 + ir
                xs[n * rows : (n + 1) * rows, :] = v
    low = lane_iota((64, HALF)) < GROUP
    cols = []
    for h in range(2):
        one = xs[pl.ds(2 + 2 * h, 64, stride=rows), :]
        two = xs[pl.ds(3 + 2 * h, 64, stride=rows), :]
        cols.append(jnp.where(low, lroll(one, -32), lroll(two, 32)))
    for lower, upper in ((1, 6), (0, 7)):
        one = xs[pl.ds(lower, 64, stride=rows), :]
        one = jnp.concatenate([one[48:64], one[32:48], one[16:32], one[0:16]], axis=0)
        two = xs[pl.ds(upper, 64, stride=rows), :]
        cols.append(jnp.where(low, lroll(one, -32), lroll(two, 32)))
    high, low_part = pair_of(jnp.concatenate(cols, axis=1))
    raised = jnp.dot(kron[...], jnp.concatenate([high, low_part, high], axis=0), preferred_element_type=jnp.float32)
    g[...] = raised[:, 0:256].reshape(8, 8, 8, 256)
    gf[...] = raised[:, 256:512].reshape(8, 8, 8, 256)
    for iz, ia, sl in every_fine():
        x_out[iz, ia, :, sl] = x[iz, ia, :, sl] + g[iz, ia, :, sl]
    masks = radial_masks()
    fine_apply(g, q, rho, halves(ghost), -1.0)
    for iz, ia, sl in every_fine():
        q[iz, ia, :, sl] = radial_add(q[iz, ia, :, sl], masks)
    sum_inside(q)

    fine_apply(gf, yf, None, [far[0]], 1.0)
    s0, s1, s2 = stretch_rows(far[1])
    wr, rolls, place = column(W7), radial_columns(), place_of()
    second = half_of(1)
    part_a = along(K7, [gf[0, ia, :, second] for ia in range(8)])
    for ia in range(8):
        part_z = weighted_sum(K7[0], [gf[j, ia, :, second] for j in range(8)])
        part_r = radial_apply(rolls, gf[0, ia, :, second])
        v = s0 * wr * part_z * float(W7[ia]) + (s1 * wr * part_a[ia] + s2 * part_r * float(W7[ia])) * float(W7[0])
        yf[7, ia] = yf[7, ia] + v
    for j in range(8):
        line = [radial_add(yf[j, ia], masks) for ia in range(8)]
        lo = line[0] + jnp.where(place > 0, lroll(line[7], ER), 0.0)
        hi = line[7] + jnp.where(place < EA - 1, lroll(line[0], -ER), 0.0)
        line[0], line[7] = lo, hi
        for ia in range(8):
            if j:
                line[ia] = inv_far[j - 1, ia] * line[ia] * float(K7[0, j] / THETA)
            yf[j, ia] = line[ia]

    def entries(block, start):
        out = []
        for i in range(start, start + 4):
            out.append(block[56 + 8 * (i // 2) : 64 + 8 * (i // 2), half_of(i % 2)])
        return out

    q_below, q_above, t_below, t_above = entries(from_below, 0), entries(from_above, 0), entries(from_below, 4), entries(from_above, 4)
    for ia in range(8):
        qz[ia] = both_z(q_below, q_above, ia) - yf[0, ia]
        total = yf[1, ia]
        for j in range(2, 8):
            total = total + yf[j, ia]
        tz[ia] = both_z(t_below, t_above, ia) - total
    send_a(q, qz, lambda iz, ia, h: inv[iz, ia, :, half_of(h)], m1, m2)
    post("row", [tz[0]], [tz[7]], m1, m2, 8)


FINE = (8, 8, 8, 256)


def call(body, outs, scratch=(), name=None, cost=None):
    shapes = [jax.ShapeDtypeStruct(s, jnp.float32) for s in outs]
    return pl.pallas_call(
        body,
        out_shape=shapes,
        scratch_shapes=[pltpu.VMEM(s, jnp.float32) for s in scratch],
        compiler_params=pltpu.CompilerParams(vmem_limit_bytes=32 * 1024 * 1024),
        cost_estimate=cost,
        name=name,
    )


def per_device(gz, row, rhs, stretch):
    mate_row = [(i, i ^ 1) for i in range(row)]
    other_row = [(i, (((i + 1) ^ 1) - 1) % row) for i in range(row)]
    mate_gz = [(i, i ^ 1) for i in range(gz)]
    other_gz = [(i, (((i + 1) ^ 1) - 1) % gz) for i in range(gz)]

    def swap_a(m1, m2):
        return lax.ppermute(m1, "row", mate_row), lax.ppermute(m2, "row", other_row)

    def swap_z(m1, m2):
        return lax.ppermute(m1, "gz", mate_gz), lax.ppermute(m2, "gz", other_gz)

    def message(entries):
        return (entries, 8, HALF)

    stretch = jnp.pad(stretch, ((0, 5), (0, 0)))
    ghosts = (6, 8, HALF)
    work = pl.CostEstimate(flops=40 * rhs.size, bytes_accessed=4 * rhs.size, transcendentals=0)
    g = call(k_diag, [FINE], name="diag", cost=work)(stretch)[0]
    q, m1, m2 = call(k_first, [FINE, message(FIRST), message(FIRST)], name="first")(rhs, stretch, g)
    z1, z2 = swap_z(m1, m2)
    m1, m2 = call(k_first_a, [message(FIRST), message(FIRST)], name="first_a")(q, g, stretch, z1, z2)
    r1, r2 = swap_a(m1, m2)
    inv, d, y = call(k_first_mean, [FINE, FINE, FINE], name="first_mean")(q, g, stretch, z1, z2)
    faces = (8, 2, 8, HALF)
    inv, x, rho, block, up, down, ghost = call(k_first_done, [FINE, FINE, FINE, (56, 256), (88, 256), (88, 256), ghosts], [faces, FINE], name="first_done")(
        rhs, q, g, inv, d, y, stretch, jnp.asarray(RESTRICT), z1, z2, r1, r2
    )

    rows = gz * EZ
    blocks = [block] + [
        lax.ppermute(up if k == 1 else down if k == gz - 1 else block, "gz", [(i, (i + k) % gz) for i in range(gz)]) for k in range(1, gz)
    ]
    column_ = call(functools.partial(k_column, rows), [(PACKED, rows, HALF)], [(56 * rows, HALF)], name="column")(*blocks)[0]
    r1, r2 = swap_a(column_, column_)
    cube, wide = (27, rows, HALF), (27, rows, 2 * HALF)
    coarse, res, xm, inv3, c3, far = call(
        k_mid,
        [(4, rows, GROUP), cube, cube, (8, rows, HALF), (12, rows, HALF), (4, 8, HALF)],
        [wide, wide, wide, (27, rows, HALF)],
        name="mid",
    )(column_, r1, r2)

    inv_far = call(k_far, [(7, 8, 8, HALF)], name="far")(far)[0]

    bit = 1
    while bit < row:
        size = 2 if bit == 1 or bit * 2 >= row else 4
        digit = (lax.axis_index("row") // bit) % size
        parts = [coarse] + [lax.ppermute(coarse, "row", [(i, i ^ (k * bit)) for i in range(row)]) for k in range(1, size)]
        ordered = []
        for place in range(size):
            v = parts[place]
            for m in range(1, size):
                v = jnp.where(digit == m, parts[place ^ m], v)
            ordered.append(v)
        coarse = jnp.concatenate(ordered, 2)
        bit *= size

    line = (8, 8, HALF)
    x, q, qz, tz, m1, m2 = call(
        k_fifth,
        [FINE, FINE, line, line, message(LATER), message(LATER)],
        [cube, cube, cube, (64 * rows, HALF), FINE, FINE, (8, 8, 8, HALF)],
        name="fifth",
    )(coarse, res, xm, inv3, c3, x, rho, inv, ghost, jnp.asarray(KRON73), far, inv_far, blocks[1], blocks[gz - 1])
    r1, r2 = swap_a(m1, m2)
    d, y = call(k_later_mean, [FINE, FINE], name="later_mean")(q, inv, ghost, qz)
    return call(k_last, [FINE], [faces, FINE], name="last")(q, inv, d, y, x, ghost, qz, tz, r1, r2)[0]


def solution(mesh):
    gz, row = mesh.shape["gz"], mesh.shape["row"]
    return jax.shard_map(
        functools.partial(per_device, gz, row),
        mesh=mesh,
        in_specs=(P(None, None, None, ("gz", "row")), P(None, ("gz", "row"))),
        out_specs=P(None, None, None, ("gz", "row")),
        check_vma=False,
    )
```
